32 devices in a mesh: decade: 2 (over x), row: 8 (over z, y), col: 2 (over core).
Axes of the slice: x: 2, y: 2, z: 4, core: 2. Of those that a mesh axis runs over, the one named last changes fastest.
Arguments:
- counts: int32 [144, 256, 256], P(('decade', 'row')), parts along dimension 0, may hold values from 0 to 96, as said below
- block_pairs: int32 [16, 9, 3], P('decade'), parts along dimension 0, may hold values from 0 to 15, as said below
- sketch: bfloat16 [16, 4096, 256], P(None, ('decade', 'row'), 'col'), parts along dimension 1, may hold values from -6 to 6
Outputs:
- basis: float32 [16, 4096, 256], P(None, ('decade', 'row'), 'col'), parts along dimension 1
The draws below stay inside these ranges and needn't reach their ends.
There are 2 independent parts, one for each index of `decade`. The reference program is written for one: setup_inputs(seed, part) draws one part's arguments, and reference() takes and returns one part's arrays. A program takes and returns all parts, laid end to end along the dimension named above; each array names one. Nothing has to cross between parts.
Inputs may be any that keep to these rules, and one draw needn't show every extreme that they name: Counts of each stored block, in row group r's range of rows of counts. `block_pairs`: i < j, both within 0 to 15. The first 8 stored blocks of a row group name every row group once as g; the last 1 name 1 row groups a second time, the same 1 group for every row group, each with another i than the first time; so no row group stores more than 2 blocks against one group, and no unordered pair of blocks is stored twice.
All inputs are finite; a program needn't handle non-finite values.
Results may differ from the reference program's by a relative error of at most 0.014.
Values may be sent and summed in bfloat16 or wider, within the bound.
No kernel may reach another device: no remote copies, remote signals or barrier semaphores. Data moves between devices by JAX's collectives and lax.ppermute only.
A program may use at most 128 MiB of HBM per device.

```python
import jax
import jax.numpy as jnp
from jax import lax

B = 256
SK = 256
BPG = 16
HOT = 1
NNZ = 9
V = 32768
N_ROW = 8


def draw_counts(key, part):
    key = jax.random.fold_in(key, 5)
    level_key, spread_key, value_key = jax.random.split(key, 3)
    total_blocks = N_ROW * NNZ
    owner = jnp.arange(total_blocks) // NNZ
    group_scale = 1 + 2 * (N_ROW - 1 - owner) // (N_ROW - 1)
    row_level = jax.random.randint(level_key, (total_blocks, B, 1), 1, 5)
    col_level = jax.random.randint(spread_key, (total_blocks, 1, B), 1, 5)
    ceiling = 1 + 2 * row_level * col_level * group_scale[:, None, None]
    return jax.random.randint(value_key, (total_blocks, B, B), 0, ceiling).astype(jnp.int32)


def draw_block_pairs(key, part):
    key = jax.random.fold_in(key, 11)
    perm_key, hot_key, first_key, second_key, column_key = jax.random.split(key, 5)
    orders = jax.vmap(lambda single: jax.random.permutation(single, N_ROW))(jax.random.split(perm_key, N_ROW))
    chosen = jax.random.permutation(hot_key, N_ROW)[:HOT]
    groups = jnp.concatenate([orders, jnp.broadcast_to(chosen[None, :], (N_ROW, HOT))], axis=1)
    first_rows = jax.random.randint(first_key, (N_ROW, N_ROW), 0, BPG - 1)
    earlier_rows = jnp.sum(jnp.where(orders[:, None, :] == chosen[None, :, None], first_rows[:, None, :], 0), axis=2)
    second_rows = (earlier_rows + 1 + jax.random.randint(second_key, (N_ROW, HOT), 0, BPG - 2)) % (BPG - 1)
    row_blocks = jnp.concatenate([first_rows, second_rows], axis=1)
    col_blocks = row_blocks + 1 + jax.random.randint(column_key, (N_ROW, NNZ), 0, BPG - 1 - row_blocks)
    return jnp.stack([row_blocks, groups, col_blocks], axis=-1).astype(jnp.int32)


def block_levels(own_key, dims, pieces, least, top_value):
    def one(dim, parts):
        heights = jax.random.uniform(jax.random.fold_in(jax.random.fold_in(own_key, 6), dim), (parts,), jnp.float32, least / len(pieces), top_value / len(pieces))
        return jnp.repeat(jnp.exp(heights), dims[dim] // parts).reshape((-1,) + (1,) * (len(dims) - dim - 1))

    level = one(*pieces[0])
    for cut in pieces[1:]:
        level = level * one(*cut)
    return level


def normal_values(key, extent, width, reach, cuts=(), held_as=jnp.bfloat16):
    values = width * jax.random.normal(key, extent, jnp.float32)
    if cuts:
        values = values * block_levels(key, extent, cuts, -0.22, 0.18)
    return jnp.clip(values, -reach, reach).astype(held_as)


def setup_inputs(seed: int = 0, part: int = 0) -> dict:
    splits = jax.random.split(jax.random.key(seed), 4)
    part_splits = jax.random.split(jax.random.fold_in(splits[3], part), 4)
    return {
        "counts": draw_counts(jax.random.fold_in(jax.random.fold_in(splits[3], part), 71), part),
        "block_pairs": draw_block_pairs(jax.random.fold_in(jax.random.fold_in(splits[3], part), 71), part),
        "sketch": normal_values(part_splits[2], (BPG, N_ROW * B, SK), 1.0, 6.0, ((1, 8), (2, 2))),
    }


highest = lax.Precision.HIGHEST

def orthonormal(result):
    flat_rows = result.reshape(BPG * N_ROW * B, SK)
    gram = jnp.dot(flat_rows.T.astype(jnp.float32), flat_rows.astype(jnp.float32), precision=highest, preferred_element_type=jnp.float32) / V
    lower_factor = jnp.linalg.cholesky(gram)
    inverse_factor = jax.scipy.linalg.solve_triangular(lower_factor, jnp.eye(SK, dtype=jnp.float32), lower=True).T
    return jnp.dot(flat_rows.astype(jnp.float32), inverse_factor.astype(jnp.float32), precision=highest, preferred_element_type=jnp.float32)

def reference(counts, block_pairs, sketch):
    total_blocks = N_ROW * NNZ
    pairs = block_pairs.reshape(total_blocks, 3)
    owner = (jnp.arange(total_blocks) // NNZ).astype(jnp.int32)
    row_index = (pairs[:, 0] * N_ROW + owner).astype(jnp.int32)
    col_index = (pairs[:, 2] * N_ROW + pairs[:, 1]).astype(jnp.int32)
    count_float = counts.astype(jnp.float32)
    margins = jnp.zeros((BPG * N_ROW, B), jnp.float32)
    margins = margins.at[row_index].add(jnp.sum(count_float, axis=2))
    margins = margins.at[col_index].add(jnp.sum(count_float, axis=1))
    log_total = jnp.log(jnp.sum(margins))
    log_margin = jnp.log(margins)
    scores = jnp.log(count_float) + log_total - log_margin[row_index][:, :, None] - log_margin[col_index][:, None, :]
    ppmi_blocks = jnp.where(counts > 0, jnp.maximum(scores, 0.0), 0.0).astype(jnp.bfloat16)
    ppmi_wide = ppmi_blocks.astype(jnp.float32)

    def apply_matrix(source):
        forward = jnp.einsum('sab,sbh->sah', ppmi_wide, source[col_index].astype(jnp.float32)).astype(jnp.bfloat16)
        transposed = jnp.einsum('sab,sah->sbh', ppmi_wide, source[row_index].astype(jnp.float32)).astype(jnp.bfloat16)
        result = jnp.zeros((BPG * N_ROW, B, SK), jnp.float32)
        result = result.at[row_index].add(forward.astype(jnp.float32))
        return result.at[col_index].add(transposed.astype(jnp.float32))
    omega = sketch.reshape(BPG * N_ROW, B, SK)
    first_basis = orthonormal(apply_matrix(omega)).astype(jnp.bfloat16).reshape(BPG * N_ROW, B, SK)
    basis = orthonormal(apply_matrix(first_basis))
    return basis.reshape(BPG, N_ROW * B, SK)
```

```python
import jax
import jax.numpy as jnp
from jax import lax
from jax.experimental import pallas as pl
from jax.experimental.pallas import tpu as pltpu
from jax.sharding import PartitionSpec as P

CAP = 2
MIB = 1 << 20
HIGHEST = lax.Precision.HIGHEST
VMEM = pl.BlockSpec(memory_space=pltpu.VMEM)
SMEM = pl.BlockSpec(memory_space=pltpu.SMEM)


def contract(a, b, a_dim, b_dim, precision=None):
    return lax.dot_general(
        a,
        b,
        (((a_dim,), (b_dim,)), ((), ())),
        precision=precision,
        preferred_element_type=jnp.float32,
    )


def call(kernel, out_shape, in_specs, scratch=(), flops=0, vmem=40):
    return pl.pallas_call(
        kernel,
        out_shape=out_shape,
        in_specs=in_specs,
        out_specs=jax.tree.map(lambda _: VMEM, out_shape),
        scratch_shapes=list(scratch),
        compiler_params=pltpu.CompilerParams(vmem_limit_bytes=vmem * MIB),
        cost_estimate=pl.CostEstimate(flops=flops, bytes_accessed=4 * MIB, transcendentals=0),
    )


def sums_kernel(counts_ref, sums_ref):
    nnz, rows, cols = counts_ref.shape
    ones = jnp.ones((8, cols), jnp.bfloat16)
    for s in range(nnz):
        block = counts_ref[s].astype(jnp.bfloat16)
        sums_ref[pl.ds(s, 1), :] = contract(ones, block, 1, 1)[0:1, :]
        sums_ref[pl.ds(nnz + s, 1), :] = contract(ones, block, 1, 0)[0:1, :]


def source_kernel(me_ref, pairs_ref, answer_ref, sketch_ref, send_ref, own_ref, turned):
    groups = send_ref.shape[0]
    nnz = own_ref.shape[0]
    me = me_ref[0]

    @pl.loop(0, sketch_ref.shape[0])
    def _(i):
        turned[i] = sketch_ref[i].T

    gather_blocks(me, groups, nnz, pairs_ref, answer_ref, turned, send_ref)

    @pl.loop(0, nnz)
    def _(s):
        own_ref[s] = turned[pairs_ref[me, s, 0]]


def gather_blocks(me, groups, nnz, pairs_ref, answer_ref, blocks, send_ref):
    @pl.loop(0, groups)
    def _(r):
        send_ref[r, 0] = blocks[answer_ref[0, r]]

        @pl.when(answer_ref[1, r] >= 0)
        def _():
            send_ref[r, 1] = blocks[answer_ref[1, r]]


def first_kernel(
    me_ref, pairs_ref, sums_ref, match_ref, counts_ref, recv_ref, own_ref,
    ppmi_ref, forward_ref, send_ref, cols_log,
):
    nnz = counts_ref.shape[0]
    groups = recv_ref.shape[0]
    me = me_ref[0]
    sums = sums_ref[...]
    high = jnp.floor(sums * (1.0 / 256.0))
    low = sums - high * 256.0
    match = match_ref[...]
    margins = 256.0 * contract(match, high.astype(jnp.bfloat16), 1, 0) + contract(
        match, low.astype(jnp.bfloat16), 1, 0
    )
    log_total = jnp.log(jnp.sum(sums))
    log_margin = jnp.log(margins)
    cols_log[...] = log_margin
    padded = jnp.concatenate(
        [log_margin, jnp.zeros((128 - log_margin.shape[0] % 128, log_margin.shape[1]), jnp.float32)],
        axis=0,
    )
    row_log = padded.T
    for s in range(nnz):
        counts = counts_ref[s]
        scores = (
            jnp.log(counts.astype(jnp.float32))
            + log_total
            - row_log[:, s : s + 1]
            - cols_log[pl.ds(nnz + s, 1), :]
        )
        ppmi = jnp.where(counts > 0, jnp.maximum(scores, 0.0), 0.0).astype(jnp.bfloat16)
        ppmi_ref[s] = ppmi
        group, rank = pairs_ref[me, s, 1], int(s >= groups)
        forward_ref[s] = contract(recv_ref[group, rank], ppmi, 1, 1).astype(jnp.bfloat16)
        send_ref[group, rank] = contract(own_ref[s], ppmi, 1, 0).astype(jnp.bfloat16)


def result_kernel(
    me_ref, pairs_ref, answer_ref, forward_ref, arrived_ref, other_forward_ref, other_arrived_ref,
    result_ref, gram_ref,
):
    nnz = forward_ref.shape[0]
    groups = arrived_ref.shape[0]
    blocks, half = result_ref.shape[1:3]
    me, my_col = me_ref[0], me_ref[1]
    result_ref[...] = jnp.zeros_like(result_ref)

    def add(side, forward, arrived):
        @pl.loop(0, nnz)
        def _(s):
            i = pairs_ref[me, s, 0]
            result_ref[side, i] += forward[s].astype(jnp.float32)

        @pl.loop(0, groups)
        def _(r):
            j = answer_ref[0, r]
            result_ref[side, j] += arrived[r, 0].astype(jnp.float32)
            k = answer_ref[1, r]

            @pl.when(k >= 0)
            def _():
                result_ref[side, k] += arrived[r, 1].astype(jnp.float32)

    add(my_col, forward_ref, arrived_ref)
    add(1 - my_col, other_forward_ref, other_arrived_ref)
    gram_ref[...] = jnp.zeros_like(gram_ref)

    @pl.loop(0, blocks // 2)
    def _(n):
        i = n + my_col * (blocks // 2)
        low, high = result_ref[0, i], result_ref[1, i]
        gram_ref[0] += contract(low, low, 1, 1, HIGHEST)
        gram_ref[1] += contract(high, low, 1, 1, HIGHEST)
        gram_ref[2] += contract(high, high, 1, 1, HIGHEST)


def inverse_factor(block):
    size = block.shape[0]
    tiles = size // 8
    full = (8, size)
    lane = lax.broadcasted_iota(jnp.int32, full, 1)
    sub = lax.broadcasted_iota(jnp.int32, full, 0)
    left = [block[8 * t : 8 * t + 8, :] for t in range(tiles)]
    right = [(lane == sub + 8 * t).astype(jnp.float32) for t in range(tiles)]
    for j in range(tiles):
        cols = [jnp.broadcast_to(left[j][:, 8 * j + k : 8 * j + k + 1], full) for k in range(8)]
        pivot = [
            [jnp.broadcast_to(cols[k][i : i + 1, :], full) for k in range(i + 1)] for i in range(8)
        ]
        row_l = [jnp.broadcast_to(left[j][i : i + 1, :], full) for i in range(8)]
        row_r = [jnp.broadcast_to(right[j][i : i + 1, :], full) for i in range(8)]
        scale = []
        for k in range(8):
            scale.append(lax.rsqrt(pivot[k][k]))
            for i in range(k + 1, 8):
                pivot[i][k] = pivot[i][k] * scale[k]
            for i in range(k + 1, 8):
                for m in range(k + 1, i + 1):
                    pivot[i][m] = pivot[i][m] - pivot[i][k] * pivot[m][k]
            row_l[k] = row_l[k] * scale[k]
            row_r[k] = row_r[k] * scale[k]
            for i in range(k + 1, 8):
                row_l[i] = row_l[i] - pivot[i][k] * row_l[k]
                row_r[i] = row_r[i] - pivot[i][k] * row_r[k]
        done = row_r[0]
        for i in range(1, 8):
            done = jnp.where(sub == i, row_r[i], done)
        right[j] = done
        if j < tiles - 1:
            for k in range(7, -1, -1):
                row_l[k] = row_l[k] * scale[k]
                row_r[k] = row_r[k] * scale[k]
                for i in range(k):
                    row_l[i] = row_l[i] - pivot[k][i] * row_l[k]
                    row_r[i] = row_r[i] - pivot[k][i] * row_r[k]
            for t in range(j + 1, tiles):
                cur = left[t]
                new_l, new_r = cur, right[t]
                for k in range(8):
                    col = jnp.broadcast_to(cur[:, 8 * j + k : 8 * j + k + 1], full)
                    new_l = new_l - col * row_l[k]
                    new_r = new_r - col * row_r[k]
                left[t], right[t] = new_l, new_r
    return jnp.concatenate(right, axis=0)


def invert(gram_ref, vocab, inverse):
    low = inverse_factor(gram_ref[0] * vocab)
    across = contract(gram_ref[1] * vocab, low, 1, 1, HIGHEST)
    high = inverse_factor(gram_ref[2] * vocab - contract(across, across, 1, 1, HIGHEST))
    inverse[0, 0] = low
    inverse[0, 1] = jnp.zeros_like(low)
    inverse[1, 0] = -contract(high, contract(across, low, 1, 0, HIGHEST), 1, 0, HIGHEST)
    inverse[1, 1] = high


def normal_block(inverse, result_ref, my_col, i):
    return contract(inverse[my_col, 0], result_ref[0, i], 1, 0, HIGHEST) + contract(
        inverse[my_col, 1], result_ref[1, i], 1, 0, HIGHEST
    )


def second_kernel(
    inv_vocab, me_ref, pairs_ref, answer_ref, gram_ref, result_ref, ppmi_ref,
    x_send_ref, send_ref, inverse, normal,
):
    nnz = ppmi_ref.shape[0]
    groups = send_ref.shape[0]
    me, my_col = me_ref[0], me_ref[1]
    invert(gram_ref, inv_vocab, inverse)

    @pl.loop(0, normal.shape[0])
    def _(i):
        normal[i] = normal_block(inverse, result_ref, my_col, i).astype(jnp.bfloat16)

    gather_blocks(me, groups, nnz, pairs_ref, answer_ref, normal, x_send_ref)

    for s in range(nnz):
        group, rank = pairs_ref[me, s, 1], int(s >= groups)
        own = normal[pairs_ref[me, s, 0]]
        send_ref[group, rank] = contract(own, ppmi_ref[s], 1, 0).astype(jnp.bfloat16)


def forward_kernel(me_ref, pairs_ref, recv_ref, ppmi_ref, forward_ref):
    groups = recv_ref.shape[0]
    me = me_ref[0]
    for s in range(ppmi_ref.shape[0]):
        group, rank = pairs_ref[me, s, 1], int(s >= groups)
        forward_ref[s] = contract(recv_ref[group, rank], ppmi_ref[s], 1, 1).astype(jnp.bfloat16)


def final_kernel(inv_vocab, me_ref, gram_ref, result_ref, out_ref, inverse):
    my_col = me_ref[1]
    invert(gram_ref, inv_vocab, inverse)

    @pl.loop(0, out_ref.shape[0])
    def _(i):
        out_ref[i] = normal_block(inverse, result_ref, my_col, i).T


def body(counts, block_pairs, sketch):
    groups = lax.axis_size("row")
    cols = lax.axis_size("col")
    me = lax.axis_index("row")
    my_col = lax.axis_index("col")
    nnz, rows, _ = counts.shape
    blocks, _, half = sketch.shape
    vocab = blocks * rows * groups
    f32, bf16 = jnp.float32, jnp.bfloat16
    shape = jax.ShapeDtypeStruct

    place = jnp.stack([me, my_col]).astype(jnp.int32)
    hit = block_pairs[:, :, 1] == me
    late = jnp.arange(nnz)[None, :] >= groups
    first_answer = jnp.sum(jnp.where(hit & ~late, block_pairs[:, :, 2], 0), axis=1)
    more_answer = jnp.sum(jnp.where(hit & late, block_pairs[:, :, 2] + 1, 0), axis=1) - 1
    answer = jnp.stack([first_answer, more_answer]).astype(jnp.int32)

    owner = jnp.arange(groups)[:, None]
    row_ids = block_pairs[:, :, 0] * groups + owner
    col_ids = block_pairs[:, :, 2] * groups + block_pairs[:, :, 1]
    depth = -(-2 * nnz // 8) * 8
    no_id = jnp.full((groups, depth - 2 * nnz), -1, jnp.int32)
    all_ids = jnp.concatenate([row_ids, col_ids, no_id], axis=1)
    my_ids = lax.dynamic_index_in_dim(all_ids, me, 0, keepdims=False)
    match = (my_ids[:, None] == all_ids.reshape(-1)[None, :]).astype(bf16)

    def swap(x):
        return lax.ppermute(x, "col", [(0, 1), (1, 0)])

    def exchange(x):
        return lax.all_to_all(x, "row", split_axis=0, concat_axis=0, tiled=True)

    def exchange_all(x):
        return lax.all_to_all(x, ("row", "col"), split_axis=0, concat_axis=0, tiled=True)

    def reduce_gram(part):
        ranks = groups * cols
        pieces = part.reshape(ranks, 3 * half // ranks, half)
        mine = jnp.sum(exchange_all(pieces), axis=0)
        every = exchange_all(jnp.broadcast_to(mine[None], pieces.shape))
        return every.reshape(3, half, half)

    sums = call(sums_kernel, shape((depth, rows), f32), [VMEM])(counts)
    sums_all = exchange(jnp.broadcast_to(sums[None], (groups, depth, rows)))

    x_send, own = call(
        source_kernel,
        (shape((groups, CAP, half, rows), bf16), shape((nnz, half, rows), bf16)),
        [SMEM, SMEM, SMEM, VMEM],
        [pltpu.VMEM((blocks, half, rows), bf16)],
    )(place, block_pairs, answer, sketch)
    x_recv = exchange(x_send)

    live = (jnp.arange(depth) < 2 * nnz)[None, :, None]
    sums_live = jnp.where(live, sums_all, 0.0).reshape(groups * depth, rows)
    ppmi, forward, send = call(
        first_kernel,
        (
            shape((nnz, rows, rows), bf16),
            shape((nnz, half, rows), bf16),
            shape((groups, CAP, half, rows), bf16),
        ),
        [SMEM, SMEM, VMEM, VMEM, VMEM, VMEM, VMEM],
        [pltpu.VMEM((depth, rows), f32)],
    )(place, block_pairs, sums_live, match, counts, x_recv, own)

    def finish(forward, send):
        other_forward = swap(forward)
        arrived = exchange(send)
        other_arrived = swap(arrived)
        result, gram = call(
            result_kernel,
            (shape((2, blocks, half, rows), f32), shape((3, half, half), f32)),
            [SMEM, SMEM, SMEM, VMEM, VMEM, VMEM, VMEM],
        )(place, block_pairs, answer, forward, arrived, other_forward, other_arrived)
        return result, reduce_gram(gram)

    result, gram = finish(forward, send)

    def second(*refs):
        second_kernel(1.0 / vocab, *refs)

    x_send, send = call(
        second,
        (shape((groups, CAP, half, rows), bf16), shape((groups, CAP, half, rows), bf16)),
        [SMEM, SMEM, SMEM, VMEM, VMEM, VMEM],
        [pltpu.VMEM((2, 2, half, half), f32), pltpu.VMEM((blocks, half, rows), bf16)],
    )(place, block_pairs, answer, gram, result, ppmi)
    x_recv = exchange(x_send)
    forward = call(
        forward_kernel,
        shape((nnz, half, rows), bf16),
        [SMEM, SMEM, VMEM, VMEM],
    )(place, block_pairs, x_recv, ppmi)
    result, gram = finish(forward, send)

    def final(*refs):
        final_kernel(1.0 / vocab, *refs)

    return call(
        final,
        shape((blocks, rows, half), f32),
        [SMEM, VMEM, VMEM],
        [pltpu.VMEM((2, 2, half, half), f32)],
    )(place, gram, result)


def solution(mesh):
    placed = (
        P(("decade", "row"), None, None),
        P("decade", None, None),
        P(None, ("decade", "row"), "col"),
    )
    return jax.shard_map(
        body,
        mesh=mesh,
        in_specs=placed,
        out_specs=P(None, ("decade", "row"), "col"),
        check_vma=False,
    )
```

```python
import jax
import jax.numpy as jnp
from jax import lax
from jax.experimental import pallas as pl
from jax.experimental.pallas import tpu as pltpu
from jax.sharding import PartitionSpec as P

MIB = 1 << 20
HIGHEST = lax.Precision.HIGHEST
VMEM = pl.BlockSpec(memory_space=pltpu.VMEM)
SMEM = pl.BlockSpec(memory_space=pltpu.SMEM)
ANY = pl.BlockSpec(memory_space=pl.ANY)
shape = jax.ShapeDtypeStruct
f32, bf16, i32 = jnp.float32, jnp.bfloat16, jnp.int32


def contract(a, b, a_dim, b_dim, precision=None):
    return lax.dot_general(
        a,
        b,
        (((a_dim,), (b_dim,)), ((), ())),
        precision=precision,
        preferred_element_type=f32,
    )


def call(kernel, out_shape, in_specs, out_specs=None, scratch=(), flops=0, vmem=32):
    if out_specs is None:
        out_specs = jax.tree.map(lambda _: VMEM, out_shape)
    return pl.pallas_call(
        kernel,
        out_shape=out_shape,
        in_specs=in_specs,
        out_specs=out_specs,
        scratch_shapes=list(scratch),
        compiler_params=pltpu.CompilerParams(vmem_limit_bytes=vmem * MIB),
        cost_estimate=pl.CostEstimate(flops=flops, bytes_accessed=4 * MIB, transcendentals=0),
    )


class Table:
    def __init__(self, groups, nnz):
        self.groups, self.nnz, self.hot = groups, nnz, nnz - groups
        self.main_j = 0
        self.my_s = self.main_j + groups
        self.hot_j = self.my_s + groups
        self.row_i = self.hot_j + groups * self.hot
        self.hot_k = self.row_i + nnz
        self.me = self.hot_k + self.hot
        self.col = self.me + 1

    def build(self, block_pairs, me, my_col):
        groups = self.groups
        peers = me ^ jnp.arange(groups)
        theirs = jnp.take(block_pairs, peers, axis=0)
        mine = theirs[0]
        hit = theirs[:, :, 1] == me
        main_j = jnp.sum(jnp.where(hit[:, :groups], theirs[:, :groups, 2], 0), axis=1)
        my_s = jnp.sum(
            jnp.where(mine[None, :groups, 1] == peers[:, None], jnp.arange(groups)[None, :], 0),
            axis=1,
        )
        hot_j = jnp.where(hit[:, groups:], theirs[:, groups:, 2], -1).reshape(-1)
        hot_k = (mine[groups:, 1] ^ me) & ~1
        parts = [main_j, my_s, hot_j, mine[:, 0], hot_k, jnp.stack([me, my_col])]
        return jnp.concatenate([p.astype(i32) for p in parts]), theirs


def sums_kernel(counts_ref, sums_ref):
    nnz, rows, cols = counts_ref.shape
    ones = jnp.ones((8, cols), bf16)
    sums_ref[...] = jnp.zeros_like(sums_ref)
    for s in range(nnz):
        block = counts_ref[s].astype(bf16)
        sums_ref[pl.ds(s, 1), :] = contract(ones, block, 1, 1)[0:1, :]
        sums_ref[pl.ds(nnz + s, 1), :] = contract(ones, block, 1, 0)[0:1, :]


def gather_blocks(t, tab, blocks, main, hot):
    for k in range(t.groups):
        main[k][...] = blocks[tab[t.main_j + k]]
        for m in range(t.hot):
            j = tab[t.hot_j + k * t.hot + m]

            @pl.when(j >= 0)
            def _():
                hot[k][m] = blocks[j]


def products(t, tab, blocks, ppmi, main, hot):
    def product(s):
        return contract(blocks[tab[t.row_i + s]], ppmi[s], 1, 0).astype(bf16)

    for k in range(t.groups):
        main[k][...] = product(tab[t.my_s + k])
    for m in range(t.hot):
        hot[m] = product(t.groups + m)


def make_source_kernel(t):
    def kernel(tab, sketch_ref, turned, *outs):
        main, hot = outs[: t.groups], outs[t.groups :]

        @pl.loop(0, sketch_ref.shape[0])
        def _(i):
            turned[i] = sketch_ref[i].T

        gather_blocks(t, tab, turned, main, hot)

    return kernel


def make_ppmi_kernel(t):
    def kernel(tab, match_ref, counts_ref, turned, *refs):
        sums_refs = refs[: t.groups]
        ppmi_ref, hot = refs[t.groups : t.groups + 2]
        main = refs[t.groups + 2 : 2 * t.groups + 2]
        cols_log = refs[-1]
        sums = jnp.concatenate([ref[...] for ref in sums_refs], axis=0)
        high = jnp.floor(sums * (1.0 / 256.0))
        low = sums - high * 256.0
        match = match_ref[...]
        margins = 256.0 * contract(match, high.astype(bf16), 1, 0) + contract(
            match, low.astype(bf16), 1, 0
        )
        log_total = jnp.log(jnp.sum(sums))
        log_margin = jnp.log(margins)
        cols_log[...] = log_margin
        fill = 128 - log_margin.shape[0] % 128
        row_log = jnp.concatenate(
            [log_margin, jnp.zeros((fill, log_margin.shape[1]), f32)], axis=0
        ).T
        for s in range(t.nnz):
            counts = counts_ref[s]
            scores = (
                jnp.log(counts.astype(f32))
                + log_total
                - row_log[:, s : s + 1]
                - cols_log[pl.ds(t.nnz + s, 1), :]
            )
            ppmi_ref[s] = jnp.where(counts > 0, jnp.maximum(scores, 0.0), 0.0).astype(bf16)
        products(t, tab, turned, ppmi_ref, main, hot)

    return kernel


def make_forward_kernel(t):
    def kernel(tab, ppmi_ref, *refs):
        main, hot = refs[: t.groups], refs[t.groups : t.groups + t.groups // 2]
        forward, picked = refs[-2:]
        for k in range(t.groups):
            s = tab[t.my_s + k]
            forward[s] = contract(main[k][...], ppmi_ref[s], 1, 1).astype(bf16)
        for m in range(t.hot):
            for n in range(t.groups // 2):

                @pl.when(tab[t.hot_k + m] == 2 * n)
                def _():
                    picked[...] = hot[n][m]

            s = t.groups + m
            forward[s] = contract(picked[...], ppmi_ref[s], 1, 1).astype(bf16)

    return kernel


def make_result_kernel(t):
    def kernel(tab, forward, *refs):
        main, hot = refs[: t.groups], refs[t.groups : 2 * t.groups]
        result = refs[-1]
        result[...] = jnp.zeros_like(result)
        for s in range(t.nnz):
            result[tab[t.row_i + s]] += forward[s].astype(f32)
        for k in range(t.groups):
            result[tab[t.main_j + k]] += main[k][...].astype(f32)
            for m in range(t.hot):
                j = tab[t.hot_j + k * t.hot + m]

                @pl.when(j >= 0)
                def _():
                    result[j] += hot[k][m].astype(f32)

    return kernel


def make_gram_kernel(t, chunk):
    def kernel(tab, own, other, *refs):
        outs, gram = refs[: t.groups], refs[-1]
        blocks, half, _ = own.shape
        me, my_col = tab[t.me], tab[t.col]
        gram[...] = jnp.zeros_like(gram)
        cut = half // 2

        @pl.loop(0, blocks)
        def _(i):
            mine = own[i]
            gram[pl.ds(0, half), :] += contract(mine, mine, 1, 1, HIGHEST)

            @pl.when(my_col == 0)
            def _():
                gram[pl.ds(half, cut), :] += contract(
                    other[i, pl.ds(0, cut), :], mine, 1, 1, HIGHEST
                )

            @pl.when(my_col == 1)
            def _():
                gram[pl.ds(half, cut), :] += contract(
                    own[i, pl.ds(cut, cut), :], other[i], 1, 1, HIGHEST
                )

        for k in range(t.groups):
            start = pl.multiple_of((me ^ k) * chunk, 8)
            outs[k][...] = gram[pl.ds(start, chunk), :]

    return kernel


def inverse_factor(block):
    size = block.shape[0]
    tiles = size // 8
    full = (8, size)
    lane = lax.broadcasted_iota(i32, full, 1)
    sub = lax.broadcasted_iota(i32, full, 0)
    left = [block[8 * t : 8 * t + 8, :] for t in range(tiles)]
    right = [(lane == sub + 8 * t).astype(f32) for t in range(tiles)]
    for j in range(tiles):
        cols = [jnp.broadcast_to(left[j][:, 8 * j + k : 8 * j + k + 1], full) for k in range(8)]
        pivot = [
            [jnp.broadcast_to(cols[k][i : i + 1, :], full) for k in range(i + 1)] for i in range(8)
        ]
        row_l = [jnp.broadcast_to(left[j][i : i + 1, :], full) for i in range(8)]
        row_r = [jnp.broadcast_to(right[j][i : i + 1, :], full) for i in range(8)]
        scale = []
        for k in range(8):
            scale.append(lax.rsqrt(pivot[k][k]))
            for i in range(k + 1, 8):
                pivot[i][k] = pivot[i][k] * scale[k]
            for i in range(k + 1, 8):
                for m in range(k + 1, i + 1):
                    pivot[i][m] = pivot[i][m] - pivot[i][k] * pivot[m][k]
            row_l[k] = row_l[k] * scale[k]
            row_r[k] = row_r[k] * scale[k]
            for i in range(k + 1, 8):
                row_l[i] = row_l[i] - pivot[i][k] * row_l[k]
                row_r[i] = row_r[i] - pivot[i][k] * row_r[k]
        done = row_r[0]
        for i in range(1, 8):
            done = jnp.where(sub == i, row_r[i], done)
        right[j] = done
        if j < tiles - 1:
            for k in range(7, -1, -1):
                row_l[k] = row_l[k] * scale[k]
                row_r[k] = row_r[k] * scale[k]
                for i in range(k):
                    row_l[i] = row_l[i] - pivot[k][i] * row_l[k]
                    row_r[i] = row_r[i] - pivot[k][i] * row_r[k]
            for t in range(j + 1, tiles):
                cur = left[t]
                new_l, new_r = cur, right[t]
                for k in range(8):
                    col = jnp.broadcast_to(cur[:, 8 * j + k : 8 * j + k + 1], full)
                    new_l = new_l - col * row_l[k]
                    new_r = new_r - col * row_r[k]
                left[t], right[t] = new_l, new_r
    return jnp.concatenate(right, axis=0)


def invert(t, tab, own, other, gram, inverse, scale):
    chunk, half = own[0].shape
    me, my_col = tab[t.me], tab[t.col]
    for k in range(t.groups):
        rows = pl.ds(pl.multiple_of((me ^ k) * chunk, 8), chunk)
        gram[my_col, rows, :] = own[k][...] * scale
        gram[1 - my_col, rows, :] = other[k][...] * scale
    cut = half // 2
    low = inverse_factor(gram[0, pl.ds(0, half), :])
    lower = jnp.concatenate([gram[0, pl.ds(half, cut), :], gram[1, pl.ds(half, cut), :]], axis=0)
    across = contract(lower, low, 1, 1, HIGHEST)
    high = inverse_factor(
        gram[1, pl.ds(0, half), :] - contract(across, across, 1, 1, HIGHEST)
    )
    inverse[0, 0] = low
    inverse[0, 1] = jnp.zeros_like(low)
    inverse[1, 0] = -contract(high, contract(across, low, 1, 0, HIGHEST), 1, 0, HIGHEST)
    inverse[1, 1] = high


def normal_block(inverse, mine, other, my_col, i):
    return contract(inverse[my_col, my_col], mine[i], 1, 0, HIGHEST) + contract(
        inverse[my_col, 1 - my_col], other[i], 1, 0, HIGHEST
    )


def start_copies(pairs, sems):
    copies = [pltpu.make_async_copy(a, b, sems.at[n]) for n, (a, b) in enumerate(pairs)]
    for copy in copies:
        copy.start()
    return copies


def make_second_kernel(t, scale):
    def kernel(tab, *refs):
        g = t.groups
        own_g, other_g = refs[:g], refs[g : 2 * g]
        mine_hbm, other_hbm, ppmi_hbm = refs[2 * g : 2 * g + 3]
        outs = refs[2 * g + 3 : 5 * g + 4]
        x_main, x_hot, t_main, t_hot = outs[:g], outs[g : 2 * g], outs[2 * g : 3 * g], outs[3 * g]
        gram, inverse, normal, mine, other, ppmi, sems = refs[5 * g + 4 :]
        copies = start_copies([(mine_hbm, mine), (other_hbm, other), (ppmi_hbm, ppmi)], sems)
        invert(t, tab, own_g, other_g, gram, inverse, scale)
        my_col = tab[t.col]
        for copy in copies:
            copy.wait()

        @pl.loop(0, normal.shape[0])
        def _(i):
            normal[i] = normal_block(inverse, mine, other, my_col, i).astype(bf16)

        gather_blocks(t, tab, normal, x_main, x_hot)
        products(t, tab, normal, ppmi, t_main, t_hot)

    return kernel


def make_final_kernel(t, scale):
    def kernel(tab, *refs):
        g = t.groups
        own_g, other_g = refs[:g], refs[g : 2 * g]
        mine_hbm, other_hbm, out_ref, gram, inverse, mine, other, sems = refs[2 * g :]
        copies = start_copies([(mine_hbm, mine), (other_hbm, other)], sems)
        invert(t, tab, own_g, other_g, gram, inverse, scale)
        my_col = tab[t.col]
        for copy in copies:
            copy.wait()

        @pl.loop(0, out_ref.shape[0])
        def _(i):
            out_ref[i] = normal_block(inverse, mine, other, my_col, i).T

    return kernel


def body(counts, block_pairs, sketch):
    groups = lax.axis_size("row")
    me = lax.axis_index("row")
    my_col = lax.axis_index("col")
    nnz, rows, _ = counts.shape
    blocks, _, half = sketch.shape
    vocab = blocks * rows * groups
    t = Table(groups, nnz)
    hot = t.hot
    chunk = -(-(half + half // 2) // (8 * groups)) * 8
    depth = -(-2 * nnz // 8) * 8

    def peer(x, k):
        return lax.ppermute(x, "row", [(r, r ^ k) for r in range(groups)])

    def swap(x):
        return lax.ppermute(x, "col", [(0, 1), (1, 0)])

    far_first = sorted(range(1, groups), reverse=True)

    def exchange(parts):
        got = {0: parts[0]}
        for k in far_first:
            got[k] = peer(parts[k], k)
        return [got[k] for k in range(groups)]

    def spread(part):
        return exchange([part] * groups)

    def spread_hot(part):
        got = {0: part}
        for k in far_first:
            if k % 2 == 0:
                got[k] = peer(part, k)
        for k in range(0, groups, 2):
            got[k + 1] = peer(got[k], 1)
        return [got[k] for k in range(groups)]

    def scatter_hot(parts, live):
        passed = {k: peer(parts[k + 1], 1) for k in range(0, groups, 2)}
        out = []
        for k in range(0, groups, 2):
            part = jnp.where(live[k][:, None, None], parts[k], passed[k])
            out.append(peer(part, k) if k else part)
        return out

    main_shapes = [shape((half, rows), bf16)] * groups
    hot_shape = shape((hot, half, rows), bf16)
    ppmi_shape = shape((nnz, rows, rows), bf16)
    result_shape = shape((blocks, half, rows), f32)

    sums = call(sums_kernel, shape((depth, rows), f32), [VMEM])(counts)
    sums_all = spread(sums)
    tab, theirs = t.build(block_pairs, me, my_col)
    hot_live = (tab[t.hot_j : t.hot_j + groups * hot] >= 0).reshape(groups, hot)

    source = call(
        make_source_kernel(t),
        [shape((blocks, half, rows), bf16)] + main_shapes + [hot_shape] * groups,
        [SMEM, VMEM],
    )(tab, sketch)
    turned = source[0]
    x_main = exchange(source[1 : 1 + groups])
    x_hot = scatter_hot(source[1 + groups :], hot_live)

    owner = (me ^ jnp.arange(groups))[:, None]
    row_ids = theirs[:, :, 0] * groups + owner
    col_ids = theirs[:, :, 2] * groups + theirs[:, :, 1]
    no_id = jnp.full((groups, depth - 2 * nnz), -1, i32)
    ids = jnp.concatenate([row_ids, col_ids, no_id], axis=1)
    match = (ids[0][:, None] == ids.reshape(-1)[None, :]).astype(bf16)

    found = call(
        make_ppmi_kernel(t),
        [ppmi_shape, hot_shape] + main_shapes,
        [SMEM] + [VMEM] * (3 + groups),
        scratch=[pltpu.VMEM((depth, rows), f32)],
    )(tab, match, counts, turned, *sums_all)
    ppmi, t_hot, t_main = found[0], found[1], found[2:]

    def finish(x_main, x_hot, t_main, t_hot):
        t_main = exchange(t_main)
        t_hot = spread_hot(t_hot)
        forward = call(
            make_forward_kernel(t),
            shape((nnz, half, rows), bf16),
            [SMEM] + [VMEM] * (1 + groups + groups // 2),
            scratch=[pltpu.VMEM((half, rows), bf16)],
        )(tab, ppmi, *x_main, *x_hot)
        result = call(
            make_result_kernel(t),
            result_shape,
            [SMEM] + [VMEM] * (1 + 2 * groups),
        )(tab, forward, *t_main, *t_hot)
        other = swap(result)
        part = call(
            make_gram_kernel(t, chunk),
            [shape((chunk, half), f32)] * groups,
            [SMEM, VMEM, VMEM],
            scratch=[pltpu.VMEM((groups * chunk, half), f32)],
        )(tab, result, other)
        gram = spread(sum(exchange(part)[1:], part[0]))
        return result, other, gram, [swap(x) for x in gram]

    gram_scratch = [
        pltpu.VMEM((2, groups * chunk, half), f32),
        pltpu.VMEM((2, 2, half, half), f32),
    ]
    result_scratch = [pltpu.VMEM((blocks, half, rows), f32)] * 2
    result, other, gram, other_gram = finish(x_main, x_hot, t_main, t_hot)
    second = call(
        make_second_kernel(t, 1.0 / vocab),
        main_shapes + [hot_shape] * groups + main_shapes + [hot_shape],
        [SMEM] + [VMEM] * (2 * groups) + [ANY] * 3,
        scratch=gram_scratch
        + [pltpu.VMEM((blocks, half, rows), bf16)]
        + result_scratch
        + [pltpu.VMEM((nnz, rows, rows), bf16), pltpu.SemaphoreType.DMA((3,))],
    )(tab, *gram, *other_gram, result, other, ppmi)
    x_main = exchange(second[:groups])
    x_hot = scatter_hot(second[groups : 2 * groups], hot_live)
    result, other, gram, other_gram = finish(
        x_main, x_hot, second[2 * groups : 3 * groups], second[3 * groups]
    )
    return call(
        make_final_kernel(t, 1.0 / vocab),
        shape((blocks, rows, half), f32),
        [SMEM] + [VMEM] * (2 * groups) + [ANY] * 2,
        scratch=gram_scratch + result_scratch + [pltpu.SemaphoreType.DMA((2,))],
    )(tab, *gram, *other_gram, result, other)


def solution(mesh):
    placed = (
        P(("decade", "row"), None, None),
        P("decade", None, None),
        P(None, ("decade", "row"), "col"),
    )
    return jax.shard_map(
        body,
        mesh=mesh,
        in_specs=placed,
        out_specs=P(None, ("decade", "row"), "col"),
        check_vma=False,
    )
```

```python
import jax
import jax.numpy as jnp
from jax import lax
from jax.experimental import pallas as pl
from jax.experimental.pallas import tpu as pltpu
from jax.sharding import PartitionSpec as P

MIB = 1 << 20
HIGHEST = lax.Precision.HIGHEST
VMEM = pl.BlockSpec(memory_space=pltpu.VMEM)
SMEM = pl.BlockSpec(memory_space=pltpu.SMEM)
ANY = pl.BlockSpec(memory_space=pl.ANY)
shape = jax.ShapeDtypeStruct
f32, bf16, i32 = jnp.float32, jnp.bfloat16, jnp.int32


def contract(a, b, a_dim, b_dim, precision=None):
    return lax.dot_general(
        a,
        b,
        (((a_dim,), (b_dim,)), ((), ())),
        precision=precision,
        preferred_element_type=f32,
    )


def call(kernel, out_shape, in_specs, out_specs=None, scratch=(), flops=0, vmem=32):
    if out_specs is None:
        out_specs = jax.tree.map(lambda _: VMEM, out_shape)
    return pl.pallas_call(
        kernel,
        out_shape=out_shape,
        in_specs=in_specs,
        out_specs=out_specs,
        scratch_shapes=list(scratch),
        compiler_params=pltpu.CompilerParams(vmem_limit_bytes=vmem * MIB),
        cost_estimate=pl.CostEstimate(flops=flops, bytes_accessed=4 * MIB, transcendentals=0),
    )


class Table:
    def __init__(self, groups, nnz):
        self.groups, self.nnz, self.hot = groups, nnz, nnz - groups
        self.main_j = 0
        self.hot_j = self.main_j + groups
        self.row_i = self.hot_j + groups * self.hot
        self.dest = self.row_i + nnz
        self.col = self.dest + nnz

    def build(self, block_pairs, me, my_col):
        groups = self.groups
        mine = lax.dynamic_index_in_dim(block_pairs, me, 0, keepdims=False)
        main = block_pairs[:, :groups]
        main_j = jnp.sum(jnp.where(main[:, :, 1] == me, main[:, :, 2], 0), axis=1)
        late = jnp.take(block_pairs[:, groups:], me ^ jnp.arange(groups), axis=0)
        hot_j = jnp.where(late[:, :, 1] == me, late[:, :, 2], -1).reshape(-1)
        parts = [main_j, hot_j, mine[:, 0], mine[:, 1], my_col[None]]
        return jnp.concatenate([p.astype(i32) for p in parts]), late[:, :, 1] ^ me


def sums_kernel(counts_ref, sums_ref):
    nnz, rows, cols = counts_ref.shape
    ones = jnp.ones((8, cols), bf16)
    sums_ref[0] = jnp.zeros(sums_ref.shape[1:], f32)
    for s in range(nnz):
        block = counts_ref[s].astype(bf16)
        sums_ref[0, pl.ds(s, 1), :] = contract(ones, block, 1, 1)[0:1, :]
        sums_ref[0, pl.ds(nnz + s, 1), :] = contract(ones, block, 1, 0)[0:1, :]
    for r in range(1, sums_ref.shape[0]):
        sums_ref[r] = sums_ref[0]


def gather_main(t, tab, blocks, send):
    for r in range(t.groups):
        send[r, 1] = blocks[tab[t.main_j + r]]


def gather_hot(t, tab, blocks, near, far):
    for k in range(t.groups):
        for m in range(t.hot):
            j = tab[t.hot_j + k * t.hot + m]

            @pl.when(j >= 0)
            def _():
                (far if k % 2 else near)[k // 2, m] = blocks[j]


def products(t, tab, blocks, ppmi, send, hot):
    for s in range(t.nnz):
        value = contract(blocks[tab[t.row_i + s]], ppmi[s], 1, 0).astype(bf16)
        if s < t.groups:
            send[tab[t.dest + s], 0] = value
        else:
            hot[0, s - t.groups] = value


def make_source_kernel(t):
    def kernel(tab, sketch_ref, turned, near, far):
        @pl.loop(0, sketch_ref.shape[0])
        def _(i):
            turned[i] = sketch_ref[i].T

        gather_hot(t, tab, turned, near, far)

    return kernel


def make_ppmi_kernel(t):
    def kernel(tab, match_ref, counts_ref, turned, sums_ref, ppmi_ref, send, hot, cols_log):
        sums = jnp.concatenate([sums_ref[r] for r in range(t.groups)], axis=0)
        high = jnp.floor(sums * (1.0 / 256.0))
        low = sums - high * 256.0
        match = match_ref[...]
        margins = 256.0 * contract(match, high.astype(bf16), 1, 0) + contract(
            match, low.astype(bf16), 1, 0
        )
        log_total = jnp.log(jnp.sum(sums))
        log_margin = jnp.log(margins)
        cols_log[...] = log_margin
        fill = 128 - log_margin.shape[0] % 128
        row_log = jnp.concatenate(
            [log_margin, jnp.zeros((fill, log_margin.shape[1]), f32)], axis=0
        ).T
        for s in range(t.nnz):
            counts = counts_ref[s]
            scores = (
                jnp.log(counts.astype(f32))
                + log_total
                - row_log[:, s : s + 1]
                - cols_log[pl.ds(t.nnz + s, 1), :]
            )
            ppmi_ref[s] = jnp.where(counts > 0, jnp.maximum(scores, 0.0), 0.0).astype(bf16)
        gather_main(t, tab, turned, send)
        products(t, tab, turned, ppmi_ref, send, hot)

    return kernel


def make_result_kernel(t, order):
    def kernel(tab, ppmi_ref, got, hot_x, hot_a, hot_b, result):
        result[...] = jnp.zeros_like(result)
        for s in range(t.nnz):
            block = got[tab[t.dest + s], 1] if s < t.groups else hot_x[0, s - t.groups]
            forward = contract(block, ppmi_ref[s], 1, 1).astype(bf16)
            result[tab[t.row_i + s]] += forward.astype(f32)
        for r in range(t.groups):
            result[tab[t.main_j + r]] += got[r, 0].astype(f32)
        for n, k in enumerate(order):
            ref, place = (hot_a, n) if n < t.groups // 2 else (hot_b, n - t.groups // 2)
            for m in range(t.hot):
                j = tab[t.hot_j + k * t.hot + m]

                @pl.when(j >= 0)
                def _():
                    result[j] += ref[place, m].astype(f32)

    return kernel


def split(x):
    high = x.astype(bf16)
    rest = x - high.astype(f32)
    mid = rest.astype(bf16)
    return high, mid, (rest - mid.astype(f32)).astype(bf16)


def lanes(ref, start, count, rows=None):
    picked = [ref[start + n] if rows is None else ref[start + n, rows, :] for n in range(count)]
    return jnp.concatenate(picked, axis=1)


def own_gram_kernel(own, gram):
    blocks, half, _ = own.shape
    step = 4
    square = jnp.zeros((half, half), f32)
    skew = jnp.zeros((half, half), f32)
    for i in range(0, blocks, step):
        high, mid, low = split(lanes(own, i, step))
        stack = contract(jnp.concatenate([high, mid, low], axis=0), high, 1, 1)
        square += stack[0:half] + contract(mid, mid, 1, 1)
        skew += stack[half : 2 * half] + stack[2 * half :]
    gram[...] = square + (skew + skew.T)


def make_cross_gram_kernel(t):
    def kernel(tab, own, other, square, gram):
        blocks, half, _ = own.shape
        cut = half // 2
        step = 4
        gram[pl.ds(0, half), :] = square[...]

        def cross(left, rows, right):
            total = jnp.zeros((cut, half), f32)
            for i in range(0, blocks, step):
                high, mid, low = split(lanes(left, i, step, rows))
                r_high, r_mid, r_low = split(lanes(right, i, step))
                by_high = contract(jnp.concatenate([high, mid, low], axis=0), r_high, 1, 1)
                by_mid = contract(jnp.concatenate([high, mid], axis=0), r_mid, 1, 1)
                small = by_high[2 * cut :] + by_mid[cut:] + contract(high, r_low, 1, 1)
                total += by_high[:cut] + (by_high[cut : 2 * cut] + by_mid[:cut] + small)
            gram[pl.ds(half, cut), :] = total

        @pl.when(tab[t.col] == 0)
        def _():
            cross(other, pl.ds(0, cut), own)

        @pl.when(tab[t.col] == 1)
        def _():
            cross(own, pl.ds(cut, cut), other)

    return kernel


def inverse_factor(block):
    size = block.shape[0]
    tiles = size // 8
    full = (8, size)
    lane = lax.broadcasted_iota(i32, full, 1)
    sub = lax.broadcasted_iota(i32, full, 0)
    left = [block[8 * t : 8 * t + 8, :] for t in range(tiles)]
    right = [(lane == sub + 8 * t).astype(f32) for t in range(tiles)]
    for j in range(tiles):
        cols = [jnp.broadcast_to(left[j][:, 8 * j + k : 8 * j + k + 1], full) for k in range(8)]
        pivot = [
            [jnp.broadcast_to(cols[k][i : i + 1, :], full) for k in range(i + 1)] for i in range(8)
        ]
        row_l = [jnp.broadcast_to(left[j][i : i + 1, :], full) for i in range(8)]
        row_r = [jnp.broadcast_to(right[j][i : i + 1, :], full) for i in range(8)]
        scale = []
        for k in range(8):
            scale.append(lax.rsqrt(pivot[k][k]))
            for i in range(k + 1, 8):
                pivot[i][k] = pivot[i][k] * scale[k]
            for i in range(k + 1, 8):
                for m in range(k + 1, i + 1):
                    pivot[i][m] = pivot[i][m] - pivot[i][k] * pivot[m][k]
            row_l[k] = row_l[k] * scale[k]
            row_r[k] = row_r[k] * scale[k]
            for i in range(k + 1, 8):
                row_l[i] = row_l[i] - pivot[i][k] * row_l[k]
                row_r[i] = row_r[i] - pivot[i][k] * row_r[k]
        done = row_r[0]
        for i in range(1, 8):
            done = jnp.where(sub == i, row_r[i], done)
        right[j] = done
        if j < tiles - 1:
            for k in range(7, -1, -1):
                row_l[k] = row_l[k] * scale[k]
                row_r[k] = row_r[k] * scale[k]
                for i in range(k):
                    row_l[i] = row_l[i] - pivot[k][i] * row_l[k]
                    row_r[i] = row_r[i] - pivot[k][i] * row_r[k]
            for t in range(j + 1, tiles):
                cur = left[t]
                new_l, new_r = cur, right[t]
                for k in range(8):
                    col = jnp.broadcast_to(cur[:, 8 * j + k : 8 * j + k + 1], full)
                    new_l = new_l - col * row_l[k]
                    new_r = new_r - col * row_r[k]
                left[t], right[t] = new_l, new_r
    return jnp.concatenate(right, axis=0)


def invert(t, tab, own, other, gram, inverse, scale):
    half = own.shape[1]
    cut = half // 2
    my_col = tab[t.col]
    gram[my_col] = own[...] * scale
    gram[1 - my_col] = other[...] * scale
    low = inverse_factor(gram[0, pl.ds(0, half), :])
    lower = jnp.concatenate([gram[0, pl.ds(half, cut), :], gram[1, pl.ds(half, cut), :]], axis=0)
    across = contract(lower, low, 1, 1, HIGHEST)
    high = inverse_factor(
        gram[1, pl.ds(0, half), :] - contract(across, across, 1, 1, HIGHEST)
    )
    inverse[0, 0] = low
    inverse[0, 1] = jnp.zeros_like(low)
    inverse[1, 0] = -contract(high, contract(across, low, 1, 0, HIGHEST), 1, 0, HIGHEST)
    inverse[1, 1] = high


def normal_blocks(t, tab, inverse, mine, other, store):
    my_col = tab[t.col]
    half = mine.shape[1]
    factor = jnp.concatenate([inverse[my_col, my_col], inverse[my_col, 1 - my_col]], axis=1)
    high, mid, low = split(factor)
    three = jnp.concatenate([high, mid, low], axis=0)
    two = jnp.concatenate([high, mid], axis=0)

    @pl.loop(0, mine.shape[0])
    def _(i):
        y_high, y_mid, y_low = split(jnp.concatenate([mine[i], other[i]], axis=0))
        by_high = contract(three, y_high, 1, 0)
        by_mid = contract(two, y_mid, 1, 0)
        small = by_high[2 * half :] + by_mid[half:] + contract(high, y_low, 1, 0)
        store(i, by_high[:half] + (by_high[half : 2 * half] + by_mid[:half] + small))


def start_copies(pairs, sems):
    copies = [pltpu.make_async_copy(a, b, sems.at[n]) for n, (a, b) in enumerate(pairs)]
    for copy in copies:
        copy.start()
    return copies


def make_second_kernel(t, scale):
    def kernel(
        tab, own_g, other_g, mine_hbm, other_hbm, ppmi_hbm, send, near, far, hot,
        gram, inverse, normal, mine, other, ppmi, sems,
    ):
        copies = start_copies([(mine_hbm, mine), (other_hbm, other), (ppmi_hbm, ppmi)], sems)
        invert(t, tab, own_g, other_g, gram, inverse, scale)
        for copy in copies:
            copy.wait()

        def store(i, value):
            normal[i] = value.astype(bf16)

        normal_blocks(t, tab, inverse, mine, other, store)
        gather_main(t, tab, normal, send)
        gather_hot(t, tab, normal, near, far)
        products(t, tab, normal, ppmi, send, hot)

    return kernel


def make_final_kernel(t, scale):
    def kernel(tab, own_g, other_g, mine_hbm, other_hbm, out, gram, inverse, mine, other, sems):
        copies = start_copies([(mine_hbm, mine), (other_hbm, other)], sems)
        invert(t, tab, own_g, other_g, gram, inverse, scale)
        for copy in copies:
            copy.wait()

        def store(i, value):
            out[i] = value.T

        normal_blocks(t, tab, inverse, mine, other, store)

    return kernel


def body(counts, block_pairs, sketch):
    groups = lax.axis_size("row")
    me = lax.axis_index("row")
    my_col = lax.axis_index("col")
    nnz, rows, _ = counts.shape
    blocks, _, half = sketch.shape
    vocab = blocks * rows * groups
    t = Table(groups, nnz)
    hot = t.hot
    depth = -(-2 * nnz // 8) * 8
    bits = [1 << b for b in range(groups.bit_length() - 1)]

    def peer(x, k):
        return lax.ppermute(x, "row", [(r, r ^ k) for r in range(groups)])

    def swap(x):
        return lax.ppermute(x, "col", [(0, 1), (1, 0)])

    def exchange(x):
        return lax.all_to_all(x, "row", split_axis=0, concat_axis=0, tiled=True)

    def add_up(x):
        for bit in bits:
            x = x + peer(x, bit)
        return x

    def spread_hot(part):
        for bit in bits[:0:-1]:
            part = jnp.concatenate([part, peer(part, bit)], axis=0)
        return part, peer(part, bits[0])

    hot_order = [0]
    for bit in bits[::-1]:
        hot_order += [k ^ bit for k in hot_order]

    def scatter_hot(near, far, towards):
        for bit in bits:
            got = peer(far, bit)
            towards = towards[::2]
            stay = (towards & bit) == 0
            part = jnp.where(stay[:, :, None, None], near, got)
            near, far = part[::2], part[1::2]
        return part

    send_shape = shape((groups, 2, half, rows), bf16)
    hot_shape = shape((1, hot, half, rows), bf16)
    side_shape = shape((groups // 2, hot, half, rows), bf16)
    ppmi_shape = shape((nnz, rows, rows), bf16)
    result_shape = shape((blocks, half, rows), f32)

    sums = call(sums_kernel, shape((groups, depth, rows), f32), [VMEM])(counts)
    sums_all = exchange(sums)
    tab, towards = t.build(block_pairs, me, my_col)
    turned, near, far = call(
        make_source_kernel(t),
        [shape((blocks, half, rows), bf16), side_shape, side_shape],
        [SMEM, VMEM],
    )(tab, sketch)
    hot_x = scatter_hot(near, far, towards)

    row_ids = block_pairs[:, :, 0] * groups + jnp.arange(groups)[:, None]
    col_ids = block_pairs[:, :, 2] * groups + block_pairs[:, :, 1]
    no_id = jnp.full((groups, depth - 2 * nnz), -1, i32)
    ids = jnp.concatenate([row_ids, col_ids, no_id], axis=1)
    my_ids = lax.dynamic_index_in_dim(ids, me, 0, keepdims=False)
    match = (my_ids[:, None] == ids.reshape(-1)[None, :]).astype(bf16)

    ppmi, send, hot_t = call(
        make_ppmi_kernel(t),
        [ppmi_shape, send_shape, hot_shape],
        [SMEM] + [VMEM] * 4,
        scratch=[pltpu.VMEM((depth, rows), f32)],
    )(tab, match, counts, turned, sums_all)

    def finish(send, hot_x, hot_t):
        got = exchange(send)
        hot_a, hot_b = spread_hot(hot_t)
        result = call(
            make_result_kernel(t, hot_order),
            result_shape,
            [SMEM] + [VMEM] * 5,
        )(tab, ppmi, got, hot_x, hot_a, hot_b)
        other = swap(result)
        square = call(own_gram_kernel, shape((half, half), f32), [VMEM])(result)
        gram = call(
            make_cross_gram_kernel(t),
            shape((half + half // 2, half), f32),
            [SMEM] + [VMEM] * 3,
        )(tab, result, other, square)
        gram = add_up(gram)
        return result, other, gram, swap(gram)

    gram_scratch = [
        pltpu.VMEM((2, half + half // 2, half), f32),
        pltpu.VMEM((2, 2, half, half), f32),
    ]
    result_scratch = [pltpu.VMEM((blocks, half, rows), f32)] * 2
    result, other, gram, other_gram = finish(send, hot_x, hot_t)
    send, near, far, hot_t = call(
        make_second_kernel(t, 1.0 / vocab),
        [send_shape, side_shape, side_shape, hot_shape],
        [SMEM] + [VMEM] * 2 + [ANY] * 3,
        scratch=gram_scratch
        + [pltpu.VMEM((blocks, half, rows), bf16)]
        + result_scratch
        + [pltpu.VMEM((nnz, rows, rows), bf16), pltpu.SemaphoreType.DMA((3,))],
    )(tab, gram, other_gram, result, other, ppmi)
    hot_x = scatter_hot(near, far, towards)
    result, other, gram, other_gram = finish(send, hot_x, hot_t)
    return call(
        make_final_kernel(t, 1.0 / vocab),
        shape((blocks, rows, half), f32),
        [SMEM] + [VMEM] * 2 + [ANY] * 2,
        scratch=gram_scratch + result_scratch + [pltpu.SemaphoreType.DMA((2,))],
    )(tab, gram, other_gram, result, other)


def solution(mesh):
    placed = (
        P(("decade", "row"), None, None),
        P("decade", None, None),
        P(None, ("decade", "row"), "col"),
    )
    return jax.shard_map(
        body,
        mesh=mesh,
        in_specs=placed,
        out_specs=P(None, ("decade", "row"), "col"),
        check_vma=False,
    )
```

```python
import jax
import jax.numpy as jnp
from jax import lax
from jax.experimental import pallas as pl
from jax.experimental.pallas import tpu as pltpu
from jax.sharding import PartitionSpec as P

MIB = 1 << 20
HIGHEST = lax.Precision.HIGHEST
VMEM = pl.BlockSpec(memory_space=pltpu.VMEM)
SMEM = pl.BlockSpec(memory_space=pltpu.SMEM)
ANY = pl.BlockSpec(memory_space=pl.ANY)
shape = jax.ShapeDtypeStruct
f32, bf16, i32 = jnp.float32, jnp.bfloat16, jnp.int32


def contract(a, b, a_dim, b_dim, precision=None):
    return lax.dot_general(
        a,
        b,
        (((a_dim,), (b_dim,)), ((), ())),
        precision=precision,
        preferred_element_type=f32,
    )


def call(kernel, out_shape, in_specs, out_specs=None, scratch=(), flops=0, vmem=32):
    if out_specs is None:
        out_specs = jax.tree.map(lambda _: VMEM, out_shape)
    return pl.pallas_call(
        kernel,
        out_shape=out_shape,
        in_specs=in_specs,
        out_specs=out_specs,
        scratch_shapes=list(scratch),
        compiler_params=pltpu.CompilerParams(vmem_limit_bytes=vmem * MIB),
        cost_estimate=pl.CostEstimate(flops=flops, bytes_accessed=4 * MIB, transcendentals=0),
    )


class Table:
    def __init__(self, groups, nnz):
        self.groups, self.nnz, self.hot = groups, nnz, nnz - groups
        self.main_j = 0
        self.hot_j = self.main_j + groups
        self.row_i = self.hot_j + groups * self.hot
        self.dest = self.row_i + nnz
        self.col = self.dest + nnz

    def build(self, block_pairs, me, my_col):
        groups = self.groups
        mine = lax.dynamic_index_in_dim(block_pairs, me, 0, keepdims=False)
        main = block_pairs[:, :groups]
        main_j = jnp.sum(jnp.where(main[:, :, 1] == me, main[:, :, 2], 0), axis=1)
        late = jnp.take(block_pairs[:, groups:], me ^ jnp.arange(groups), axis=0)
        hot_j = jnp.where(late[:, :, 1] == me, late[:, :, 2], -1).reshape(-1)
        parts = [main_j, hot_j, mine[:, 0], mine[:, 1], my_col[None]]
        return jnp.concatenate([p.astype(i32) for p in parts]), late[:, :, 1] ^ me


def sums_kernel(counts_ref, sums_ref):
    nnz, rows, cols = counts_ref.shape
    ones = jnp.ones((8, cols), bf16)
    sums_ref[0] = jnp.zeros(sums_ref.shape[1:], f32)
    for s in range(nnz):
        block = counts_ref[s].astype(bf16)
        sums_ref[0, pl.ds(s, 1), :] = contract(ones, block, 1, 1)[0:1, :]
        sums_ref[0, pl.ds(nnz + s, 1), :] = contract(ones, block, 1, 0)[0:1, :]
    for r in range(1, sums_ref.shape[0]):
        sums_ref[r] = sums_ref[0]


def gather_hot(t, tab, blocks, near, far):
    for k in range(t.groups):
        for m in range(t.hot):
            j = tab[t.hot_j + k * t.hot + m]

            @pl.when(j >= 0)
            def _():
                (far if k % 2 else near)[k // 2, m] = blocks[j]


def product(t, tab, blocks, ppmi, s):
    return contract(blocks[tab[t.row_i + s]], ppmi[s], 1, 0).astype(bf16)


def hot_products(t, tab, blocks, ppmi, hot):
    for m in range(t.hot):
        hot[0, m] = product(t, tab, blocks, ppmi, t.groups + m)


def make_main_kernel(t):
    def kernel(tab, blocks, ppmi, send):
        for r in range(t.groups):
            send[r, 1] = blocks[tab[t.main_j + r]]
        for s in range(t.groups):
            send[tab[t.dest + s], 0] = product(t, tab, blocks, ppmi, s)

    return kernel


def make_source_kernel(t):
    def kernel(tab, sketch_ref, turned, near, far):
        @pl.loop(0, sketch_ref.shape[0])
        def _(i):
            turned[i] = sketch_ref[i].T

        gather_hot(t, tab, turned, near, far)

    return kernel


def make_ppmi_kernel(t):
    def kernel(tab, match_ref, counts_ref, turned, sums_ref, ppmi_ref, hot, cols_log):
        sums = jnp.concatenate([sums_ref[r] for r in range(t.groups)], axis=0)
        high = jnp.floor(sums * (1.0 / 256.0))
        low = sums - high * 256.0
        match = match_ref[...]
        margins = 256.0 * contract(match, high.astype(bf16), 1, 0) + contract(
            match, low.astype(bf16), 1, 0
        )
        log_total = jnp.log(jnp.sum(sums))
        log_margin = jnp.log(margins)
        cols_log[...] = log_margin
        fill = 128 - log_margin.shape[0] % 128
        row_log = jnp.concatenate(
            [log_margin, jnp.zeros((fill, log_margin.shape[1]), f32)], axis=0
        ).T
        for s in range(t.nnz):
            counts = counts_ref[s]
            scores = (
                jnp.log(counts.astype(f32))
                + log_total
                - row_log[:, s : s + 1]
                - cols_log[pl.ds(t.nnz + s, 1), :]
            )
            ppmi_ref[s] = jnp.where(counts > 0, jnp.maximum(scores, 0.0), 0.0).astype(bf16)
        hot_products(t, tab, turned, ppmi_ref, hot)

    return kernel


def make_result_kernel(t, order):
    def kernel(tab, ppmi_ref, got, hot_x, hot_a, hot_b, result):
        result[...] = jnp.zeros_like(result)
        for s in range(t.nnz):
            block = got[tab[t.dest + s], 1] if s < t.groups else hot_x[0, s - t.groups]
            forward = contract(block, ppmi_ref[s], 1, 1).astype(bf16)
            result[tab[t.row_i + s]] += forward.astype(f32)
        for r in range(t.groups):
            result[tab[t.main_j + r]] += got[r, 0].astype(f32)
        for n, k in enumerate(order):
            ref, place = (hot_a, n) if n < t.groups // 2 else (hot_b, n - t.groups // 2)
            for m in range(t.hot):
                j = tab[t.hot_j + k * t.hot + m]

                @pl.when(j >= 0)
                def _():
                    result[j] += ref[place, m].astype(f32)

    return kernel


def split(x):
    high = x.astype(bf16)
    rest = x - high.astype(f32)
    mid = rest.astype(bf16)
    return high, mid, (rest - mid.astype(f32)).astype(bf16)


def lanes(ref, start, count, rows=None):
    picked = [ref[start + n] if rows is None else ref[start + n, rows, :] for n in range(count)]
    return jnp.concatenate(picked, axis=1)


def own_gram_kernel(own, gram):
    blocks, half, _ = own.shape
    step = 4
    square = jnp.zeros((half, half), f32)
    skew = jnp.zeros((half, half), f32)
    for i in range(0, blocks, step):
        high, mid, low = split(lanes(own, i, step))
        stack = contract(jnp.concatenate([high, mid, low], axis=0), high, 1, 1)
        square += stack[0:half] + contract(mid, mid, 1, 1)
        skew += stack[half : 2 * half] + stack[2 * half :]
    gram[...] = square + (skew + skew.T)


def make_cross_gram_kernel(t):
    def kernel(tab, own, other, square, gram):
        blocks, half, _ = own.shape
        cut = half // 2
        step = 4
        gram[pl.ds(0, half), :] = square[...]

        def cross(left, rows, right):
            total = jnp.zeros((cut, half), f32)
            for i in range(0, blocks, step):
                high, mid, low = split(lanes(left, i, step, rows))
                r_high, r_mid, r_low = split(lanes(right, i, step))
                by_high = contract(jnp.concatenate([high, mid, low], axis=0), r_high, 1, 1)
                by_mid = contract(jnp.concatenate([high, mid], axis=0), r_mid, 1, 1)
                small = by_high[2 * cut :] + by_mid[cut:] + contract(high, r_low, 1, 1)
                total += by_high[:cut] + (by_high[cut : 2 * cut] + by_mid[:cut] + small)
            gram[pl.ds(half, cut), :] = total

        @pl.when(tab[t.col] == 0)
        def _():
            cross(other, pl.ds(0, cut), own)

        @pl.when(tab[t.col] == 1)
        def _():
            cross(own, pl.ds(cut, cut), other)

    return kernel


def pivot_rows(left, right, base):
    full = left.shape
    cols = [jnp.broadcast_to(left[:, base + k : base + k + 1], full) for k in range(8)]
    piv = [[jnp.broadcast_to(cols[k][i : i + 1, :], full) for k in range(i + 1)] for i in range(8)]
    rows = [
        [jnp.broadcast_to(side[i : i + 1, :], full) for side in (left, right)] for i in range(8)
    ]
    scale = []
    for k in range(0, 8, 2):
        a, b, c = piv[k][k], piv[k + 1][k], piv[k + 1][k + 1]
        det = a * c - b * b
        root, det_root = lax.rsqrt(a), lax.rsqrt(det)
        both = det_root * root
        scale += [root, det_root * (a * root)]
        piv[k + 1][k] = b * root
        for i in range(k + 2, 8):
            p, q = piv[i][k], piv[i][k + 1]
            piv[i][k] = p * root
            piv[i][k + 1] = (a * q - b * p) * both
        for i in range(k + 2, 8):
            for m in range(k + 2, i + 1):
                piv[i][m] = piv[i][m] - (
                    piv[i][k] * piv[m][k] + piv[i][k + 1] * piv[m][k + 1]
                )
        for side in range(2):
            first = rows[k][side] * root
            second = (rows[k + 1][side] - piv[k + 1][k] * first) * scale[k + 1]
            rows[k][side], rows[k + 1][side] = first, second
            for i in range(k + 2, 8):
                rows[i][side] = rows[i][side] - (piv[i][k] * first + piv[i][k + 1] * second)
    solved = [list(row) for row in rows]
    for k in range(7, -1, -1):
        for side in range(2):
            solved[k][side] = solved[k][side] * scale[k]
            for i in range(k):
                solved[i][side] = solved[i][side] - piv[k][i] * solved[k][side]
    return rows, solved


def inverse_factor(block):
    size = block.shape[0]
    tiles = size // 8
    panel = 4
    full = (8, size)
    lane = lax.broadcasted_iota(i32, full, 1)
    sub = lax.broadcasted_iota(i32, full, 0)
    sides = [
        [block[8 * t : 8 * t + 8, :], (lane == sub + 8 * t).astype(f32)] for t in range(tiles)
    ]
    for first in range(0, tiles, panel):
        last = first + panel
        for j in range(first, last):
            rows, solved = pivot_rows(*sides[j], 8 * j)
            for t in range(j + 1, last):
                old = sides[t][0]
                new = list(sides[t])
                for k in range(8):
                    col = jnp.broadcast_to(old[:, 8 * j + k : 8 * j + k + 1], full)
                    new = [new[n] - col * solved[k][n] for n in range(2)]
                sides[t] = new
            for n in range(2):
                done = rows[0][n]
                for i in range(1, 8):
                    done = jnp.where(sub == i, rows[i][n], done)
                sides[j][n] = done
        if last < tiles:
            left = jnp.concatenate([sides[t][0] for t in range(first, last)], axis=0)
            right = jnp.concatenate([sides[t][1] for t in range(first, last)], axis=0)
            high, mid, low = split(left)
            r_high, r_mid, r_low = split(jnp.concatenate([left, right], axis=1))
            change = contract(
                jnp.concatenate([high, high, mid, mid, high, low], axis=0),
                jnp.concatenate([r_high, r_mid, r_high, r_mid, r_low, r_high], axis=0),
                0,
                0,
            )
            for t in range(last, tiles):
                part = change[8 * t : 8 * t + 8, :]
                sides[t] = [sides[t][0] - part[:, :size], sides[t][1] - part[:, size:]]
    return jnp.concatenate([side[1] for side in sides], axis=0)


def invert(t, tab, own, other, gram, inverse, scale):
    half = own.shape[1]
    cut = half // 2
    my_col = tab[t.col]
    gram[my_col] = own[...] * scale
    gram[1 - my_col] = other[...] * scale
    low = inverse_factor(gram[0, pl.ds(0, half), :])
    lower = jnp.concatenate([gram[0, pl.ds(half, cut), :], gram[1, pl.ds(half, cut), :]], axis=0)
    across = contract(lower, low, 1, 1, HIGHEST)
    high = inverse_factor(
        gram[1, pl.ds(0, half), :] - contract(across, across, 1, 1, HIGHEST)
    )
    inverse[0, 0] = low
    inverse[0, 1] = jnp.zeros_like(low)
    inverse[1, 0] = -contract(high, contract(across, low, 1, 0, HIGHEST), 1, 0, HIGHEST)
    inverse[1, 1] = high


def normal_blocks(t, tab, inverse, mine, other, store):
    my_col = tab[t.col]
    half = mine.shape[1]
    factor = jnp.concatenate([inverse[my_col, my_col], inverse[my_col, 1 - my_col]], axis=1)
    high, mid, low = split(factor)
    three = jnp.concatenate([high, mid, low], axis=0)
    two = jnp.concatenate([high, mid], axis=0)

    @pl.loop(0, mine.shape[0])
    def _(i):
        y_high, y_mid, y_low = split(jnp.concatenate([mine[i], other[i]], axis=0))
        by_high = contract(three, y_high, 1, 0)
        by_mid = contract(two, y_mid, 1, 0)
        small = by_high[2 * half :] + by_mid[half:] + contract(high, y_low, 1, 0)
        store(i, by_high[:half] + (by_high[half : 2 * half] + by_mid[:half] + small))


def start_copies(pairs, sems):
    copies = [pltpu.make_async_copy(a, b, sems.at[n]) for n, (a, b) in enumerate(pairs)]
    for copy in copies:
        copy.start()
    return copies


def make_second_kernel(t, scale):
    def kernel(
        tab, own_g, other_g, mine_hbm, other_hbm, ppmi_hbm, normal, near, far, hot,
        gram, inverse, mine, other, ppmi, sems,
    ):
        copies = start_copies([(mine_hbm, mine), (other_hbm, other), (ppmi_hbm, ppmi)], sems)
        invert(t, tab, own_g, other_g, gram, inverse, scale)
        for copy in copies:
            copy.wait()

        def store(i, value):
            normal[i] = value.astype(bf16)

        normal_blocks(t, tab, inverse, mine, other, store)
        gather_hot(t, tab, normal, near, far)
        hot_products(t, tab, normal, ppmi, hot)

    return kernel


def make_final_kernel(t, scale):
    def kernel(tab, own_g, other_g, mine_hbm, other_hbm, out, gram, inverse, mine, other, sems):
        copies = start_copies([(mine_hbm, mine), (other_hbm, other)], sems)
        invert(t, tab, own_g, other_g, gram, inverse, scale)
        for copy in copies:
            copy.wait()

        def store(i, value):
            out[i] = value.T

        normal_blocks(t, tab, inverse, mine, other, store)

    return kernel


def body(counts, block_pairs, sketch):
    groups = lax.axis_size("row")
    me = lax.axis_index("row")
    my_col = lax.axis_index("col")
    nnz, rows, _ = counts.shape
    blocks, _, half = sketch.shape
    vocab = blocks * rows * groups
    t = Table(groups, nnz)
    hot = t.hot
    depth = -(-2 * nnz // 8) * 8
    bits = [1 << b for b in range(groups.bit_length() - 1)]

    def peer(x, k):
        return lax.ppermute(x, "row", [(r, r ^ k) for r in range(groups)])

    def swap(x):
        return lax.ppermute(x, "col", [(0, 1), (1, 0)])

    def exchange(x):
        return lax.all_to_all(x, "row", split_axis=0, concat_axis=0, tiled=True)

    def add_up(x):
        for bit in bits:
            x = x + peer(x, bit)
        return x

    def spread_hot(part, got):
        part = jnp.concatenate([part, got], axis=0)
        for bit in bits[-2:0:-1]:
            part = jnp.concatenate([part, peer(part, bit)], axis=0)
        return part, peer(part, bits[0])

    hot_order = [0]
    for bit in bits[::-1]:
        hot_order += [k ^ bit for k in hot_order]

    def scatter_hot(near, far, got, towards):
        for bit in bits:
            if bit > 1:
                got = peer(far, bit)
            towards = towards[::2]
            stay = (towards & bit) == 0
            part = jnp.where(stay[:, :, None, None], near, got)
            near, far = part[::2], part[1::2]
        return part

    send_shape = shape((groups, 2, half, rows), bf16)
    hot_shape = shape((1, hot, half, rows), bf16)
    side_shape = shape((groups // 2, hot, half, rows), bf16)
    ppmi_shape = shape((nnz, rows, rows), bf16)
    result_shape = shape((blocks, half, rows), f32)

    sums = call(sums_kernel, shape((groups, depth, rows), f32), [VMEM])(counts)
    sums_all = exchange(sums)
    tab, towards = t.build(block_pairs, me, my_col)
    turned, near, far = call(
        make_source_kernel(t),
        [shape((blocks, half, rows), bf16), side_shape, side_shape],
        [SMEM, VMEM],
    )(tab, sketch)

    row_ids = block_pairs[:, :, 0] * groups + jnp.arange(groups)[:, None]
    col_ids = block_pairs[:, :, 2] * groups + block_pairs[:, :, 1]
    no_id = jnp.full((groups, depth - 2 * nnz), -1, i32)
    ids = jnp.concatenate([row_ids, col_ids, no_id], axis=1)
    my_ids = lax.dynamic_index_in_dim(ids, me, 0, keepdims=False)
    match = (my_ids[:, None] == ids.reshape(-1)[None, :]).astype(bf16)

    ppmi, hot_t = call(
        make_ppmi_kernel(t),
        [ppmi_shape, hot_shape],
        [SMEM] + [VMEM] * 4,
        scratch=[pltpu.VMEM((depth, rows), f32)],
    )(tab, match, counts, turned, sums_all)

    def finish(source, near, far, hot_t):
        send = call(make_main_kernel(t), send_shape, [SMEM, VMEM, VMEM])(tab, source, ppmi)
        send, x_step, t_step = lax.optimization_barrier(
            (send, peer(far, bits[0]), peer(hot_t, bits[-1]))
        )
        got = exchange(send)
        hot_x = scatter_hot(near, far, x_step, towards)
        hot_a, hot_b = spread_hot(hot_t, t_step)
        result = call(
            make_result_kernel(t, hot_order),
            result_shape,
            [SMEM] + [VMEM] * 5,
        )(tab, ppmi, got, hot_x, hot_a, hot_b)
        other = swap(result)
        square = call(own_gram_kernel, shape((half, half), f32), [VMEM])(result)
        gram = call(
            make_cross_gram_kernel(t),
            shape((half + half // 2, half), f32),
            [SMEM] + [VMEM] * 3,
        )(tab, result, other, square)
        gram = add_up(gram)
        return result, other, gram, swap(gram)

    gram_scratch = [
        pltpu.VMEM((2, half + half // 2, half), f32),
        pltpu.VMEM((2, 2, half, half), f32),
    ]
    result_scratch = [pltpu.VMEM((blocks, half, rows), f32)] * 2
    result, other, gram, other_gram = finish(turned, near, far, hot_t)
    normal, near, far, hot_t = call(
        make_second_kernel(t, 1.0 / vocab),
        [shape((blocks, half, rows), bf16), side_shape, side_shape, hot_shape],
        [SMEM] + [VMEM] * 2 + [ANY] * 3,
        scratch=gram_scratch
        + result_scratch
        + [pltpu.VMEM((nnz, rows, rows), bf16), pltpu.SemaphoreType.DMA((3,))],
    )(tab, gram, other_gram, result, other, ppmi)
    result, other, gram, other_gram = finish(normal, near, far, hot_t)
    return call(
        make_final_kernel(t, 1.0 / vocab),
        shape((blocks, rows, half), f32),
        [SMEM] + [VMEM] * 2 + [ANY] * 2,
        scratch=gram_scratch + result_scratch + [pltpu.SemaphoreType.DMA((2,))],
    )(tab, gram, other_gram, result, other)


def solution(mesh):
    placed = (
        P(("decade", "row"), None, None),
        P("decade", None, None),
        P(None, ("decade", "row"), "col"),
    )
    return jax.shard_map(
        body,
        mesh=mesh,
        in_specs=placed,
        out_specs=P(None, ("decade", "row"), "col"),
        check_vma=False,
    )
```

```python
import jax
import jax.numpy as jnp
from jax import lax
from jax.experimental import pallas as pl
from jax.experimental.pallas import tpu as pltpu
from jax.sharding import PartitionSpec as P

MIB = 1 << 20
HIGHEST = lax.Precision.HIGHEST
VMEM = pl.BlockSpec(memory_space=pltpu.VMEM)
SMEM = pl.BlockSpec(memory_space=pltpu.SMEM)
ANY = pl.BlockSpec(memory_space=pl.ANY)
shape = jax.ShapeDtypeStruct
f32, bf16, i32 = jnp.float32, jnp.bfloat16, jnp.int32


def contract(a, b, a_dim, b_dim, precision=None):
    return lax.dot_general(
        a,
        b,
        (((a_dim,), (b_dim,)), ((), ())),
        precision=precision,
        preferred_element_type=f32,
    )


def call(kernel, out_shape, in_specs, out_specs=None, scratch=(), flops=0, vmem=20):
    if out_specs is None:
        out_specs = jax.tree.map(lambda _: VMEM, out_shape)
    return pl.pallas_call(
        kernel,
        out_shape=out_shape,
        in_specs=in_specs,
        out_specs=out_specs,
        scratch_shapes=list(scratch),
        compiler_params=pltpu.CompilerParams(vmem_limit_bytes=vmem * MIB),
        cost_estimate=pl.CostEstimate(flops=flops, bytes_accessed=4 * MIB, transcendentals=0),
    )


class Table:
    def __init__(self, groups, nnz):
        self.groups, self.nnz, self.hot = groups, nnz, nnz - groups
        bits = [1 << b for b in range(groups.bit_length() - 1)]
        self.bits = bits
        self.steps = bits[1:-1] + bits[:1] + bits[-1:]
        self.main_j = 0
        self.hot_j = self.main_j + groups
        self.row_i = self.hot_j + groups * self.hot
        self.dest = self.row_i + nnz
        self.col = self.dest + nnz

    def build(self, block_pairs, me, my_col):
        groups = self.groups
        mine = lax.dynamic_index_in_dim(block_pairs, me, 0, keepdims=False)
        main = block_pairs[:, :groups]
        main_j = jnp.sum(jnp.where(main[:, :, 1] == me, main[:, :, 2], 0), axis=1)
        late = jnp.take(block_pairs[:, groups:], me ^ jnp.arange(groups), axis=0)
        hot_j = jnp.where(late[:, :, 1] == me, late[:, :, 2], -1).reshape(-1)
        parts = [main_j, hot_j, mine[:, 0], mine[:, 1], my_col[None]]
        return jnp.concatenate([p.astype(i32) for p in parts]), late[:, :, 1] ^ me


def sums_kernel(counts_ref, sums_ref):
    nnz, rows, cols = counts_ref.shape
    ones = jnp.ones((8, cols), bf16)
    sums_ref[0] = jnp.zeros(sums_ref.shape[1:], f32)
    for s in range(nnz):
        block = counts_ref[s].astype(bf16)
        sums_ref[0, pl.ds(s, 1), :] = contract(ones, block, 1, 1)[0:1, :]
        sums_ref[0, pl.ds(nnz + s, 1), :] = contract(ones, block, 1, 0)[0:1, :]
    for r in range(1, sums_ref.shape[0]):
        sums_ref[r] = sums_ref[0]


def gather_hot(t, tab, blocks, near, far):
    bit = t.steps[0]
    for k in range(t.groups):
        place = (k // (2 * bit)) * bit + k % bit
        for m in range(t.hot):
            j = tab[t.hot_j + k * t.hot + m]

            @pl.when(j >= 0)
            def _():
                (far if k & bit else near)[place, m] = blocks[j]


def product(t, tab, blocks, ppmi, s):
    return contract(blocks[tab[t.row_i + s]], ppmi[s], 1, 0).astype(bf16)


def hot_products(t, tab, blocks, ppmi, hot):
    for m in range(t.hot):
        hot[0, m] = product(t, tab, blocks, ppmi, t.groups + m)


def gather_main(t, tab, blocks, send, slot):
    for r in range(t.groups):
        send[r, slot] = blocks[tab[t.main_j + r]]


def make_main_kernel(t, with_blocks):
    def kernel(tab, blocks, ppmi, send):
        if with_blocks:
            gather_main(t, tab, blocks, send, 1)
        for s in range(t.groups):
            send[tab[t.dest + s], 0] = product(t, tab, blocks, ppmi, s)

    return kernel


def make_source_kernel(t):
    def kernel(tab, sketch_ref, turned, send, near, far):
        @pl.loop(0, sketch_ref.shape[0])
        def _(i):
            turned[i] = sketch_ref[i].T

        gather_main(t, tab, turned, send, 0)
        gather_hot(t, tab, turned, near, far)

    return kernel


def make_ppmi_kernel(t):
    def kernel(tab, match_ref, counts_ref, turned, sums_ref, ppmi_ref, hot, cols_log):
        sums = jnp.concatenate([sums_ref[r] for r in range(t.groups)], axis=0)
        high = jnp.floor(sums * (1.0 / 256.0))
        low = sums - high * 256.0
        match = match_ref[...]
        margins = 256.0 * contract(match, high.astype(bf16), 1, 0) + contract(
            match, low.astype(bf16), 1, 0
        )
        log_total = jnp.log(jnp.sum(sums))
        log_margin = jnp.log(margins)
        cols_log[...] = log_margin
        fill = 128 - log_margin.shape[0] % 128
        row_log = jnp.concatenate(
            [log_margin, jnp.zeros((fill, log_margin.shape[1]), f32)], axis=0
        ).T
        for s in range(t.nnz):
            counts = counts_ref[s]
            scores = (
                jnp.log(counts.astype(f32))
                + log_total
                - row_log[:, s : s + 1]
                - cols_log[pl.ds(t.nnz + s, 1), :]
            )
            ppmi_ref[s] = jnp.where(counts > 0, jnp.maximum(scores, 0.0), 0.0).astype(bf16)
        hot_products(t, tab, turned, ppmi_ref, hot)

    return kernel


def make_result_kernel(t, order):
    def kernel(tab, ppmi_ref, *refs):
        got_t, got_x = refs[0], refs[-5]
        hot_x, hot_a, hot_b, result = refs[-4:]
        slot = got_x.shape[1] - 1
        result[...] = jnp.zeros_like(result)
        for s in range(t.nnz):
            block = got_x[tab[t.dest + s], slot] if s < t.groups else hot_x[0, s - t.groups]
            forward = contract(block, ppmi_ref[s], 1, 1).astype(bf16)
            result[tab[t.row_i + s]] += forward.astype(f32)
        for r in range(t.groups):
            result[tab[t.main_j + r]] += got_t[r, 0].astype(f32)
        for n, k in enumerate(order):
            ref, place = (hot_a, n) if n < t.groups // 2 else (hot_b, n - t.groups // 2)
            for m in range(t.hot):
                j = tab[t.hot_j + k * t.hot + m]

                @pl.when(j >= 0)
                def _():
                    result[j] += ref[place, m].astype(f32)

    return kernel


def split(x):
    high = x.astype(bf16)
    rest = x - high.astype(f32)
    mid = rest.astype(bf16)
    return high, mid, (rest - mid.astype(f32)).astype(bf16)


def lanes(ref, start, count, rows=None):
    picked = [ref[start + n] if rows is None else ref[start + n, rows, :] for n in range(count)]
    return jnp.concatenate(picked, axis=1)


def own_gram_kernel(own, gram):
    blocks, half, _ = own.shape
    step = 4
    square = jnp.zeros((half, half), f32)
    skew = jnp.zeros((half, half), f32)
    for i in range(0, blocks, step):
        high, mid, low = split(lanes(own, i, step))
        stack = contract(jnp.concatenate([high, mid, low], axis=0), high, 1, 1)
        square += stack[0:half] + contract(mid, mid, 1, 1)
        skew += stack[half : 2 * half] + stack[2 * half :]
    gram[...] = square + (skew + skew.T)


def make_cross_gram_kernel(t):
    def kernel(tab, own, other, square, gram):
        blocks, half, _ = own.shape
        cut = half // 2
        step = 4
        gram[pl.ds(0, half), :] = square[...]

        def cross(left, rows, right):
            total = jnp.zeros((cut, half), f32)
            for i in range(0, blocks, step):
                high, mid, low = split(lanes(left, i, step, rows))
                r_high, r_mid, r_low = split(lanes(right, i, step))
                by_high = contract(jnp.concatenate([high, mid, low], axis=0), r_high, 1, 1)
                by_mid = contract(jnp.concatenate([high, mid], axis=0), r_mid, 1, 1)
                small = by_high[2 * cut :] + by_mid[cut:] + contract(high, r_low, 1, 1)
                total += by_high[:cut] + (by_high[cut : 2 * cut] + by_mid[:cut] + small)
            gram[pl.ds(half, cut), :] = total

        @pl.when(tab[t.col] == 0)
        def _():
            cross(other, pl.ds(0, cut), own)

        @pl.when(tab[t.col] == 1)
        def _():
            cross(own, pl.ds(cut, cut), other)

    return kernel


def pivot_rows(left, right, base):
    full = left.shape
    cols = [jnp.broadcast_to(left[:, base + k : base + k + 1], full) for k in range(8)]
    piv = [[jnp.broadcast_to(cols[k][i : i + 1, :], full) for k in range(i + 1)] for i in range(8)]
    rows = [
        [jnp.broadcast_to(side[i : i + 1, :], full) for side in (left, right)] for i in range(8)
    ]
    scale = []
    for k in range(0, 8, 2):
        a, b, c = piv[k][k], piv[k + 1][k], piv[k + 1][k + 1]
        det = a * c - b * b
        root, det_root = lax.rsqrt(a), lax.rsqrt(det)
        both = det_root * root
        scale += [root, det_root * (a * root)]
        piv[k + 1][k] = b * root
        for i in range(k + 2, 8):
            p, q = piv[i][k], piv[i][k + 1]
            piv[i][k] = p * root
            piv[i][k + 1] = (a * q - b * p) * both
        for i in range(k + 2, 8):
            for m in range(k + 2, i + 1):
                piv[i][m] = piv[i][m] - (
                    piv[i][k] * piv[m][k] + piv[i][k + 1] * piv[m][k + 1]
                )
        for side in range(2):
            first = rows[k][side] * root
            second = (rows[k + 1][side] - piv[k + 1][k] * first) * scale[k + 1]
            rows[k][side], rows[k + 1][side] = first, second
            for i in range(k + 2, 8):
                rows[i][side] = rows[i][side] - (piv[i][k] * first + piv[i][k + 1] * second)
    solved = [list(row) for row in rows]
    for k in range(7, -1, -1):
        for side in range(2):
            solved[k][side] = solved[k][side] * scale[k]
            for i in range(k):
                solved[i][side] = solved[i][side] - piv[k][i] * solved[k][side]
    return rows, solved


def inverse_factor(block):
    size = block.shape[0]
    tiles = size // 8
    panel = 4
    full = (8, size)
    lane = lax.broadcasted_iota(i32, full, 1)
    sub = lax.broadcasted_iota(i32, full, 0)
    sides = [
        [block[8 * t : 8 * t + 8, :], (lane == sub + 8 * t).astype(f32)] for t in range(tiles)
    ]
    for first in range(0, tiles, panel):
        last = first + panel
        for j in range(first, last):
            rows, solved = pivot_rows(*sides[j], 8 * j)
            for t in range(j + 1, last):
                old = sides[t][0]
                new = list(sides[t])
                for k in range(8):
                    col = jnp.broadcast_to(old[:, 8 * j + k : 8 * j + k + 1], full)
                    new = [new[n] - col * solved[k][n] for n in range(2)]
                sides[t] = new
            for n in range(2):
                done = rows[0][n]
                for i in range(1, 8):
                    done = jnp.where(sub == i, rows[i][n], done)
                sides[j][n] = done
        if last < tiles:
            left = jnp.concatenate([sides[t][0] for t in range(first, last)], axis=0)
            right = jnp.concatenate([sides[t][1] for t in range(first, last)], axis=0)
            high, mid, low = split(left)
            r_high, r_mid, r_low = split(jnp.concatenate([left, right], axis=1))
            change = contract(
                jnp.concatenate([high, high, mid, mid, high, low], axis=0),
                jnp.concatenate([r_high, r_mid, r_high, r_mid, r_low, r_high], axis=0),
                0,
                0,
            )
            for t in range(last, tiles):
                part = change[8 * t : 8 * t + 8, :]
                sides[t] = [sides[t][0] - part[:, :size], sides[t][1] - part[:, size:]]
    return jnp.concatenate([side[1] for side in sides], axis=0)


def invert(t, tab, own, other, gram, inverse, scale):
    half = own.shape[1]
    cut = half // 2
    my_col = tab[t.col]
    gram[my_col] = own[...] * scale
    gram[1 - my_col] = other[...] * scale
    low = inverse_factor(gram[0, pl.ds(0, half), :])
    lower = jnp.concatenate([gram[0, pl.ds(half, cut), :], gram[1, pl.ds(half, cut), :]], axis=0)
    across = contract(lower, low, 1, 1, HIGHEST)
    high = inverse_factor(
        gram[1, pl.ds(0, half), :] - contract(across, across, 1, 1, HIGHEST)
    )
    inverse[0, 0] = low
    inverse[0, 1] = jnp.zeros_like(low)
    inverse[1, 0] = -contract(high, contract(across, low, 1, 0, HIGHEST), 1, 0, HIGHEST)
    inverse[1, 1] = high


def normal_blocks(t, tab, inverse, mine, other, store):
    my_col = tab[t.col]
    half = mine.shape[1]
    factor = jnp.concatenate([inverse[my_col, my_col], inverse[my_col, 1 - my_col]], axis=1)
    high, mid, low = split(factor)
    three = jnp.concatenate([high, mid, low], axis=0)
    two = jnp.concatenate([high, mid], axis=0)

    @pl.loop(0, mine.shape[0])
    def _(i):
        y_high, y_mid, y_low = split(jnp.concatenate([mine[i], other[i]], axis=0))
        by_high = contract(three, y_high, 1, 0)
        by_mid = contract(two, y_mid, 1, 0)
        small = by_high[2 * half :] + by_mid[half:] + contract(high, y_low, 1, 0)
        store(i, by_high[:half] + (by_high[half : 2 * half] + by_mid[:half] + small))


def start_copies(pairs, sems):
    copies = [pltpu.make_async_copy(a, b, sems.at[n]) for n, (a, b) in enumerate(pairs)]
    for copy in copies:
        copy.start()
    return copies


def make_second_kernel(t, scale):
    def kernel(
        tab, own_g, other_g, mine_hbm, other_hbm, ppmi_hbm, normal, near, far, hot,
        gram, inverse, mine, other, ppmi, sems,
    ):
        copies = start_copies([(mine_hbm, mine), (other_hbm, other), (ppmi_hbm, ppmi)], sems)
        invert(t, tab, own_g, other_g, gram, inverse, scale)
        for copy in copies:
            copy.wait()

        def store(i, value):
            normal[i] = value.astype(bf16)

        normal_blocks(t, tab, inverse, mine, other, store)
        gather_hot(t, tab, normal, near, far)
        hot_products(t, tab, normal, ppmi, hot)

    return kernel


def make_final_kernel(t, scale):
    def kernel(tab, own_g, other_g, mine_hbm, other_hbm, out, gram, inverse, mine, other, sems):
        copies = start_copies([(mine_hbm, mine), (other_hbm, other)], sems)
        invert(t, tab, own_g, other_g, gram, inverse, scale)
        for copy in copies:
            copy.wait()

        def store(i, value):
            out[i] = value.T

        normal_blocks(t, tab, inverse, mine, other, store)

    return kernel


def body(counts, block_pairs, sketch):
    groups = lax.axis_size("row")
    me = lax.axis_index("row")
    my_col = lax.axis_index("col")
    nnz, rows, _ = counts.shape
    blocks, _, half = sketch.shape
    vocab = blocks * rows * groups
    t = Table(groups, nnz)
    hot = t.hot
    depth = -(-2 * nnz // 8) * 8

    def peer(x, k):
        return lax.ppermute(x, "row", [(r, r ^ k) for r in range(groups)])

    def swap(x):
        return lax.ppermute(x, "col", [(0, 1), (1, 0)])

    def exchange(x):
        return lax.all_to_all(x, "row", split_axis=0, concat_axis=0, tiled=True)

    def add_up(x):
        for bit in t.bits:
            x = x + peer(x, bit)
        return x

    def spread_hot(part, got):
        part = jnp.concatenate([part, got], axis=0)
        for bit in t.steps[-2:0:-1]:
            part = jnp.concatenate([part, peer(part, bit)], axis=0)
        return part, peer(part, t.steps[0])

    hot_order = [0]
    for bit in t.steps[::-1]:
        hot_order += [k ^ bit for k in hot_order]

    def halve(x, kept, bit):
        low = sum(1 for k in kept if k < bit)
        x = x.reshape(-1, 2, low, *x.shape[1:])
        return [x[:, n].reshape(-1, *x.shape[3:]) for n in range(2)]

    def scatter_hot(near, far, got, towards):
        kept = list(range(groups))
        for bit in t.steps:
            if bit != t.steps[0]:
                near, far = halve(part, kept, bit)
                got = peer(far, bit)
            towards = halve(towards, kept, bit)[0]
            kept = [k for k in kept if not k & bit]
            stay = (towards & bit) == 0
            part = jnp.where(stay[:, :, None, None], near, got)
        return part

    send_shape = shape((groups, 2, half, rows), bf16)
    one_shape = shape((groups, 1, half, rows), bf16)
    hot_shape = shape((1, hot, half, rows), bf16)
    side_shape = shape((groups // 2, hot, half, rows), bf16)
    ppmi_shape = shape((nnz, rows, rows), bf16)
    result_shape = shape((blocks, half, rows), f32)

    sums = call(sums_kernel, shape((groups, depth, rows), f32), [VMEM], vmem=8)(counts)
    sums_all = exchange(sums)
    tab, towards = t.build(block_pairs, me, my_col)
    turned, send_x, near, far = call(
        make_source_kernel(t),
        [shape((blocks, half, rows), bf16), one_shape, side_shape, side_shape],
        [SMEM, VMEM],
        vmem=8,
    )(tab, sketch)
    send_x, sums_all = lax.optimization_barrier((send_x, sums_all))
    got_x = exchange(send_x)
    x_step = peer(far, t.steps[0])

    row_ids = block_pairs[:, :, 0] * groups + jnp.arange(groups)[:, None]
    col_ids = block_pairs[:, :, 2] * groups + block_pairs[:, :, 1]
    no_id = jnp.full((groups, depth - 2 * nnz), -1, i32)
    ids = jnp.concatenate([row_ids, col_ids, no_id], axis=1)
    my_ids = lax.dynamic_index_in_dim(ids, me, 0, keepdims=False)
    match = (my_ids[:, None] == ids.reshape(-1)[None, :]).astype(bf16)

    ppmi, hot_t = call(
        make_ppmi_kernel(t),
        [ppmi_shape, hot_shape],
        [SMEM] + [VMEM] * 4,
        scratch=[pltpu.VMEM((depth, rows), f32)],
        vmem=12,
    )(tab, match, counts, turned, sums_all)

    def finish(source, got_x, near, far, x_step, hot_t):
        t_step = peer(hot_t, t.steps[-1])
        if x_step is None:
            x_step = peer(far, t.steps[0])
        send = call(
            make_main_kernel(t, got_x is None),
            one_shape if got_x is not None else send_shape,
            [SMEM, VMEM, VMEM],
            vmem=8,
        )(tab, source, ppmi)
        if got_x is None:
            send, x_step, t_step = lax.optimization_barrier((send, x_step, t_step))
        else:
            send, t_step = lax.optimization_barrier((send, t_step))
        got = [exchange(send)] + ([] if got_x is None else [got_x])
        hot_x = scatter_hot(near, far, x_step, towards)
        hot_a, hot_b = spread_hot(hot_t, t_step)
        result = call(
            make_result_kernel(t, hot_order),
            result_shape,
            [SMEM] + [VMEM] * (4 + len(got)),
            vmem=12,
        )(tab, ppmi, *got, hot_x, hot_a, hot_b)
        other = swap(result)
        square = call(own_gram_kernel, shape((half, half), f32), [VMEM], vmem=12)(result)
        gram = call(
            make_cross_gram_kernel(t),
            shape((half + half // 2, half), f32),
            [SMEM] + [VMEM] * 3,
            vmem=16,
        )(tab, result, other, square)
        gram = add_up(gram)
        return result, other, gram, swap(gram)

    gram_scratch = [
        pltpu.VMEM((2, half + half // 2, half), f32),
        pltpu.VMEM((2, 2, half, half), f32),
    ]
    result_scratch = [pltpu.VMEM((blocks, half, rows), f32)] * 2
    result, other, gram, other_gram = finish(
        turned, got_x, near, far, x_step, hot_t
    )
    normal, near, far, hot_t = call(
        make_second_kernel(t, 1.0 / vocab),
        [shape((blocks, half, rows), bf16), side_shape, side_shape, hot_shape],
        [SMEM] + [VMEM] * 2 + [ANY] * 3,
        scratch=gram_scratch
        + result_scratch
        + [pltpu.VMEM((nnz, rows, rows), bf16), pltpu.SemaphoreType.DMA((3,))],
    )(tab, gram, other_gram, result, other, ppmi)
    result, other, gram, other_gram = finish(
        normal, None, near, far, None, hot_t
    )
    return call(
        make_final_kernel(t, 1.0 / vocab),
        shape((blocks, rows, half), f32),
        [SMEM] + [VMEM] * 2 + [ANY] * 2,
        scratch=gram_scratch + result_scratch + [pltpu.SemaphoreType.DMA((2,))],
    )(tab, gram, other_gram, result, other)


def solution(mesh):
    placed = (
        P(("decade", "row"), None, None),
        P("decade", None, None),
        P(None, ("decade", "row"), "col"),
    )
    return jax.shard_map(
        body,
        mesh=mesh,
        in_specs=placed,
        out_specs=P(None, ("decade", "row"), "col"),
        check_vma=False,
    )
```

```python
import jax
import jax.numpy as jnp
from jax import lax
from jax.experimental import pallas as pl
from jax.experimental.pallas import tpu as pltpu
from jax.sharding import PartitionSpec as P

MIB = 1 << 20
HIGHEST = lax.Precision.HIGHEST
VMEM = pl.BlockSpec(memory_space=pltpu.VMEM)
SMEM = pl.BlockSpec(memory_space=pltpu.SMEM)
ANY = pl.BlockSpec(memory_space=pl.ANY)
shape = jax.ShapeDtypeStruct
f32, bf16, i32 = jnp.float32, jnp.bfloat16, jnp.int32


def contract(a, b, a_dim, b_dim, precision=None):
    return lax.dot_general(
        a,
        b,
        (((a_dim,), (b_dim,)), ((), ())),
        precision=precision,
        preferred_element_type=f32,
    )


def call(kernel, out_shape, in_specs, out_specs=None, scratch=(), flops=0, vmem=20):
    if out_specs is None:
        out_specs = jax.tree.map(lambda _: VMEM, out_shape)
    return pl.pallas_call(
        kernel,
        out_shape=out_shape,
        in_specs=in_specs,
        out_specs=out_specs,
        scratch_shapes=list(scratch),
        compiler_params=pltpu.CompilerParams(vmem_limit_bytes=vmem * MIB),
        cost_estimate=pl.CostEstimate(flops=flops, bytes_accessed=4 * MIB, transcendentals=0),
    )


class Table:
    def __init__(self, groups, nnz):
        self.groups, self.nnz, self.hot = groups, nnz, nnz - groups
        bits = [1 << b for b in range(groups.bit_length() - 1)]
        self.bits = bits
        self.steps = bits[1:-1] + bits[:1] + bits[-1:]
        self.main_j = 0
        self.hot_j = self.main_j + groups
        self.row_i = self.hot_j + groups * self.hot
        self.dest = self.row_i + nnz
        self.col = self.dest + nnz

    def build(self, block_pairs, me, my_col):
        groups = self.groups
        mine = lax.dynamic_index_in_dim(block_pairs, me, 0, keepdims=False)
        main = block_pairs[:, :groups]
        main_j = jnp.sum(jnp.where(main[:, :, 1] == me, main[:, :, 2], 0), axis=1)
        late = jnp.take(block_pairs[:, groups:], me ^ jnp.arange(groups), axis=0)
        hot_j = jnp.where(late[:, :, 1] == me, late[:, :, 2], -1).reshape(-1)
        parts = [main_j, hot_j, mine[:, 0], mine[:, 1], my_col[None]]
        return jnp.concatenate([p.astype(i32) for p in parts]), late[:, :, 1] ^ me


def sums_kernel(counts_ref, sums_ref):
    nnz, rows, cols = counts_ref.shape
    ones = jnp.ones((8, cols), bf16)
    sums_ref[0] = jnp.zeros(sums_ref.shape[1:], f32)
    for s in range(nnz):
        block = counts_ref[s].astype(bf16)
        sums_ref[0, pl.ds(s, 1), :] = contract(ones, block, 1, 1)[0:1, :]
        sums_ref[0, pl.ds(nnz + s, 1), :] = contract(ones, block, 1, 0)[0:1, :]
    for r in range(1, sums_ref.shape[0]):
        sums_ref[r] = sums_ref[0]


def gather_hot(t, tab, blocks, near, far):
    bit = t.steps[0]
    for k in range(t.groups):
        place = (k // (2 * bit)) * bit + k % bit
        for m in range(t.hot):
            j = tab[t.hot_j + k * t.hot + m]

            @pl.when(j >= 0)
            def _():
                (far if k & bit else near)[place, m] = blocks[j]


def product(t, tab, blocks, ppmi, s):
    return contract(blocks[tab[t.row_i + s]], ppmi[s], 1, 0).astype(bf16)


def hot_products(t, tab, blocks, ppmi, hot):
    for m in range(t.hot):
        hot[0, m] = product(t, tab, blocks, ppmi, t.groups + m)


def gather_main(t, tab, blocks, send):
    for r in range(t.groups):
        send[r] = blocks[tab[t.main_j + r]]


def make_main_kernel(t):
    def kernel(tab, blocks, ppmi, send):
        for s in range(t.groups):
            send[tab[t.dest + s]] = product(t, tab, blocks, ppmi, s)

    return kernel


def make_source_kernel(t):
    def kernel(tab, sketch_ref, turned, send, near, far):
        @pl.loop(0, sketch_ref.shape[0])
        def _(i):
            turned[i] = sketch_ref[i].T

        gather_main(t, tab, turned, send)
        gather_hot(t, tab, turned, near, far)

    return kernel


def make_ppmi_kernel(t):
    def kernel(tab, match_ref, counts_ref, turned, sums_ref, ppmi_ref, hot, cols_log):
        sums = jnp.concatenate([sums_ref[r] for r in range(t.groups)], axis=0)
        high = jnp.floor(sums * (1.0 / 256.0))
        low = sums - high * 256.0
        match = match_ref[...]
        margins = 256.0 * contract(match, high.astype(bf16), 1, 0) + contract(
            match, low.astype(bf16), 1, 0
        )
        log_total = jnp.log(jnp.sum(sums))
        log_margin = jnp.log(margins)
        cols_log[...] = log_margin
        fill = 128 - log_margin.shape[0] % 128
        row_log = jnp.concatenate(
            [log_margin, jnp.zeros((fill, log_margin.shape[1]), f32)], axis=0
        ).T
        for s in range(t.nnz):
            counts = counts_ref[s]
            scores = (
                jnp.log(counts.astype(f32))
                + log_total
                - row_log[:, s : s + 1]
                - cols_log[pl.ds(t.nnz + s, 1), :]
            )
            ppmi_ref[s] = jnp.where(counts > 0, jnp.maximum(scores, 0.0), 0.0).astype(bf16)
        hot_products(t, tab, turned, ppmi_ref, hot)

    return kernel


def make_result_kernel(t, order):
    def kernel(tab, ppmi_ref, got_t, got_x, hot_x, hot_a, hot_b, result):
        result[...] = jnp.zeros_like(result)
        for s in range(t.nnz):
            block = got_x[tab[t.dest + s]] if s < t.groups else hot_x[0, s - t.groups]
            forward = contract(block, ppmi_ref[s], 1, 1).astype(bf16)
            result[tab[t.row_i + s]] += forward.astype(f32)
        for r in range(t.groups):
            result[tab[t.main_j + r]] += got_t[r].astype(f32)
        for n, k in enumerate(order):
            ref, place = (hot_a, n) if n < t.groups // 2 else (hot_b, n - t.groups // 2)
            for m in range(t.hot):
                j = tab[t.hot_j + k * t.hot + m]

                @pl.when(j >= 0)
                def _():
                    result[j] += ref[place, m].astype(f32)

    return kernel


def split(x):
    high = x.astype(bf16)
    rest = x - high.astype(f32)
    mid = rest.astype(bf16)
    return high, mid, (rest - mid.astype(f32)).astype(bf16)


def lanes(ref, start, count, rows=None):
    picked = [ref[start + n] if rows is None else ref[start + n, rows, :] for n in range(count)]
    return jnp.concatenate(picked, axis=1)


def own_gram_kernel(own, gram):
    blocks, half, _ = own.shape
    step = 4
    square = jnp.zeros((half, half), f32)
    skew = jnp.zeros((half, half), f32)
    for i in range(0, blocks, step):
        high, mid, low = split(lanes(own, i, step))
        stack = contract(jnp.concatenate([high, mid, low], axis=0), high, 1, 1)
        square += stack[0:half] + contract(mid, mid, 1, 1)
        skew += stack[half : 2 * half] + stack[2 * half :]
    gram[...] = square + (skew + skew.T)


def make_cross_gram_kernel(t):
    def kernel(tab, own, other, square, gram):
        blocks, half, _ = own.shape
        cut = half // 2
        step = 4
        gram[pl.ds(0, half), :] = square[...]

        def cross(left, rows, right):
            total = jnp.zeros((cut, half), f32)
            for i in range(0, blocks, step):
                high, mid, low = split(lanes(left, i, step, rows))
                r_high, r_mid, r_low = split(lanes(right, i, step))
                by_high = contract(jnp.concatenate([high, mid, low], axis=0), r_high, 1, 1)
                by_mid = contract(jnp.concatenate([high, mid], axis=0), r_mid, 1, 1)
                small = by_high[2 * cut :] + by_mid[cut:] + contract(high, r_low, 1, 1)
                total += by_high[:cut] + (by_high[cut : 2 * cut] + by_mid[:cut] + small)
            gram[pl.ds(half, cut), :] = total

        @pl.when(tab[t.col] == 0)
        def _():
            cross(other, pl.ds(0, cut), own)

        @pl.when(tab[t.col] == 1)
        def _():
            cross(own, pl.ds(cut, cut), other)

    return kernel


def pivot_rows(left, right, base):
    full = left.shape
    cols = [jnp.broadcast_to(left[:, base + k : base + k + 1], full) for k in range(8)]
    piv = [[jnp.broadcast_to(cols[k][i : i + 1, :], full) for k in range(i + 1)] for i in range(8)]
    rows = [
        [jnp.broadcast_to(side[i : i + 1, :], full) for side in (left, right)] for i in range(8)
    ]
    zero = jnp.zeros(full, f32)
    inv = [[None] * 8 for _ in range(8)]
    done = []
    solved = [[zero, zero] for _ in range(8)]
    for k in range(0, 8, 2):
        a, b, c = piv[k][k], piv[k + 1][k], piv[k + 1][k + 1]
        det = a * c - b * b
        root, det_root = lax.rsqrt(a), lax.rsqrt(det)
        both = det_root * root
        scale = det_root * (a * root)
        across = b * root
        for i in range(k + 2, 8):
            p, q = piv[i][k], piv[i][k + 1]
            piv[i][k] = p * root
            piv[i][k + 1] = (a * q - b * p) * both
        for i in range(k + 2, 8):
            for m in range(k + 2, i + 1):
                piv[i][m] = piv[i][m] - (
                    piv[i][k] * piv[m][k] + piv[i][k + 1] * piv[m][k + 1]
                )
        pair = []
        for side in range(2):
            first = rows[k][side] * root
            second = (rows[k + 1][side] - across * first) * scale
            pair.append((first, second))
            for i in range(k + 2, 8):
                rows[i][side] = rows[i][side] - (piv[i][k] * first + piv[i][k + 1] * second)
        done += [[pair[0][0], pair[1][0]], [pair[0][1], pair[1][1]]]
        for i in range(k):
            inv[k][i] = inv[k][i] * root
            inv[k + 1][i] = (inv[k + 1][i] - across * inv[k][i]) * scale
        inv[k][k] = root
        inv[k + 1][k] = -across * root * scale
        inv[k + 1][k + 1] = scale
        for i in range(k + 2, 8):
            for m in range(k + 2):
                part = piv[i][k + 1] * inv[k + 1][m]
                if m <= k:
                    part = part + piv[i][k] * inv[k][m]
                inv[i][m] = -part if inv[i][m] is None else inv[i][m] - part
        for n in (k, k + 1):
            for i in range(n + 1):
                for side in range(2):
                    solved[i][side] = solved[i][side] + inv[n][i] * done[n][side]
    return done, solved


def inverse_factor(block):
    size = block.shape[0]
    tiles = size // 8
    panel = 4
    full = (8, size)
    lane = lax.broadcasted_iota(i32, full, 1)
    sub = lax.broadcasted_iota(i32, full, 0)
    sides = [
        [block[8 * t : 8 * t + 8, :], (lane == sub + 8 * t).astype(f32)] for t in range(tiles)
    ]
    for first in range(0, tiles, panel):
        last = first + panel
        for j in range(first, last):
            rows, solved = pivot_rows(*sides[j], 8 * j)
            for t in range(j + 1, last):
                old = sides[t][0]
                new = list(sides[t])
                for k in range(8):
                    col = jnp.broadcast_to(old[:, 8 * j + k : 8 * j + k + 1], full)
                    new = [new[n] - col * solved[k][n] for n in range(2)]
                sides[t] = new
            for n in range(2):
                done = rows[0][n]
                for i in range(1, 8):
                    done = jnp.where(sub == i, rows[i][n], done)
                sides[j][n] = done
        if last < tiles:
            left = jnp.concatenate([sides[t][0] for t in range(first, last)], axis=0)
            right = jnp.concatenate([sides[t][1] for t in range(first, last)], axis=0)
            high, mid, low = split(left)
            r_high, r_mid, r_low = split(jnp.concatenate([left, right], axis=1))
            change = contract(
                jnp.concatenate([high, high, mid, mid, high, low], axis=0),
                jnp.concatenate([r_high, r_mid, r_high, r_mid, r_low, r_high], axis=0),
                0,
                0,
            )
            for t in range(last, tiles):
                part = change[8 * t : 8 * t + 8, :]
                sides[t] = [sides[t][0] - part[:, :size], sides[t][1] - part[:, size:]]
    return jnp.concatenate([side[1] for side in sides], axis=0)


def invert(t, tab, own, other, gram, inverse, scale):
    half = own.shape[1]
    cut = half // 2
    my_col = tab[t.col]
    gram[my_col] = own[...] * scale
    gram[1 - my_col] = other[...] * scale
    low = inverse_factor(gram[0, pl.ds(0, half), :])
    lower = jnp.concatenate([gram[0, pl.ds(half, cut), :], gram[1, pl.ds(half, cut), :]], axis=0)
    across = contract(lower, low, 1, 1, HIGHEST)
    high = inverse_factor(
        gram[1, pl.ds(0, half), :] - contract(across, across, 1, 1, HIGHEST)
    )
    inverse[0, 0] = low
    inverse[0, 1] = jnp.zeros_like(low)
    inverse[1, 0] = -contract(high, contract(across, low, 1, 0, HIGHEST), 1, 0, HIGHEST)
    inverse[1, 1] = high


def normal_blocks(t, tab, inverse, mine, other, store):
    my_col = tab[t.col]
    half = mine.shape[1]
    factor = jnp.concatenate([inverse[my_col, my_col], inverse[my_col, 1 - my_col]], axis=1)
    high, mid, _ = split(factor)
    two = jnp.concatenate([high, mid], axis=0)

    @pl.loop(0, mine.shape[0])
    def _(i):
        y_high, y_mid, _ = split(jnp.concatenate([mine[i], other[i]], axis=0))
        by_high = contract(two, y_high, 1, 0)
        store(i, by_high[:half] + (by_high[half:] + contract(high, y_mid, 1, 0)))


def start_copies(pairs, sems):
    copies = [pltpu.make_async_copy(a, b, sems.at[n]) for n, (a, b) in enumerate(pairs)]
    for copy in copies:
        copy.start()
    return copies


def make_second_kernel(t, scale):
    def kernel(
        tab, own_g, other_g, mine_hbm, other_hbm, ppmi_hbm, normal, send, near, far, hot,
        gram, inverse, mine, other, ppmi, sems,
    ):
        copies = start_copies([(mine_hbm, mine), (other_hbm, other), (ppmi_hbm, ppmi)], sems)
        invert(t, tab, own_g, other_g, gram, inverse, scale)
        for copy in copies:
            copy.wait()

        def store(i, value):
            normal[i] = value.astype(bf16)

        normal_blocks(t, tab, inverse, mine, other, store)
        gather_main(t, tab, normal, send)
        gather_hot(t, tab, normal, near, far)
        hot_products(t, tab, normal, ppmi, hot)

    return kernel


def make_final_kernel(t, scale):
    def kernel(
        tab, own_g, other_g, mine_hbm, other_hbm, out, gram, inverse, mine, other, held, sems
    ):
        copies = start_copies([(mine_hbm, mine), (other_hbm, other)], sems)
        invert(t, tab, own_g, other_g, gram, inverse, scale)
        for copy in copies:
            copy.wait()

        def leave(i):
            return pltpu.make_async_copy(held.at[i], out.at[i], sems.at[2])

        def store(i, value):
            held[i] = value.T
            leave(i).start()

        normal_blocks(t, tab, inverse, mine, other, store)

        @pl.loop(0, held.shape[0])
        def _(i):
            leave(i).wait()

    return kernel


def body(counts, block_pairs, sketch):
    groups = lax.axis_size("row")
    me = lax.axis_index("row")
    my_col = lax.axis_index("col")
    nnz, rows, _ = counts.shape
    blocks, _, half = sketch.shape
    vocab = blocks * rows * groups
    t = Table(groups, nnz)
    hot = t.hot
    depth = -(-2 * nnz // 8) * 8

    def peer(x, k):
        return lax.ppermute(x, "row", [(r, r ^ k) for r in range(groups)])

    def swap(x):
        return lax.ppermute(x, "col", [(0, 1), (1, 0)])

    def exchange(x):
        return lax.all_to_all(x, "row", split_axis=0, concat_axis=0, tiled=True)

    def send_blocks(send, far):
        return exchange(send), peer(far, t.steps[0])

    def add_up(x):
        for bit in t.bits:
            x = x + peer(x, bit)
        return x

    def spread_hot(part, got):
        part = jnp.concatenate([part, got], axis=0)
        for bit in t.steps[-2:0:-1]:
            part = jnp.concatenate([part, peer(part, bit)], axis=0)
        return part, peer(part, t.steps[0])

    hot_order = [0]
    for bit in t.steps[::-1]:
        hot_order += [k ^ bit for k in hot_order]

    def halve(x, kept, bit):
        low = sum(1 for k in kept if k < bit)
        x = x.reshape(-1, 2, low, *x.shape[1:])
        return [x[:, n].reshape(-1, *x.shape[3:]) for n in range(2)]

    def scatter_hot(near, far, got, towards):
        kept = list(range(groups))
        for bit in t.steps:
            if bit != t.steps[0]:
                near, far = halve(part, kept, bit)
                got = peer(far, bit)
            towards = halve(towards, kept, bit)[0]
            kept = [k for k in kept if not k & bit]
            stay = (towards & bit) == 0
            part = jnp.where(stay[:, :, None, None], near, got)
        return part

    send_shape = shape((groups, half, rows), bf16)
    hot_shape = shape((1, hot, half, rows), bf16)
    side_shape = shape((groups // 2, hot, half, rows), bf16)
    ppmi_shape = shape((nnz, rows, rows), bf16)
    result_shape = shape((blocks, half, rows), f32)

    sums = call(sums_kernel, shape((groups, depth, rows), f32), [VMEM], vmem=8)(counts)
    sums, sketch = lax.optimization_barrier((sums, sketch))
    sums_all = exchange(sums)
    tab, towards = t.build(block_pairs, me, my_col)
    turned, send_x, near, far = call(
        make_source_kernel(t),
        [shape((blocks, half, rows), bf16), send_shape, side_shape, side_shape],
        [SMEM, VMEM],
        vmem=8,
    )(tab, sketch)

    row_ids = block_pairs[:, :, 0] * groups + jnp.arange(groups)[:, None]
    col_ids = block_pairs[:, :, 2] * groups + block_pairs[:, :, 1]
    no_id = jnp.full((groups, depth - 2 * nnz), -1, i32)
    ids = jnp.concatenate([row_ids, col_ids, no_id], axis=1)
    my_ids = lax.dynamic_index_in_dim(ids, me, 0, keepdims=False)
    match = (my_ids[:, None] == ids.reshape(-1)[None, :]).astype(bf16)

    got_x, x_step = send_blocks(send_x, far)
    ppmi, hot_t = call(
        make_ppmi_kernel(t),
        [ppmi_shape, hot_shape],
        [SMEM] + [VMEM] * 4,
        scratch=[pltpu.VMEM((depth, rows), f32)],
        vmem=12,
    )(tab, match, counts, turned, sums_all)

    def finish(source, got_x, near, far, x_step, hot_t):
        t_step = peer(hot_t, t.steps[-1])
        send = call(make_main_kernel(t), send_shape, [SMEM, VMEM, VMEM], vmem=8)(
            tab, source, ppmi
        )
        send, t_step = lax.optimization_barrier((send, t_step))
        got_t = exchange(send)
        hot_x = scatter_hot(near, far, x_step, towards)
        hot_a, hot_b = spread_hot(hot_t, t_step)
        result = call(
            make_result_kernel(t, hot_order),
            result_shape,
            [SMEM] + [VMEM] * 6,
            vmem=12,
        )(tab, ppmi, got_t, got_x, hot_x, hot_a, hot_b)
        other = swap(result)
        square = call(own_gram_kernel, shape((half, half), f32), [VMEM], vmem=12)(result)
        gram = call(
            make_cross_gram_kernel(t),
            shape((half + half // 2, half), f32),
            [SMEM] + [VMEM] * 3,
            vmem=16,
        )(tab, result, other, square)
        gram = add_up(gram)
        return result, other, gram, swap(gram)

    gram_scratch = [
        pltpu.VMEM((2, half + half // 2, half), f32),
        pltpu.VMEM((2, 2, half, half), f32),
    ]
    result_scratch = [pltpu.VMEM((blocks, half, rows), f32)] * 2
    result, other, gram, other_gram = finish(
        turned, got_x, near, far, x_step, hot_t
    )
    normal, send_x, near, far, hot_t = call(
        make_second_kernel(t, 1.0 / vocab),
        [shape((blocks, half, rows), bf16), send_shape, side_shape, side_shape, hot_shape],
        [SMEM] + [VMEM] * 2 + [ANY] * 3,
        scratch=gram_scratch
        + result_scratch
        + [pltpu.VMEM((nnz, rows, rows), bf16), pltpu.SemaphoreType.DMA((3,))],
    )(tab, gram, other_gram, result, other, ppmi)
    got_x, x_step = send_blocks(send_x, far)
    result, other, gram, other_gram = finish(
        normal, got_x, near, far, x_step, hot_t
    )
    return call(
        make_final_kernel(t, 1.0 / vocab),
        shape((blocks, rows, half), f32),
        [SMEM] + [VMEM] * 2 + [ANY] * 2,
        ANY,
        scratch=gram_scratch
        + result_scratch
        + [pltpu.VMEM((blocks, rows, half), f32), pltpu.SemaphoreType.DMA((3,))],
    )(tab, gram, other_gram, result, other)


def solution(mesh):
    placed = (
        P(("decade", "row"), None, None),
        P("decade", None, None),
        P(None, ("decade", "row"), "col"),
    )
    return jax.shard_map(
        body,
        mesh=mesh,
        in_specs=placed,
        out_specs=P(None, ("decade", "row"), "col"),
        check_vma=False,
    )
```

```python
import jax
import jax.numpy as jnp
from jax import lax
from jax.experimental import pallas as pl
from jax.experimental.pallas import tpu as pltpu
from jax.sharding import PartitionSpec as P

MIB = 1 << 20
HIGHEST = lax.Precision.HIGHEST
VMEM = pl.BlockSpec(memory_space=pltpu.VMEM)
SMEM = pl.BlockSpec(memory_space=pltpu.SMEM)
ANY = pl.BlockSpec(memory_space=pl.ANY)
shape = jax.ShapeDtypeStruct
f32, bf16, i32 = jnp.float32, jnp.bfloat16, jnp.int32


def contract(a, b, a_dim, b_dim, precision=None):
    return lax.dot_general(
        a,
        b,
        (((a_dim,), (b_dim,)), ((), ())),
        precision=precision,
        preferred_element_type=f32,
    )


def call(kernel, out_shape, in_specs, out_specs=None, scratch=(), flops=0, vmem=20):
    if out_specs is None:
        out_specs = jax.tree.map(lambda _: VMEM, out_shape)
    return pl.pallas_call(
        kernel,
        out_shape=out_shape,
        in_specs=in_specs,
        out_specs=out_specs,
        scratch_shapes=list(scratch),
        compiler_params=pltpu.CompilerParams(vmem_limit_bytes=vmem * MIB),
        cost_estimate=pl.CostEstimate(flops=flops, bytes_accessed=4 * MIB, transcendentals=0),
    )


class Table:
    def __init__(self, groups, nnz):
        self.groups, self.nnz, self.hot = groups, nnz, nnz - groups
        bits = [1 << b for b in range(groups.bit_length() - 1)]
        self.bits = bits
        self.steps = bits[1:-1] + bits[:1] + bits[-1:]
        self.main_j = 0
        self.hot_j = self.main_j + groups
        self.row_i = self.hot_j + groups * self.hot
        self.dest = self.row_i + nnz
        self.col = self.dest + nnz

    def build(self, block_pairs, me, my_col):
        groups = self.groups
        mine = lax.dynamic_index_in_dim(block_pairs, me, 0, keepdims=False)
        main = block_pairs[:, :groups]
        main_j = jnp.sum(jnp.where(main[:, :, 1] == me, main[:, :, 2], 0), axis=1)
        late = jnp.take(block_pairs[:, groups:], me ^ jnp.arange(groups), axis=0)
        hot_j = jnp.where(late[:, :, 1] == me, late[:, :, 2], -1).reshape(-1)
        parts = [main_j, hot_j, mine[:, 0], mine[:, 1], my_col[None]]
        return jnp.concatenate([p.astype(i32) for p in parts]), late[:, :, 1] ^ me


def sums_kernel(counts_ref, sums_ref):
    nnz, rows, cols = counts_ref.shape
    ones = jnp.ones((8, cols), bf16)
    sums_ref[...] = jnp.zeros(sums_ref.shape, f32)
    for s in range(nnz):
        block = counts_ref[s].astype(bf16)
        sums_ref[0, pl.ds(s, 1), :] = contract(ones, block, 1, 1)[0:1, :]
        sums_ref[0, pl.ds(nnz + s, 1), :] = contract(ones, block, 1, 0)[0:1, :]


def gather_hot(t, tab, blocks, near, far):
    bit = t.steps[0]
    for k in range(t.groups):
        place = (k // (2 * bit)) * bit + k % bit
        for m in range(t.hot):
            j = tab[t.hot_j + k * t.hot + m]

            @pl.when(j >= 0)
            def _():
                (far if k & bit else near)[place, m] = blocks[j]


def product(t, tab, blocks, ppmi, s):
    return contract(blocks[tab[t.row_i + s]], ppmi[s], 1, 0).astype(bf16)


def hot_products(t, tab, blocks, ppmi, hot):
    for m in range(t.hot):
        hot[0, m] = product(t, tab, blocks, ppmi, t.groups + m)


def gather_main(t, tab, blocks, send, slot):
    for r in range(t.groups):
        send[r, slot] = blocks[tab[t.main_j + r]]


def make_main_kernel(t, with_blocks):
    def kernel(tab, blocks, ppmi, send):
        if with_blocks:
            gather_main(t, tab, blocks, send, 1)
        for s in range(t.groups):
            send[tab[t.dest + s], 0] = product(t, tab, blocks, ppmi, s)

    return kernel


def make_source_kernel(t):
    def kernel(tab, sketch_ref, turned, send, near, far):
        @pl.loop(0, sketch_ref.shape[0])
        def _(i):
            turned[i] = sketch_ref[i].T

        gather_main(t, tab, turned, send, 0)
        gather_hot(t, tab, turned, near, far)

    return kernel


def make_ppmi_kernel(t):
    def kernel(tab, match_ref, counts_ref, turned, sums_a, sums_b, ppmi_ref, hot, cols_log):
        sums = jnp.concatenate(
            [ref[r] for ref in (sums_a, sums_b) for r in range(t.groups // 2)], axis=0
        )
        high = jnp.floor(sums * (1.0 / 256.0))
        low = sums - high * 256.0
        match = match_ref[...]
        margins = 256.0 * contract(match, high.astype(bf16), 1, 0) + contract(
            match, low.astype(bf16), 1, 0
        )
        log_total = jnp.log(jnp.sum(sums))
        log_margin = jnp.log(margins)
        cols_log[...] = log_margin
        fill = 128 - log_margin.shape[0] % 128
        row_log = jnp.concatenate(
            [log_margin, jnp.zeros((fill, log_margin.shape[1]), f32)], axis=0
        ).T
        for s in range(t.nnz):
            counts = counts_ref[s]
            scores = (
                jnp.log(counts.astype(f32))
                + log_total
                - row_log[:, s : s + 1]
                - cols_log[pl.ds(t.nnz + s, 1), :]
            )
            ppmi_ref[s] = jnp.where(counts > 0, jnp.maximum(scores, 0.0), 0.0).astype(bf16)
        hot_products(t, tab, turned, ppmi_ref, hot)

    return kernel


def make_result_kernel(t, order):
    def kernel(tab, ppmi_ref, *refs):
        got_t, got_x = refs[0], refs[-5]
        hot_x, hot_a, hot_b, result = refs[-4:]
        slot = got_x.shape[1] - 1
        result[...] = jnp.zeros_like(result)
        for s in range(t.nnz):
            block = got_x[tab[t.dest + s], slot] if s < t.groups else hot_x[0, s - t.groups]
            forward = contract(block, ppmi_ref[s], 1, 1).astype(bf16)
            result[tab[t.row_i + s]] += forward.astype(f32)
        for r in range(t.groups):
            result[tab[t.main_j + r]] += got_t[r, 0].astype(f32)
        for n, k in enumerate(order):
            ref, place = (hot_a, n) if n < t.groups // 2 else (hot_b, n - t.groups // 2)
            for m in range(t.hot):
                j = tab[t.hot_j + k * t.hot + m]

                @pl.when(j >= 0)
                def _():
                    result[j] += ref[place, m].astype(f32)

    return kernel


def split(x):
    high = x.astype(bf16)
    rest = x - high.astype(f32)
    mid = rest.astype(bf16)
    return high, mid, (rest - mid.astype(f32)).astype(bf16)


def lanes(ref, start, count, rows=None):
    picked = [ref[start + n] if rows is None else ref[start + n, rows, :] for n in range(count)]
    return jnp.concatenate(picked, axis=1)


def own_gram_kernel(own, gram):
    blocks, half, _ = own.shape
    step = 4
    square = jnp.zeros((half, half), f32)
    skew = jnp.zeros((half, half), f32)
    for i in range(0, blocks, step):
        high, mid, low = split(lanes(own, i, step))
        stack = contract(jnp.concatenate([high, mid, low], axis=0), high, 1, 1)
        square += stack[0:half] + contract(mid, mid, 1, 1)
        skew += stack[half : 2 * half] + stack[2 * half :]
    gram[...] = square + (skew + skew.T)


def make_cross_gram_kernel(t):
    def kernel(tab, own, other, square, gram):
        blocks, half, _ = own.shape
        cut = half // 2
        step = 4
        full = square[...]
        row = lax.broadcasted_iota(i32, (half, half), 0)
        lane = lax.broadcasted_iota(i32, (half, half), 1)
        diagonal = jnp.sum(jnp.where(row == lane, full, 0.0), axis=0, keepdims=True)
        gram[pl.ds(0, cut), :] = jnp.where(
            lane[:cut] >= row[:cut], full[:cut], pltpu.roll(full[cut:], cut, 1)
        )
        gram[pl.ds(cut, 8), :] = jnp.broadcast_to(diagonal, (8, half))

        def cross(left, rows, right):
            total = jnp.zeros((cut, half), f32)
            for i in range(0, blocks, step):
                high, mid, low = split(lanes(left, i, step, rows))
                r_high, r_mid, r_low = split(lanes(right, i, step))
                by_high = contract(jnp.concatenate([high, mid, low], axis=0), r_high, 1, 1)
                by_mid = contract(jnp.concatenate([high, mid], axis=0), r_mid, 1, 1)
                small = by_high[2 * cut :] + by_mid[cut:] + contract(high, r_low, 1, 1)
                total += by_high[:cut] + (by_high[cut : 2 * cut] + by_mid[:cut] + small)
            gram[pl.ds(cut + 8, cut), :] = total

        @pl.when(tab[t.col] == 0)
        def _():
            cross(other, pl.ds(0, cut), own)

        @pl.when(tab[t.col] == 1)
        def _():
            cross(own, pl.ds(cut, cut), other)

    return kernel


def pivot_rows(left, right, base):
    full = left.shape
    cols = [jnp.broadcast_to(left[:, base + k : base + k + 1], full) for k in range(8)]
    piv = [[jnp.broadcast_to(cols[k][i : i + 1, :], full) for k in range(i + 1)] for i in range(8)]
    rows = [
        [jnp.broadcast_to(side[i : i + 1, :], full) for side in (left, right)] for i in range(8)
    ]
    zero = jnp.zeros(full, f32)
    inv = [[None] * 8 for _ in range(8)]
    done = []
    solved = [[zero, zero] for _ in range(8)]
    for k in range(0, 8, 2):
        a, b, c = piv[k][k], piv[k + 1][k], piv[k + 1][k + 1]
        det = a * c - b * b
        root, det_root = lax.rsqrt(a), lax.rsqrt(det)
        both = det_root * root
        scale = det_root * (a * root)
        across = b * root
        for i in range(k + 2, 8):
            p, q = piv[i][k], piv[i][k + 1]
            piv[i][k] = p * root
            piv[i][k + 1] = (a * q - b * p) * both
        for i in range(k + 2, 8):
            for m in range(k + 2, i + 1):
                piv[i][m] = piv[i][m] - (
                    piv[i][k] * piv[m][k] + piv[i][k + 1] * piv[m][k + 1]
                )
        pair = []
        for side in range(2):
            first = rows[k][side] * root
            second = (rows[k + 1][side] - across * first) * scale
            pair.append((first, second))
            for i in range(k + 2, 8):
                rows[i][side] = rows[i][side] - (piv[i][k] * first + piv[i][k + 1] * second)
        done += [[pair[0][0], pair[1][0]], [pair[0][1], pair[1][1]]]
        for i in range(k):
            inv[k][i] = inv[k][i] * root
            inv[k + 1][i] = (inv[k + 1][i] - across * inv[k][i]) * scale
        inv[k][k] = root
        inv[k + 1][k] = -across * root * scale
        inv[k + 1][k + 1] = scale
        for i in range(k + 2, 8):
            for m in range(k + 2):
                part = piv[i][k + 1] * inv[k + 1][m]
                if m <= k:
                    part = part + piv[i][k] * inv[k][m]
                inv[i][m] = -part if inv[i][m] is None else inv[i][m] - part
        for n in (k, k + 1):
            for i in range(n + 1):
                for side in range(2):
                    solved[i][side] = solved[i][side] + inv[n][i] * done[n][side]
    return done, solved


def inverse_factor(block):
    size = block.shape[0]
    tiles = size // 8
    panel = 4
    full = (8, size)
    lane = lax.broadcasted_iota(i32, full, 1)
    sub = lax.broadcasted_iota(i32, full, 0)
    sides = [
        [block[8 * t : 8 * t + 8, :], (lane == sub + 8 * t).astype(f32)] for t in range(tiles)
    ]
    for first in range(0, tiles, panel):
        last = first + panel
        for j in range(first, last):
            rows, solved = pivot_rows(*sides[j], 8 * j)
            for t in range(j + 1, last):
                old = sides[t][0]
                new = list(sides[t])
                for k in range(8):
                    col = jnp.broadcast_to(old[:, 8 * j + k : 8 * j + k + 1], full)
                    new = [new[n] - col * solved[k][n] for n in range(2)]
                sides[t] = new
            for n in range(2):
                done = rows[0][n]
                for i in range(1, 8):
                    done = jnp.where(sub == i, rows[i][n], done)
                sides[j][n] = done
        if last < tiles:
            left = jnp.concatenate([sides[t][0] for t in range(first, last)], axis=0)
            right = jnp.concatenate([sides[t][1] for t in range(first, last)], axis=0)
            high, mid, low = split(left)
            r_high, r_mid, r_low = split(jnp.concatenate([left, right], axis=1))
            change = contract(
                jnp.concatenate([high, high, mid, mid, high, low], axis=0),
                jnp.concatenate([r_high, r_mid, r_high, r_mid, r_low, r_high], axis=0),
                0,
                0,
            )
            for t in range(last, tiles):
                part = change[8 * t : 8 * t + 8, :]
                sides[t] = [sides[t][0] - part[:, :size], sides[t][1] - part[:, size:]]
    return jnp.concatenate([side[1] for side in sides], axis=0)


def unpack(packed):
    half = packed.shape[1]
    cut = half // 2
    row = lax.broadcasted_iota(i32, (half, half), 0)
    lane = lax.broadcasted_iota(i32, (half, half), 1)
    folded = packed[:cut]
    keep = lane[:cut] >= row[:cut]
    upper = jnp.where(keep, folded, 0.0)
    lower = pltpu.roll(jnp.where(keep, 0.0, folded), cut, 1)
    triangle = jnp.concatenate([upper, lower], axis=0)
    return jnp.where(row == lane, packed[cut : cut + 1], triangle + triangle.T)


def invert(t, tab, own, other, gram, inverse, scale):
    cut = own.shape[1] // 2
    my_col = tab[t.col]
    gram[my_col] = own[...] * scale
    gram[1 - my_col] = other[...] * scale
    low = inverse_factor(unpack(gram[0]))
    lower = jnp.concatenate([gram[n, pl.ds(cut + 8, cut), :] for n in range(2)], axis=0)
    across = contract(lower, low, 1, 1, HIGHEST)
    high = inverse_factor(unpack(gram[1]) - contract(across, across, 1, 1, HIGHEST))
    inverse[0, 0] = low
    inverse[0, 1] = jnp.zeros_like(low)
    inverse[1, 0] = -contract(high, contract(across, low, 1, 0, HIGHEST), 1, 0, HIGHEST)
    inverse[1, 1] = high


def normal_blocks(t, tab, inverse, mine, other, store):
    my_col = tab[t.col]
    half = mine.shape[1]
    factor = jnp.concatenate([inverse[my_col, my_col], inverse[my_col, 1 - my_col]], axis=1)
    high, mid, _ = split(factor)
    two = jnp.concatenate([high, mid], axis=0)

    @pl.loop(0, mine.shape[0])
    def _(i):
        y_high, y_mid, _ = split(jnp.concatenate([mine[i], other[i]], axis=0))
        by_high = contract(two, y_high, 1, 0)
        store(i, by_high[:half] + (by_high[half:] + contract(high, y_mid, 1, 0)))


def start_copies(pairs, sems):
    copies = [pltpu.make_async_copy(a, b, sems.at[n]) for n, (a, b) in enumerate(pairs)]
    for copy in copies:
        copy.start()
    return copies


def make_second_kernel(t, scale):
    def kernel(
        tab, own_g, other_g, mine_hbm, other_hbm, ppmi_hbm, normal, near, far, hot,
        gram, inverse, mine, other, ppmi, sems,
    ):
        copies = start_copies([(mine_hbm, mine), (other_hbm, other), (ppmi_hbm, ppmi)], sems)
        invert(t, tab, own_g, other_g, gram, inverse, scale)
        for copy in copies:
            copy.wait()

        def store(i, value):
            normal[i] = value.astype(bf16)

        normal_blocks(t, tab, inverse, mine, other, store)
        gather_hot(t, tab, normal, near, far)
        hot_products(t, tab, normal, ppmi, hot)

    return kernel


def make_final_kernel(t, scale):
    def kernel(
        tab, own_g, other_g, mine_hbm, other_hbm, out, gram, inverse, mine, other, held, sems
    ):
        copies = start_copies([(mine_hbm, mine), (other_hbm, other)], sems)
        invert(t, tab, own_g, other_g, gram, inverse, scale)
        for copy in copies:
            copy.wait()

        def leave(i):
            return pltpu.make_async_copy(held.at[i], out.at[i], sems.at[2])

        def store(i, value):
            held[i] = value.T
            leave(i).start()

        normal_blocks(t, tab, inverse, mine, other, store)

        @pl.loop(0, held.shape[0])
        def _(i):
            leave(i).wait()

    return kernel


def body(counts, block_pairs, sketch):
    groups = lax.axis_size("row")
    me = lax.axis_index("row")
    my_col = lax.axis_index("col")
    nnz, rows, _ = counts.shape
    blocks, _, half = sketch.shape
    vocab = blocks * rows * groups
    t = Table(groups, nnz)
    hot = t.hot
    depth = -(-2 * nnz // 8) * 8

    def peer(x, k):
        return lax.ppermute(x, "row", [(r, r ^ k) for r in range(groups)])

    def swap(x):
        return lax.ppermute(x, "col", [(0, 1), (1, 0)])

    def exchange(x):
        return lax.all_to_all(x, "row", split_axis=0, concat_axis=0, tiled=True)

    def add_up(x):
        for bit in t.bits:
            x = x + peer(x, bit)
        return x

    def spread(part, steps, got=None):
        order = [0]
        for n, bit in enumerate(steps):
            if n or got is None:
                got = peer(part, bit)
            order += [k ^ bit for k in order]
            if n < len(steps) - 1:
                part = jnp.concatenate([part, got], axis=0)
        return part, got, order

    def halve(x, kept, bit):
        low = sum(1 for k in kept if k < bit)
        x = x.reshape(-1, 2, low, *x.shape[1:])
        return [x[:, n].reshape(-1, *x.shape[3:]) for n in range(2)]

    def scatter_hot(near, far, got, towards):
        kept = list(range(groups))
        for bit in t.steps:
            if bit != t.steps[0]:
                near, far = halve(part, kept, bit)
                got = peer(far, bit)
            towards = halve(towards, kept, bit)[0]
            kept = [k for k in kept if not k & bit]
            stay = (towards & bit) == 0
            part = jnp.where(stay[:, :, None, None], near, got)
        return part

    def send_shape(slots):
        return shape((groups, slots, half, rows), bf16)

    hot_shape = shape((1, hot, half, rows), bf16)
    side_shape = shape((groups // 2, hot, half, rows), bf16)
    ppmi_shape = shape((nnz, rows, rows), bf16)
    result_shape = shape((blocks, half, rows), f32)

    sums = call(sums_kernel, shape((1, depth, rows), f32), [VMEM], vmem=8)(counts)
    tab, towards = t.build(block_pairs, me, my_col)
    turned, send_x, near, far = call(
        make_source_kernel(t),
        [shape((blocks, half, rows), bf16), send_shape(1), side_shape, side_shape],
        [SMEM, VMEM],
        vmem=8,
    )(tab, sketch)

    row_ids = block_pairs[:, :, 0] * groups + jnp.arange(groups)[:, None]
    col_ids = block_pairs[:, :, 2] * groups + block_pairs[:, :, 1]
    no_id = jnp.full((groups, depth - 2 * nnz), -1, i32)
    ids = jnp.concatenate([row_ids, col_ids, no_id], axis=1)
    sums_a, sums_b, order = spread(sums, t.bits[::-1])
    ids = jnp.take(ids, me ^ jnp.array(order), axis=0)
    my_ids = ids[0]
    match = (my_ids[:, None] == ids.reshape(-1)[None, :]).astype(bf16)

    got_x, x_step = exchange(send_x), peer(far, t.steps[0])
    ppmi, hot_t = call(
        make_ppmi_kernel(t),
        [ppmi_shape, hot_shape],
        [SMEM] + [VMEM] * 5,
        scratch=[pltpu.VMEM((depth, rows), f32)],
        vmem=12,
    )(tab, match, counts, turned, sums_a, sums_b)

    def finish(source, got_x, near, far, x_step, hot_t):
        t_step = peer(hot_t, t.steps[-1])
        if x_step is None:
            x_step = peer(far, t.steps[0])
        merged = got_x is None
        send = call(
            make_main_kernel(t, merged), send_shape(1 + merged), [SMEM, VMEM, VMEM], vmem=8
        )(tab, source, ppmi)
        send, t_step = lax.optimization_barrier((send, t_step))
        got = [exchange(send)] + ([] if merged else [got_x])
        hot_x = scatter_hot(near, far, x_step, towards)
        hot_a, hot_b, order = spread(hot_t, t.steps[::-1], t_step)
        result = call(
            make_result_kernel(t, order),
            result_shape,
            [SMEM] + [VMEM] * (4 + len(got)),
            vmem=12,
        )(tab, ppmi, *got, hot_x, hot_a, hot_b)
        other = swap(result)
        square = call(own_gram_kernel, shape((half, half), f32), [VMEM], vmem=12)(result)
        gram = call(
            make_cross_gram_kernel(t),
            shape((half + 8, half), f32),
            [SMEM] + [VMEM] * 3,
            vmem=16,
        )(tab, result, other, square)
        gram = add_up(gram)
        return result, other, gram, swap(gram)

    gram_scratch = [
        pltpu.VMEM((2, half + 8, half), f32),
        pltpu.VMEM((2, 2, half, half), f32),
    ]
    result_scratch = [pltpu.VMEM((blocks, half, rows), f32)] * 2
    result, other, gram, other_gram = finish(
        turned, got_x, near, far, x_step, hot_t
    )
    normal, near, far, hot_t = call(
        make_second_kernel(t, 1.0 / vocab),
        [shape((blocks, half, rows), bf16), side_shape, side_shape, hot_shape],
        [SMEM] + [VMEM] * 2 + [ANY] * 3,
        scratch=gram_scratch
        + result_scratch
        + [pltpu.VMEM((nnz, rows, rows), bf16), pltpu.SemaphoreType.DMA((3,))],
    )(tab, gram, other_gram, result, other, ppmi)
    result, other, gram, other_gram = finish(normal, None, near, far, None, hot_t)
    return call(
        make_final_kernel(t, 1.0 / vocab),
        shape((blocks, rows, half), f32),
        [SMEM] + [VMEM] * 2 + [ANY] * 2,
        ANY,
        scratch=gram_scratch
        + result_scratch
        + [pltpu.VMEM((blocks, rows, half), f32), pltpu.SemaphoreType.DMA((3,))],
    )(tab, gram, other_gram, result, other)


def solution(mesh):
    placed = (
        P(("decade", "row"), None, None),
        P("decade", None, None),
        P(None, ("decade", "row"), "col"),
    )
    return jax.shard_map(
        body,
        mesh=mesh,
        in_specs=placed,
        out_specs=P(None, ("decade", "row"), "col"),
        check_vma=False,
    )
```

```python
import jax
import jax.numpy as jnp
from jax import lax
from jax.experimental import pallas as pl
from jax.experimental.pallas import tpu as pltpu
from jax.sharding import PartitionSpec as P

MIB = 1 << 20
HIGHEST = lax.Precision.HIGHEST
VMEM = pl.BlockSpec(memory_space=pltpu.VMEM)
SMEM = pl.BlockSpec(memory_space=pltpu.SMEM)
ANY = pl.BlockSpec(memory_space=pl.ANY)
HBM = pl.BlockSpec(memory_space=pltpu.HBM)
shape = jax.ShapeDtypeStruct
f32, bf16, i32 = jnp.float32, jnp.bfloat16, jnp.int32


def contract(a, b, a_dim, b_dim, precision=None):
    return lax.dot_general(
        a,
        b,
        (((a_dim,), (b_dim,)), ((), ())),
        precision=precision,
        preferred_element_type=f32,
    )


def call(kernel, out_shape, in_specs, out_specs=None, scratch=(), flops=0, vmem=20):
    if out_specs is None:
        out_specs = jax.tree.map(lambda _: VMEM, out_shape)
    return pl.pallas_call(
        kernel,
        out_shape=out_shape,
        in_specs=in_specs,
        out_specs=out_specs,
        scratch_shapes=list(scratch),
        compiler_params=pltpu.CompilerParams(vmem_limit_bytes=vmem * MIB),
        cost_estimate=pl.CostEstimate(flops=flops, bytes_accessed=4 * MIB, transcendentals=0),
    )


class Table:
    def __init__(self, groups, nnz):
        self.groups, self.nnz, self.hot = groups, nnz, nnz - groups
        bits = [1 << b for b in range(groups.bit_length() - 1)]
        self.bits = bits
        self.steps = bits[1:-1] + bits[:1] + bits[-1:]
        self.main_j = 0
        self.hot_j = self.main_j + groups
        self.row_i = self.hot_j + groups * self.hot
        self.dest = self.row_i + nnz
        self.col = self.dest + nnz

    def build(self, block_pairs, me, my_col):
        groups = self.groups
        mine = lax.dynamic_index_in_dim(block_pairs, me, 0, keepdims=False)
        main = block_pairs[:, :groups]
        main_j = jnp.sum(jnp.where(main[:, :, 1] == me, main[:, :, 2], 0), axis=1)
        late = jnp.take(block_pairs[:, groups:], me ^ jnp.arange(groups), axis=0)
        hot_j = jnp.where(late[:, :, 1] == me, late[:, :, 2], -1).reshape(-1)
        parts = [main_j, hot_j, mine[:, 0], mine[:, 1], my_col[None]]
        return jnp.concatenate([p.astype(i32) for p in parts]), late[:, :, 1] ^ me


def sums_kernel(counts_hbm, sums_hbm, counts, sums, sems):
    nnz, rows, cols = counts.shape
    groups = sums_hbm.shape[0]
    loads = start_copies([(counts_hbm.at[s], counts.at[s]) for s in range(nnz)], sems)
    ones = jnp.ones((8, cols), bf16)
    sums[...] = jnp.zeros(sums.shape, f32)
    for s in range(nnz):
        loads[s].wait()
        block = counts[s].astype(bf16)
        sums[pl.ds(s, 1), :] = contract(ones, block, 1, 1)[0:1, :]
        sums[pl.ds(nnz + s, 1), :] = contract(ones, block, 1, 0)[0:1, :]
    for copy in start_copies([(sums, sums_hbm.at[r]) for r in range(groups)], sems.at[nnz:]):
        copy.wait()


def gather_hot(t, tab, blocks, near, far):
    bit = t.steps[0]
    for k in range(t.groups):
        place = (k // (2 * bit)) * bit + k % bit
        for m in range(t.hot):
            j = tab[t.hot_j + k * t.hot + m]

            @pl.when(j >= 0)
            def _():
                (far if k & bit else near)[place, m] = blocks[j]


def product(t, tab, blocks, ppmi, s):
    return contract(blocks[tab[t.row_i + s]], ppmi[s], 1, 0).astype(bf16)


def hot_products(t, tab, blocks, ppmi, hot):
    for m in range(t.hot):
        hot[0, m] = product(t, tab, blocks, ppmi, t.groups + m)


def gather_main(t, tab, blocks, send, slot):
    for r in range(t.groups):
        send[r, slot] = blocks[tab[t.main_j + r]]


def make_main_kernel(t, with_blocks):
    def kernel(tab, blocks, ppmi, send):
        if with_blocks:
            gather_main(t, tab, blocks, send, 1)
        for s in range(t.groups):
            send[tab[t.dest + s], 0] = product(t, tab, blocks, ppmi, s)

    return kernel


def make_source_kernel(t):
    def kernel(tab, sketch_ref, turned_hbm, send, near, far, turned, sems):
        @pl.loop(0, sketch_ref.shape[0])
        def _(i):
            turned[i] = sketch_ref[i].T

        copies = start_copies(
            [(turned.at[tab[t.main_j + r]], send.at[r, 0]) for r in range(t.groups)]
            + [(turned, turned_hbm)],
            sems,
        )
        gather_hot(t, tab, turned, near, far)
        for copy in copies:
            copy.wait()

    return kernel


def make_ppmi_kernel(t):
    def kernel(tab, match_ref, counts_ref, turned, sums_ref, ppmi_ref, hot, cols_log):
        sums = jnp.concatenate([sums_ref[r] for r in range(t.groups)], axis=0)
        high = jnp.floor(sums * (1.0 / 256.0))
        low = sums - high * 256.0
        match = match_ref[...]
        margins = 256.0 * contract(match, high.astype(bf16), 1, 0) + contract(
            match, low.astype(bf16), 1, 0
        )
        log_total = jnp.log(jnp.sum(sums))
        log_margin = jnp.log(margins)
        cols_log[...] = log_margin
        fill = 128 - log_margin.shape[0] % 128
        row_log = jnp.concatenate(
            [log_margin, jnp.zeros((fill, log_margin.shape[1]), f32)], axis=0
        ).T
        for s in range(t.nnz):
            counts = counts_ref[s]
            scores = (
                jnp.log(counts.astype(f32))
                + log_total
                - row_log[:, s : s + 1]
                - cols_log[pl.ds(t.nnz + s, 1), :]
            )
            ppmi_ref[s] = jnp.where(counts > 0, jnp.maximum(scores, 0.0), 0.0).astype(bf16)
        hot_products(t, tab, turned, ppmi_ref, hot)

    return kernel


def make_result_kernel(t, order):
    def kernel(tab, ppmi_ref, *refs):
        got_t, got_x = refs[0], refs[-5]
        hot_x, hot_a, hot_b, result = refs[-4:]
        slot = got_x.shape[1] - 1
        result[...] = jnp.zeros_like(result)
        for s in range(t.nnz):
            block = got_x[tab[t.dest + s], slot] if s < t.groups else hot_x[0, s - t.groups]
            forward = contract(block, ppmi_ref[s], 1, 1).astype(bf16)
            result[tab[t.row_i + s]] += forward.astype(f32)
        for r in range(t.groups):
            result[tab[t.main_j + r]] += got_t[r, 0].astype(f32)
        for n, k in enumerate(order):
            ref, place = (hot_a, n) if n < t.groups // 2 else (hot_b, n - t.groups // 2)
            for m in range(t.hot):
                j = tab[t.hot_j + k * t.hot + m]

                @pl.when(j >= 0)
                def _():
                    result[j] += ref[place, m].astype(f32)

    return kernel


def split(x):
    high = x.astype(bf16)
    rest = x - high.astype(f32)
    mid = rest.astype(bf16)
    return high, mid, (rest - mid.astype(f32)).astype(bf16)


def lanes(ref, start, count, rows=None):
    picked = [ref[start + n] if rows is None else ref[start + n, rows, :] for n in range(count)]
    return jnp.concatenate(picked, axis=1)


def own_gram_kernel(own, gram):
    blocks, half, _ = own.shape
    step = 4
    square = jnp.zeros((half, half), f32)
    skew = jnp.zeros((half, half), f32)
    for i in range(0, blocks, step):
        high, mid, low = split(lanes(own, i, step))
        stack = contract(jnp.concatenate([high, mid, low], axis=0), high, 1, 1)
        square += stack[0:half] + contract(mid, mid, 1, 1)
        skew += stack[half : 2 * half] + stack[2 * half :]
    gram[...] = square + (skew + skew.T)


def make_cross_gram_kernel(t):
    def kernel(tab, own, other, square, gram):
        blocks, half, _ = own.shape
        cut = half // 2
        step = 4
        full = square[...]
        row = lax.broadcasted_iota(i32, (half, half), 0)
        lane = lax.broadcasted_iota(i32, (half, half), 1)
        diagonal = jnp.sum(jnp.where(row == lane, full, 0.0), axis=0, keepdims=True)
        gram[pl.ds(0, cut), :] = jnp.where(
            lane[:cut] >= row[:cut], full[:cut], pltpu.roll(full[cut:], cut, 1)
        )
        gram[pl.ds(cut, 8), :] = jnp.broadcast_to(diagonal, (8, half))

        def cross(left, rows, right):
            total = jnp.zeros((cut, half), f32)
            for i in range(0, blocks, step):
                high, mid, low = split(lanes(left, i, step, rows))
                r_high, r_mid, r_low = split(lanes(right, i, step))
                by_high = contract(jnp.concatenate([high, mid, low], axis=0), r_high, 1, 1)
                by_mid = contract(jnp.concatenate([high, mid], axis=0), r_mid, 1, 1)
                small = by_high[2 * cut :] + by_mid[cut:] + contract(high, r_low, 1, 1)
                total += by_high[:cut] + (by_high[cut : 2 * cut] + by_mid[:cut] + small)
            gram[pl.ds(cut + 8, cut), :] = total

        @pl.when(tab[t.col] == 0)
        def _():
            cross(other, pl.ds(0, cut), own)

        @pl.when(tab[t.col] == 1)
        def _():
            cross(own, pl.ds(cut, cut), other)

    return kernel


def pivot_rows(left, right, base):
    full = left.shape
    cols = [jnp.broadcast_to(left[:, base + k : base + k + 1], full) for k in range(8)]
    piv = [[jnp.broadcast_to(cols[k][i : i + 1, :], full) for k in range(i + 1)] for i in range(8)]
    rows = [
        [jnp.broadcast_to(side[i : i + 1, :], full) for side in (left, right)] for i in range(8)
    ]
    zero = jnp.zeros(full, f32)
    inv = [[None] * 8 for _ in range(8)]
    done = []
    solved = [[zero, zero] for _ in range(8)]
    for k in range(0, 8, 2):
        a, b, c = piv[k][k], piv[k + 1][k], piv[k + 1][k + 1]
        det = a * c - b * b
        root, det_root = lax.rsqrt(a), lax.rsqrt(det)
        both = det_root * root
        scale = det_root * (a * root)
        across = b * root
        for i in range(k + 2, 8):
            p, q = piv[i][k], piv[i][k + 1]
            piv[i][k] = p * root
            piv[i][k + 1] = (a * q - b * p) * both
        for i in range(k + 2, 8):
            for m in range(k + 2, i + 1):
                piv[i][m] = piv[i][m] - (
                    piv[i][k] * piv[m][k] + piv[i][k + 1] * piv[m][k + 1]
                )
        pair = []
        for side in range(2):
            first = rows[k][side] * root
            second = (rows[k + 1][side] - across * first) * scale
            pair.append((first, second))
            for i in range(k + 2, 8):
                rows[i][side] = rows[i][side] - (piv[i][k] * first + piv[i][k + 1] * second)
        done += [[pair[0][0], pair[1][0]], [pair[0][1], pair[1][1]]]
        for i in range(k):
            inv[k][i] = inv[k][i] * root
            inv[k + 1][i] = (inv[k + 1][i] - across * inv[k][i]) * scale
        inv[k][k] = root
        inv[k + 1][k] = -across * root * scale
        inv[k + 1][k + 1] = scale
        for i in range(k + 2, 8):
            for m in range(k + 2):
                part = piv[i][k + 1] * inv[k + 1][m]
                if m <= k:
                    part = part + piv[i][k] * inv[k][m]
                inv[i][m] = -part if inv[i][m] is None else inv[i][m] - part
        for n in (k, k + 1):
            for i in range(n + 1):
                for side in range(2):
                    solved[i][side] = solved[i][side] + inv[n][i] * done[n][side]
    return done, solved


def inverse_factor(block):
    size = block.shape[0]
    tiles = size // 8
    panel = 4
    full = (8, size)
    lane = lax.broadcasted_iota(i32, full, 1)
    sub = lax.broadcasted_iota(i32, full, 0)
    sides = [
        [block[8 * t : 8 * t + 8, :], (lane == sub + 8 * t).astype(f32)] for t in range(tiles)
    ]
    for first in range(0, tiles, panel):
        last = first + panel
        for j in range(first, last):
            rows, solved = pivot_rows(*sides[j], 8 * j)
            for t in range(j + 1, last):
                old = sides[t][0]
                new = list(sides[t])
                for k in range(8):
                    col = jnp.broadcast_to(old[:, 8 * j + k : 8 * j + k + 1], full)
                    new = [new[n] - col * solved[k][n] for n in range(2)]
                sides[t] = new
            for n in range(2):
                done = rows[0][n]
                for i in range(1, 8):
                    done = jnp.where(sub == i, rows[i][n], done)
                sides[j][n] = done
        if last < tiles:
            left = jnp.concatenate([sides[t][0] for t in range(first, last)], axis=0)
            right = jnp.concatenate([sides[t][1] for t in range(first, last)], axis=0)
            high, mid, low = split(left)
            r_high, r_mid, r_low = split(jnp.concatenate([left, right], axis=1))
            change = contract(
                jnp.concatenate([high, high, mid, mid, high, low], axis=0),
                jnp.concatenate([r_high, r_mid, r_high, r_mid, r_low, r_high], axis=0),
                0,
                0,
            )
            for t in range(last, tiles):
                part = change[8 * t : 8 * t + 8, :]
                sides[t] = [sides[t][0] - part[:, :size], sides[t][1] - part[:, size:]]
    return jnp.concatenate([side[1] for side in sides], axis=0)


def unpack(packed):
    half = packed.shape[1]
    cut = half // 2
    row = lax.broadcasted_iota(i32, (half, half), 0)
    lane = lax.broadcasted_iota(i32, (half, half), 1)
    folded = packed[:cut]
    keep = lane[:cut] >= row[:cut]
    upper = jnp.where(keep, folded, 0.0)
    lower = pltpu.roll(jnp.where(keep, 0.0, folded), cut, 1)
    triangle = jnp.concatenate([upper, lower], axis=0)
    return jnp.where(row == lane, packed[cut : cut + 1], triangle + triangle.T)


def invert(t, tab, own, other, gram, inverse, scale):
    cut = own.shape[1] // 2
    my_col = tab[t.col]
    gram[my_col] = own[...] * scale
    gram[1 - my_col] = other[...] * scale
    low = inverse_factor(unpack(gram[0]))
    lower = jnp.concatenate([gram[n, pl.ds(cut + 8, cut), :] for n in range(2)], axis=0)
    across = contract(lower, low, 1, 1, HIGHEST)
    high = inverse_factor(unpack(gram[1]) - contract(across, across, 1, 1, HIGHEST))
    inverse[0, 0] = low
    inverse[0, 1] = jnp.zeros_like(low)
    inverse[1, 0] = -contract(high, contract(across, low, 1, 0, HIGHEST), 1, 0, HIGHEST)
    inverse[1, 1] = high


def normal_blocks(t, tab, inverse, mine, other, store):
    my_col = tab[t.col]
    half = mine.shape[1]
    factor = jnp.concatenate([inverse[my_col, my_col], inverse[my_col, 1 - my_col]], axis=1)
    high, mid, _ = split(factor)
    two = jnp.concatenate([high, mid], axis=0)

    @pl.loop(0, mine.shape[0])
    def _(i):
        y_high, y_mid, _ = split(jnp.concatenate([mine[i], other[i]], axis=0))
        by_high = contract(two, y_high, 1, 0)
        store(i, by_high[:half] + (by_high[half:] + contract(high, y_mid, 1, 0)))


def start_copies(pairs, sems):
    copies = [pltpu.make_async_copy(a, b, sems.at[n]) for n, (a, b) in enumerate(pairs)]
    for copy in copies:
        copy.start()
    return copies


def make_second_kernel(t, scale):
    def kernel(
        tab, own_g, other_g, mine_hbm, other_hbm, ppmi_hbm, normal, near, far, hot,
        gram, inverse, mine, other, ppmi, sems,
    ):
        copies = start_copies([(mine_hbm, mine), (other_hbm, other), (ppmi_hbm, ppmi)], sems)
        invert(t, tab, own_g, other_g, gram, inverse, scale)
        for copy in copies:
            copy.wait()

        def store(i, value):
            normal[i] = value.astype(bf16)

        normal_blocks(t, tab, inverse, mine, other, store)
        gather_hot(t, tab, normal, near, far)
        hot_products(t, tab, normal, ppmi, hot)

    return kernel


def make_final_kernel(t, scale):
    def kernel(
        tab, own_g, other_g, mine_hbm, other_hbm, out, gram, inverse, mine, other, held, sems
    ):
        copies = start_copies([(mine_hbm, mine), (other_hbm, other)], sems)
        invert(t, tab, own_g, other_g, gram, inverse, scale)
        for copy in copies:
            copy.wait()

        def leave(i):
            return pltpu.make_async_copy(held.at[i], out.at[i], sems.at[2])

        def store(i, value):
            held[i] = value.T
            leave(i).start()

        normal_blocks(t, tab, inverse, mine, other, store)

        @pl.loop(0, held.shape[0])
        def _(i):
            leave(i).wait()

    return kernel


def body(counts, block_pairs, sketch):
    groups = lax.axis_size("row")
    me = lax.axis_index("row")
    my_col = lax.axis_index("col")
    nnz, rows, _ = counts.shape
    blocks, _, half = sketch.shape
    vocab = blocks * rows * groups
    t = Table(groups, nnz)
    hot = t.hot
    depth = -(-2 * nnz // 8) * 8

    def peer(x, k):
        return lax.ppermute(x, "row", [(r, r ^ k) for r in range(groups)])

    def swap(x):
        return lax.ppermute(x, "col", [(0, 1), (1, 0)])

    def exchange(x):
        return lax.all_to_all(x, "row", split_axis=0, concat_axis=0, tiled=True)

    def add_up(x):
        for bit in t.bits:
            x = x + peer(x, bit)
        return x

    def spread(part, steps, got=None):
        order = [0]
        for n, bit in enumerate(steps):
            if n or got is None:
                got = peer(part, bit)
            order += [k ^ bit for k in order]
            if n < len(steps) - 1:
                part = jnp.concatenate([part, got], axis=0)
        return part, got, order

    def halve(x, kept, bit):
        low = sum(1 for k in kept if k < bit)
        x = x.reshape(-1, 2, low, *x.shape[1:])
        return [x[:, n].reshape(-1, *x.shape[3:]) for n in range(2)]

    def scatter_hot(near, far, got, towards):
        kept = list(range(groups))
        for bit in t.steps:
            if bit != t.steps[0]:
                near, far = halve(part, kept, bit)
                got = peer(far, bit)
            towards = halve(towards, kept, bit)[0]
            kept = [k for k in kept if not k & bit]
            stay = (towards & bit) == 0
            part = jnp.where(stay[:, :, None, None], near, got)
        return part

    def send_shape(slots):
        return shape((groups, slots, half, rows), bf16)

    hot_shape = shape((1, hot, half, rows), bf16)
    side_shape = shape((groups // 2, hot, half, rows), bf16)
    ppmi_shape = shape((nnz, rows, rows), bf16)
    result_shape = shape((blocks, half, rows), f32)

    sums = call(
        sums_kernel,
        shape((groups, depth, rows), f32),
        [HBM],
        HBM,
        scratch=[
            pltpu.VMEM((nnz, rows, rows), i32),
            pltpu.VMEM((depth, rows), f32),
            pltpu.SemaphoreType.DMA((nnz + groups,)),
        ],
    )(counts)
    sums_all = exchange(sums)
    tab, towards = t.build(block_pairs, me, my_col)
    turned, send_x, near, far = call(
        make_source_kernel(t),
        [shape((blocks, half, rows), bf16), send_shape(1), side_shape, side_shape],
        [SMEM, VMEM],
        [HBM, HBM, VMEM, VMEM],
        scratch=[
            pltpu.VMEM((blocks, half, rows), bf16),
            pltpu.SemaphoreType.DMA((groups + 1,)),
        ],
        vmem=8,
    )(tab, sketch)

    row_ids = block_pairs[:, :, 0] * groups + jnp.arange(groups)[:, None]
    col_ids = block_pairs[:, :, 2] * groups + block_pairs[:, :, 1]
    no_id = jnp.full((groups, depth - 2 * nnz), -1, i32)
    ids = jnp.concatenate([row_ids, col_ids, no_id], axis=1)
    my_ids = lax.dynamic_index_in_dim(ids, me, 0, keepdims=False)
    match = (my_ids[:, None] == ids.reshape(-1)[None, :]).astype(bf16)

    send_x, sums_all = lax.optimization_barrier((send_x, sums_all))
    got_x, x_step = exchange(send_x), peer(far, t.steps[0])
    ppmi, hot_t = call(
        make_ppmi_kernel(t),
        [ppmi_shape, hot_shape],
        [SMEM] + [VMEM] * 4,
        scratch=[pltpu.VMEM((depth, rows), f32)],
        vmem=12,
    )(tab, match, counts, turned, sums_all)

    def finish(source, got_x, near, far, x_step, hot_t):
        t_step = peer(hot_t, t.steps[-1])
        if x_step is None:
            x_step = peer(far, t.steps[0])
        merged = got_x is None
        send = call(
            make_main_kernel(t, merged), send_shape(1 + merged), [SMEM, VMEM, VMEM], vmem=8
        )(tab, source, ppmi)
        if merged:
            send, x_step, t_step = lax.optimization_barrier((send, x_step, t_step))
        else:
            send, t_step = lax.optimization_barrier((send, t_step))
        got = [exchange(send)] + ([] if merged else [got_x])
        hot_x = scatter_hot(near, far, x_step, towards)
        hot_a, hot_b, order = spread(hot_t, t.steps[::-1], t_step)
        result = call(
            make_result_kernel(t, order),
            result_shape,
            [SMEM] + [VMEM] * (4 + len(got)),
            vmem=12,
        )(tab, ppmi, *got, hot_x, hot_a, hot_b)
        other = swap(result)
        square = call(own_gram_kernel, shape((half, half), f32), [VMEM], vmem=12)(result)
        gram = call(
            make_cross_gram_kernel(t),
            shape((half + 8, half), f32),
            [SMEM] + [VMEM] * 3,
            vmem=16,
        )(tab, result, other, square)
        gram = add_up(gram)
        return result, other, gram, swap(gram)

    gram_scratch = [
        pltpu.VMEM((2, half + 8, half), f32),
        pltpu.VMEM((2, 2, half, half), f32),
    ]
    result_scratch = [pltpu.VMEM((blocks, half, rows), f32)] * 2
    result, other, gram, other_gram = finish(
        turned, got_x, near, far, x_step, hot_t
    )
    normal, near, far, hot_t = call(
        make_second_kernel(t, 1.0 / vocab),
        [shape((blocks, half, rows), bf16), side_shape, side_shape, hot_shape],
        [SMEM] + [VMEM] * 2 + [ANY] * 3,
        scratch=gram_scratch
        + result_scratch
        + [pltpu.VMEM((nnz, rows, rows), bf16), pltpu.SemaphoreType.DMA((3,))],
    )(tab, gram, other_gram, result, other, ppmi)
    result, other, gram, other_gram = finish(normal, None, near, far, None, hot_t)
    return call(
        make_final_kernel(t, 1.0 / vocab),
        shape((blocks, rows, half), f32),
        [SMEM] + [VMEM] * 2 + [ANY] * 2,
        ANY,
        scratch=gram_scratch
        + result_scratch
        + [pltpu.VMEM((blocks, rows, half), f32), pltpu.SemaphoreType.DMA((3,))],
    )(tab, gram, other_gram, result, other)


def solution(mesh):
    placed = (
        P(("decade", "row"), None, None),
        P("decade", None, None),
        P(None, ("decade", "row"), "col"),
    )
    return jax.shard_map(
        body,
        mesh=mesh,
        in_specs=placed,
        out_specs=P(None, ("decade", "row"), "col"),
        check_vma=False,
    )
```

```python
import jax
import jax.numpy as jnp
from jax import lax
from jax.experimental import pallas as pl
from jax.experimental.pallas import tpu as pltpu
from jax.sharding import PartitionSpec as P

MIB = 1 << 20
HIGHEST = lax.Precision.HIGHEST
VMEM = pl.BlockSpec(memory_space=pltpu.VMEM)
SMEM = pl.BlockSpec(memory_space=pltpu.SMEM)
ANY = pl.BlockSpec(memory_space=pl.ANY)
shape = jax.ShapeDtypeStruct
f32, bf16, i32 = jnp.float32, jnp.bfloat16, jnp.int32


def contract(a, b, a_dim, b_dim, precision=None):
    return lax.dot_general(
        a,
        b,
        (((a_dim,), (b_dim,)), ((), ())),
        precision=precision,
        preferred_element_type=f32,
    )


def call(kernel, out_shape, in_specs, out_specs=None, scratch=(), flops=0, vmem=20):
    if out_specs is None:
        out_specs = jax.tree.map(lambda _: VMEM, out_shape)
    return pl.pallas_call(
        kernel,
        out_shape=out_shape,
        in_specs=in_specs,
        out_specs=out_specs,
        scratch_shapes=list(scratch),
        compiler_params=pltpu.CompilerParams(vmem_limit_bytes=vmem * MIB),
        cost_estimate=pl.CostEstimate(flops=flops, bytes_accessed=4 * MIB, transcendentals=0),
    )


class Table:
    def __init__(self, groups, nnz):
        self.groups, self.nnz, self.hot = groups, nnz, nnz - groups
        bits = [1 << b for b in range(groups.bit_length() - 1)]
        self.bits = bits
        self.steps = bits[1:-1] + bits[:1] + bits[-1:]
        self.main_j = 0
        self.hot_j = self.main_j + groups
        self.row_i = self.hot_j + groups * self.hot
        self.dest = self.row_i + nnz
        self.col = self.dest + nnz

    def build(self, block_pairs, me, my_col):
        groups = self.groups
        mine = lax.dynamic_index_in_dim(block_pairs, me, 0, keepdims=False)
        main = block_pairs[:, :groups]
        main_j = jnp.sum(jnp.where(main[:, :, 1] == me, main[:, :, 2], 0), axis=1)
        late = jnp.take(block_pairs[:, groups:], me ^ jnp.arange(groups), axis=0)
        hot_j = jnp.where(late[:, :, 1] == me, late[:, :, 2], -1).reshape(-1)
        parts = [main_j, hot_j, mine[:, 0], mine[:, 1], my_col[None]]
        return jnp.concatenate([p.astype(i32) for p in parts]), late[:, :, 1] ^ me


def sums_kernel(counts_ref, sums_ref):
    nnz, rows, cols = counts_ref.shape
    ones = jnp.ones((8, cols), bf16)
    sums_ref[0] = jnp.zeros(sums_ref.shape[1:], f32)
    for s in range(nnz):
        block = counts_ref[s].astype(bf16)
        sums_ref[0, pl.ds(s, 1), :] = contract(ones, block, 1, 1)[0:1, :]
        sums_ref[0, pl.ds(nnz + s, 1), :] = contract(ones, block, 1, 0)[0:1, :]
    for r in range(1, sums_ref.shape[0]):
        sums_ref[r] = sums_ref[0]


def gather_hot(t, tab, blocks, near, far):
    bit = t.steps[0]
    for k in range(t.groups):
        place = (k // (2 * bit)) * bit + k % bit
        for m in range(t.hot):
            j = tab[t.hot_j + k * t.hot + m]

            @pl.when(j >= 0)
            def _():
                (far if k & bit else near)[place, m] = blocks[j]


def product(t, tab, blocks, ppmi, s):
    return contract(blocks[tab[t.row_i + s]], ppmi[s], 1, 0).astype(bf16)


def hot_products(t, tab, blocks, ppmi, hot):
    for m in range(t.hot):
        hot[0, m] = product(t, tab, blocks, ppmi, t.groups + m)


def gather_main(t, tab, blocks, send, slot):
    for r in range(t.groups):
        send[r, slot] = blocks[tab[t.main_j + r]]


def make_main_kernel(t, with_blocks):
    def kernel(tab, blocks, ppmi, send):
        if with_blocks:
            gather_main(t, tab, blocks, send, 1)
        for s in range(t.groups):
            send[tab[t.dest + s], 0] = product(t, tab, blocks, ppmi, s)

    return kernel


def make_source_kernel(t):
    def kernel(tab, sketch_ref, turned, send, near, far):
        @pl.loop(0, sketch_ref.shape[0])
        def _(i):
            turned[i] = sketch_ref[i].T

        gather_main(t, tab, turned, send, 0)
        gather_hot(t, tab, turned, near, far)

    return kernel


def make_ppmi_kernel(t):
    def kernel(tab, match_ref, counts_ref, turned, sums_ref, ppmi_ref, hot, cols_log):
        sums = jnp.concatenate([sums_ref[r] for r in range(t.groups)], axis=0)
        high = jnp.floor(sums * (1.0 / 256.0))
        low = sums - high * 256.0
        match = match_ref[...]
        margins = 256.0 * contract(match, high.astype(bf16), 1, 0) + contract(
            match, low.astype(bf16), 1, 0
        )
        log_total = jnp.log(jnp.sum(sums))
        log_margin = jnp.log(margins)
        cols_log[...] = log_margin
        fill = 128 - log_margin.shape[0] % 128
        row_log = jnp.concatenate(
            [log_margin, jnp.zeros((fill, log_margin.shape[1]), f32)], axis=0
        ).T
        for s in range(t.nnz):
            counts = counts_ref[s]
            scores = (
                jnp.log(counts.astype(f32))
                + log_total
                - row_log[:, s : s + 1]
                - cols_log[pl.ds(t.nnz + s, 1), :]
            )
            ppmi_ref[s] = jnp.where(counts > 0, jnp.maximum(scores, 0.0), 0.0).astype(bf16)
        hot_products(t, tab, turned, ppmi_ref, hot)

    return kernel


def make_result_kernel(t, order):
    def kernel(tab, ppmi_ref, *refs):
        got_t, got_x = refs[0], refs[-5]
        hot_x, hot_a, hot_b, result = refs[-4:]
        slot = got_x.shape[1] - 1
        result[...] = jnp.zeros_like(result)
        for s in range(t.nnz):
            block = got_x[tab[t.dest + s], slot] if s < t.groups else hot_x[0, s - t.groups]
            forward = contract(block, ppmi_ref[s], 1, 1).astype(bf16)
            result[tab[t.row_i + s]] += forward.astype(f32)
        for r in range(t.groups):
            result[tab[t.main_j + r]] += got_t[r, 0].astype(f32)
        for n, k in enumerate(order):
            ref, place = (hot_a, n) if n < t.groups // 2 else (hot_b, n - t.groups // 2)
            for m in range(t.hot):
                j = tab[t.hot_j + k * t.hot + m]

                @pl.when(j >= 0)
                def _():
                    result[j] += ref[place, m].astype(f32)

    return kernel


def split(x):
    high = x.astype(bf16)
    rest = x - high.astype(f32)
    mid = rest.astype(bf16)
    return high, mid, (rest - mid.astype(f32)).astype(bf16)


def lanes(ref, start, count, rows=None):
    picked = [ref[start + n] if rows is None else ref[start + n, rows, :] for n in range(count)]
    return jnp.concatenate(picked, axis=1)


def own_gram_kernel(own, gram):
    blocks, half, _ = own.shape
    step = 4
    square = jnp.zeros((half, half), f32)
    skew = jnp.zeros((half, half), f32)
    for i in range(0, blocks, step):
        high, mid, low = split(lanes(own, i, step))
        stack = contract(jnp.concatenate([high, mid, low], axis=0), high, 1, 1)
        square += stack[0:half] + contract(mid, mid, 1, 1)
        skew += stack[half : 2 * half] + stack[2 * half :]
    gram[...] = square + (skew + skew.T)


def make_cross_gram_kernel(t):
    def kernel(tab, own, other, square, gram):
        blocks, half, _ = own.shape
        cut = half // 2
        step = 4
        full = square[...]
        row = lax.broadcasted_iota(i32, (half, half), 0)
        lane = lax.broadcasted_iota(i32, (half, half), 1)
        diagonal = jnp.sum(jnp.where(row == lane, full, 0.0), axis=0, keepdims=True)
        gram[pl.ds(0, cut), :] = jnp.where(
            lane[:cut] >= row[:cut], full[:cut], pltpu.roll(full[cut:], cut, 1)
        )
        gram[pl.ds(cut, 8), :] = jnp.broadcast_to(diagonal, (8, half))

        def cross(left, rows, right):
            total = jnp.zeros((cut, half), f32)
            for i in range(0, blocks, step):
                high, mid, low = split(lanes(left, i, step, rows))
                r_high, r_mid, r_low = split(lanes(right, i, step))
                by_high = contract(jnp.concatenate([high, mid, low], axis=0), r_high, 1, 1)
                by_mid = contract(jnp.concatenate([high, mid], axis=0), r_mid, 1, 1)
                small = by_high[2 * cut :] + by_mid[cut:] + contract(high, r_low, 1, 1)
                total += by_high[:cut] + (by_high[cut : 2 * cut] + by_mid[:cut] + small)
            gram[pl.ds(cut + 8, cut), :] = total

        @pl.when(tab[t.col] == 0)
        def _():
            cross(other, pl.ds(0, cut), own)

        @pl.when(tab[t.col] == 1)
        def _():
            cross(own, pl.ds(cut, cut), other)

    return kernel


def pivot_rows(left, right, base):
    full = left.shape
    cols = [jnp.broadcast_to(left[:, base + k : base + k + 1], full) for k in range(8)]
    piv = [[jnp.broadcast_to(cols[k][i : i + 1, :], full) for k in range(i + 1)] for i in range(8)]
    rows = [
        [jnp.broadcast_to(side[i : i + 1, :], full) for side in (left, right)] for i in range(8)
    ]
    zero = jnp.zeros(full, f32)
    inv = [[None] * 8 for _ in range(8)]
    done = []
    solved = [[zero, zero] for _ in range(8)]
    for k in range(0, 8, 2):
        a, b, c = piv[k][k], piv[k + 1][k], piv[k + 1][k + 1]
        det = a * c - b * b
        root, det_root = lax.rsqrt(a), lax.rsqrt(det)
        both = det_root * root
        scale = det_root * (a * root)
        across = b * root
        for i in range(k + 2, 8):
            p, q = piv[i][k], piv[i][k + 1]
            piv[i][k] = p * root
            piv[i][k + 1] = (a * q - b * p) * both
        for i in range(k + 2, 8):
            for m in range(k + 2, i + 1):
                piv[i][m] = piv[i][m] - (
                    piv[i][k] * piv[m][k] + piv[i][k + 1] * piv[m][k + 1]
                )
        pair = []
        for side in range(2):
            first = rows[k][side] * root
            second = (rows[k + 1][side] - across * first) * scale
            pair.append((first, second))
            for i in range(k + 2, 8):
                rows[i][side] = rows[i][side] - (piv[i][k] * first + piv[i][k + 1] * second)
        done += [[pair[0][0], pair[1][0]], [pair[0][1], pair[1][1]]]
        for i in range(k):
            inv[k][i] = inv[k][i] * root
            inv[k + 1][i] = (inv[k + 1][i] - across * inv[k][i]) * scale
        inv[k][k] = root
        inv[k + 1][k] = -across * root * scale
        inv[k + 1][k + 1] = scale
        for i in range(k + 2, 8):
            for m in range(k + 2):
                part = piv[i][k + 1] * inv[k + 1][m]
                if m <= k:
                    part = part + piv[i][k] * inv[k][m]
                inv[i][m] = -part if inv[i][m] is None else inv[i][m] - part
        for n in (k, k + 1):
            for i in range(n + 1):
                for side in range(2):
                    solved[i][side] = solved[i][side] + inv[n][i] * done[n][side]
    return done, solved


def inverse_factor(block):
    size = block.shape[0]
    tiles = size // 8
    panel = 4
    full = (8, size)
    lane = lax.broadcasted_iota(i32, full, 1)
    sub = lax.broadcasted_iota(i32, full, 0)
    sides = [
        [block[8 * t : 8 * t + 8, :], (lane == sub + 8 * t).astype(f32)] for t in range(tiles)
    ]
    for first in range(0, tiles, panel):
        last = first + panel
        for j in range(first, last):
            rows, solved = pivot_rows(*sides[j], 8 * j)
            for t in range(j + 1, last):
                old = sides[t][0]
                new = list(sides[t])
                for k in range(8):
                    col = jnp.broadcast_to(old[:, 8 * j + k : 8 * j + k + 1], full)
                    new = [new[n] - col * solved[k][n] for n in range(2)]
                sides[t] = new
            for n in range(2):
                done = rows[0][n]
                for i in range(1, 8):
                    done = jnp.where(sub == i, rows[i][n], done)
                sides[j][n] = done
        if last < tiles:
            left = jnp.concatenate([sides[t][0] for t in range(first, last)], axis=0)
            right = jnp.concatenate([sides[t][1] for t in range(first, last)], axis=0)
            high, mid, low = split(left)
            r_high, r_mid, r_low = split(jnp.concatenate([left, right], axis=1))
            change = contract(
                jnp.concatenate([high, high, mid, mid, high, low], axis=0),
                jnp.concatenate([r_high, r_mid, r_high, r_mid, r_low, r_high], axis=0),
                0,
                0,
            )
            for t in range(last, tiles):
                part = change[8 * t : 8 * t + 8, :]
                sides[t] = [sides[t][0] - part[:, :size], sides[t][1] - part[:, size:]]
    return jnp.concatenate([side[1] for side in sides], axis=0)


def unpack(packed):
    half = packed.shape[1]
    cut = half // 2
    row = lax.broadcasted_iota(i32, (half, half), 0)
    lane = lax.broadcasted_iota(i32, (half, half), 1)
    folded = packed[:cut]
    keep = lane[:cut] >= row[:cut]
    upper = jnp.where(keep, folded, 0.0)
    lower = pltpu.roll(jnp.where(keep, 0.0, folded), cut, 1)
    triangle = jnp.concatenate([upper, lower], axis=0)
    return jnp.where(row == lane, packed[cut : cut + 1], triangle + triangle.T)


def invert(t, tab, own, other, gram, inverse, scale):
    cut = own.shape[1] // 2
    my_col = tab[t.col]
    gram[my_col] = own[...] * scale
    gram[1 - my_col] = other[...] * scale
    low = inverse_factor(unpack(gram[0]))
    lower = jnp.concatenate([gram[n, pl.ds(cut + 8, cut), :] for n in range(2)], axis=0)
    across = contract(lower, low, 1, 1, HIGHEST)
    high = inverse_factor(unpack(gram[1]) - contract(across, across, 1, 1, HIGHEST))
    inverse[0, 0] = low
    inverse[0, 1] = jnp.zeros_like(low)
    inverse[1, 0] = -contract(high, contract(across, low, 1, 0, HIGHEST), 1, 0, HIGHEST)
    inverse[1, 1] = high


def normal_blocks(t, tab, inverse, mine, other, store):
    my_col = tab[t.col]
    half = mine.shape[1]
    factor = jnp.concatenate([inverse[my_col, my_col], inverse[my_col, 1 - my_col]], axis=1)
    high, mid, _ = split(factor)
    two = jnp.concatenate([high, mid], axis=0)

    @pl.loop(0, mine.shape[0])
    def _(i):
        y_high, y_mid, _ = split(jnp.concatenate([mine[i], other[i]], axis=0))
        by_high = contract(two, y_high, 1, 0)
        store(i, by_high[:half] + (by_high[half:] + contract(high, y_mid, 1, 0)))


def start_copies(pairs, sems):
    copies = [pltpu.make_async_copy(a, b, sems.at[n]) for n, (a, b) in enumerate(pairs)]
    for copy in copies:
        copy.start()
    return copies


def make_second_kernel(t, scale):
    def kernel(
        tab, own_g, other_g, mine_hbm, other_hbm, ppmi_hbm, normal, near, far, hot,
        gram, inverse, mine, other, ppmi, sems,
    ):
        copies = start_copies([(mine_hbm, mine), (other_hbm, other), (ppmi_hbm, ppmi)], sems)
        invert(t, tab, own_g, other_g, gram, inverse, scale)
        for copy in copies:
            copy.wait()

        def store(i, value):
            normal[i] = value.astype(bf16)

        normal_blocks(t, tab, inverse, mine, other, store)
        gather_hot(t, tab, normal, near, far)
        hot_products(t, tab, normal, ppmi, hot)

    return kernel


def make_final_kernel(t, scale):
    def kernel(
        tab, own_g, other_g, mine_hbm, other_hbm, out, gram, inverse, mine, other, held, sems
    ):
        copies = start_copies([(mine_hbm, mine), (other_hbm, other)], sems)
        invert(t, tab, own_g, other_g, gram, inverse, scale)
        for copy in copies:
            copy.wait()

        def leave(i):
            return pltpu.make_async_copy(held.at[i], out.at[i], sems.at[2])

        def store(i, value):
            held[i] = value.T
            leave(i).start()

        normal_blocks(t, tab, inverse, mine, other, store)

        @pl.loop(0, held.shape[0])
        def _(i):
            leave(i).wait()

    return kernel


def body(counts, block_pairs, sketch):
    groups = lax.axis_size("row")
    me = lax.axis_index("row")
    my_col = lax.axis_index("col")
    nnz, rows, _ = counts.shape
    blocks, _, half = sketch.shape
    vocab = blocks * rows * groups
    t = Table(groups, nnz)
    hot = t.hot
    depth = -(-2 * nnz // 8) * 8

    def peer(x, k):
        return lax.ppermute(x, "row", [(r, r ^ k) for r in range(groups)])

    def swap(x):
        return lax.ppermute(x, "col", [(0, 1), (1, 0)])

    def exchange(x):
        return lax.all_to_all(x, "row", split_axis=0, concat_axis=0, tiled=True)

    def add_up(x):
        for bit in t.bits:
            x = x + peer(x, bit)
        return x

    def spread(part, steps, got=None):
        order = [0]
        for n, bit in enumerate(steps):
            if n or got is None:
                got = peer(part, bit)
            order += [k ^ bit for k in order]
            if n < len(steps) - 1:
                part = jnp.concatenate([part, got], axis=0)
        return part, got, order

    def halve(x, kept, bit):
        low = sum(1 for k in kept if k < bit)
        x = x.reshape(-1, 2, low, *x.shape[1:])
        return [x[:, n].reshape(-1, *x.shape[3:]) for n in range(2)]

    def scatter_hot(near, far, got, towards):
        kept = list(range(groups))
        for bit in t.steps:
            if bit != t.steps[0]:
                near, far = halve(part, kept, bit)
                got = peer(far, bit)
            towards = halve(towards, kept, bit)[0]
            kept = [k for k in kept if not k & bit]
            stay = (towards & bit) == 0
            part = jnp.where(stay[:, :, None, None], near, got)
        return part

    def send_shape(slots):
        return shape((groups, slots, half, rows), bf16)

    hot_shape = shape((1, hot, half, rows), bf16)
    side_shape = shape((groups // 2, hot, half, rows), bf16)
    ppmi_shape = shape((nnz, rows, rows), bf16)
    result_shape = shape((blocks, half, rows), f32)

    sums = call(sums_kernel, shape((groups, depth, rows), f32), [VMEM], vmem=8)(counts)
    sums_all = exchange(sums)
    tab, towards = t.build(block_pairs, me, my_col)
    turned, send_x, near, far = call(
        make_source_kernel(t),
        [shape((blocks, half, rows), bf16), send_shape(1), side_shape, side_shape],
        [SMEM, VMEM],
        vmem=8,
    )(tab, sketch)

    row_ids = block_pairs[:, :, 0] * groups + jnp.arange(groups)[:, None]
    col_ids = block_pairs[:, :, 2] * groups + block_pairs[:, :, 1]
    no_id = jnp.full((groups, depth - 2 * nnz), -1, i32)
    ids = jnp.concatenate([row_ids, col_ids, no_id], axis=1)
    my_ids = lax.dynamic_index_in_dim(ids, me, 0, keepdims=False)
    match = (my_ids[:, None] == ids.reshape(-1)[None, :]).astype(bf16)

    send_x, sums_all = lax.optimization_barrier((send_x, sums_all))
    got_x, x_step = exchange(send_x), peer(far, t.steps[0])
    ppmi, hot_t = call(
        make_ppmi_kernel(t),
        [ppmi_shape, hot_shape],
        [SMEM] + [VMEM] * 4,
        scratch=[pltpu.VMEM((depth, rows), f32)],
        vmem=12,
    )(tab, match, counts, turned, sums_all)

    def finish(source, got_x, near, far, x_step, hot_t):
        t_step = peer(hot_t, t.steps[-1])
        if x_step is None:
            x_step = peer(far, t.steps[0])
        merged = got_x is None
        send = call(
            make_main_kernel(t, merged), send_shape(1 + merged), [SMEM, VMEM, VMEM], vmem=8
        )(tab, source, ppmi)
        if merged:
            send, x_step, t_step = lax.optimization_barrier((send, x_step, t_step))
        else:
            send, t_step = lax.optimization_barrier((send, t_step))
        got = [exchange(send)] + ([] if merged else [got_x])
        hot_x = scatter_hot(near, far, x_step, towards)
        hot_a, hot_b, order = spread(hot_t, t.steps[::-1], t_step)
        result = call(
            make_result_kernel(t, order),
            result_shape,
            [SMEM] + [VMEM] * (4 + len(got)),
            vmem=12,
        )(tab, ppmi, *got, hot_x, hot_a, hot_b)
        other = swap(result)
        square = call(own_gram_kernel, shape((half, half), f32), [VMEM], vmem=12)(result)
        gram = call(
            make_cross_gram_kernel(t),
            shape((half + 8, half), f32),
            [SMEM] + [VMEM] * 3,
            vmem=16,
        )(tab, result, other, square)
        gram = add_up(gram)
        return result, other, gram, swap(gram)

    gram_scratch = [
        pltpu.VMEM((2, half + 8, half), f32),
        pltpu.VMEM((2, 2, half, half), f32),
    ]
    result_scratch = [pltpu.VMEM((blocks, half, rows), f32)] * 2
    result, other, gram, other_gram = finish(
        turned, got_x, near, far, x_step, hot_t
    )
    normal, near, far, hot_t = call(
        make_second_kernel(t, 1.0 / vocab),
        [shape((blocks, half, rows), bf16), side_shape, side_shape, hot_shape],
        [SMEM] + [VMEM] * 2 + [ANY] * 3,
        scratch=gram_scratch
        + result_scratch
        + [pltpu.VMEM((nnz, rows, rows), bf16), pltpu.SemaphoreType.DMA((3,))],
    )(tab, gram, other_gram, result, other, ppmi)
    result, other, gram, other_gram = finish(normal, None, near, far, None, hot_t)
    return call(
        make_final_kernel(t, 1.0 / vocab),
        shape((blocks, rows, half), f32),
        [SMEM] + [VMEM] * 2 + [ANY] * 2,
        ANY,
        scratch=gram_scratch
        + result_scratch
        + [pltpu.VMEM((blocks, rows, half), f32), pltpu.SemaphoreType.DMA((3,))],
    )(tab, gram, other_gram, result, other)


def solution(mesh):
    placed = (
        P(("decade", "row"), None, None),
        P("decade", None, None),
        P(None, ("decade", "row"), "col"),
    )
    return jax.shard_map(
        body,
        mesh=mesh,
        in_specs=placed,
        out_specs=P(None, ("decade", "row"), "col"),
        check_vma=False,
    )
```

```python
import jax
import jax.numpy as jnp
from jax import lax
from jax.experimental import pallas as pl
from jax.experimental.pallas import tpu as pltpu
from jax.sharding import PartitionSpec as P

MIB = 1 << 20
HIGHEST = lax.Precision.HIGHEST
VMEM = pl.BlockSpec(memory_space=pltpu.VMEM)
SMEM = pl.BlockSpec(memory_space=pltpu.SMEM)
ANY = pl.BlockSpec(memory_space=pl.ANY)
shape = jax.ShapeDtypeStruct
f32, bf16, i32 = jnp.float32, jnp.bfloat16, jnp.int32


def contract(a, b, a_dim, b_dim, precision=None):
    return lax.dot_general(
        a,
        b,
        (((a_dim,), (b_dim,)), ((), ())),
        precision=precision,
        preferred_element_type=f32,
    )


def call(kernel, out_shape, in_specs, out_specs=None, scratch=(), flops=0, vmem=20):
    if out_specs is None:
        out_specs = jax.tree.map(lambda _: VMEM, out_shape)
    return pl.pallas_call(
        kernel,
        out_shape=out_shape,
        in_specs=in_specs,
        out_specs=out_specs,
        scratch_shapes=list(scratch),
        compiler_params=pltpu.CompilerParams(vmem_limit_bytes=vmem * MIB),
        cost_estimate=pl.CostEstimate(flops=flops, bytes_accessed=4 * MIB, transcendentals=0),
    )


class Table:
    def __init__(self, groups, nnz):
        self.groups, self.nnz, self.hot = groups, nnz, nnz - groups
        bits = [1 << b for b in range(groups.bit_length() - 1)]
        self.bits = bits
        self.steps = bits[1:-1] + bits[:1] + bits[-1:]
        self.main_j = 0
        self.hot_j = self.main_j + groups
        self.row_i = self.hot_j + groups * self.hot
        self.dest = self.row_i + nnz
        self.col = self.dest + nnz

    def build(self, block_pairs, me, my_col):
        groups = self.groups
        mine = lax.dynamic_index_in_dim(block_pairs, me, 0, keepdims=False)
        main = block_pairs[:, :groups]
        main_j = jnp.sum(jnp.where(main[:, :, 1] == me, main[:, :, 2], 0), axis=1)
        late = jnp.take(block_pairs[:, groups:], me ^ jnp.arange(groups), axis=0)
        hot_j = jnp.where(late[:, :, 1] == me, late[:, :, 2], -1).reshape(-1)
        parts = [main_j, hot_j, mine[:, 0], mine[:, 1], my_col[None]]
        return jnp.concatenate([p.astype(i32) for p in parts]), late[:, :, 1] ^ me


def sums_kernel(counts_ref, sums_ref):
    nnz, rows, cols = counts_ref.shape
    ones = jnp.ones((8, cols), bf16)
    sums_ref[0] = jnp.zeros(sums_ref.shape[1:], f32)
    for s in range(nnz):
        block = counts_ref[s].astype(bf16)
        sums_ref[0, pl.ds(s, 1), :] = contract(ones, block, 1, 1)[0:1, :]
        sums_ref[0, pl.ds(nnz + s, 1), :] = contract(ones, block, 1, 0)[0:1, :]
    for r in range(1, sums_ref.shape[0]):
        sums_ref[r] = sums_ref[0]


def gather_hot(t, tab, blocks, near, far):
    bit = t.steps[0]
    for k in range(t.groups):
        place = (k // (2 * bit)) * bit + k % bit
        for m in range(t.hot):
            j = tab[t.hot_j + k * t.hot + m]

            @pl.when(j >= 0)
            def _():
                (far if k & bit else near)[place, m] = blocks[j]


def product(t, tab, blocks, ppmi, s):
    return contract(blocks[tab[t.row_i + s]], ppmi[s], 1, 0).astype(bf16)


def hot_products(t, tab, blocks, ppmi, hot):
    for m in range(t.hot):
        hot[0, m] = product(t, tab, blocks, ppmi, t.groups + m)


def gather_main(t, tab, blocks, send, slot):
    for r in range(t.groups):
        send[r, slot] = blocks[tab[t.main_j + r]]


def make_main_kernel(t, with_blocks):
    def kernel(tab, blocks, ppmi, send):
        if with_blocks:
            gather_main(t, tab, blocks, send, 1)
        for s in range(t.groups):
            send[tab[t.dest + s], 0] = product(t, tab, blocks, ppmi, s)

    return kernel


def make_source_kernel(t):
    def kernel(tab, sketch_ref, turned, send, near, far):
        @pl.loop(0, sketch_ref.shape[0])
        def _(i):
            turned[i] = sketch_ref[i].T

        gather_main(t, tab, turned, send, 0)
        gather_hot(t, tab, turned, near, far)

    return kernel


def make_ppmi_kernel(t):
    def kernel(tab, match_ref, counts_ref, turned, sums_ref, ppmi_ref, hot, cols_log):
        sums = jnp.concatenate([sums_ref[r] for r in range(t.groups)], axis=0)
        high = jnp.floor(sums * (1.0 / 256.0))
        low = sums - high * 256.0
        match = match_ref[...]
        margins = 256.0 * contract(match, high.astype(bf16), 1, 0) + contract(
            match, low.astype(bf16), 1, 0
        )
        log_total = jnp.log(jnp.sum(sums))
        log_margin = jnp.log(margins)
        cols_log[...] = log_margin
        fill = 128 - log_margin.shape[0] % 128
        row_log = jnp.concatenate(
            [log_margin, jnp.zeros((fill, log_margin.shape[1]), f32)], axis=0
        ).T
        for s in range(t.nnz):
            counts = counts_ref[s]
            scores = (
                jnp.log(counts.astype(f32))
                + log_total
                - row_log[:, s : s + 1]
                - cols_log[pl.ds(t.nnz + s, 1), :]
            )
            ppmi_ref[s] = jnp.where(counts > 0, jnp.maximum(scores, 0.0), 0.0).astype(bf16)
        hot_products(t, tab, turned, ppmi_ref, hot)

    return kernel


def make_result_kernel(t, order):
    def kernel(tab, ppmi_ref, *refs):
        got_t, got_x = refs[0], refs[-5]
        hot_x, hot_a, hot_b, result = refs[-4:]
        slot = got_x.shape[1] - 1
        result[...] = jnp.zeros_like(result)
        for s in range(t.nnz):
            block = got_x[tab[t.dest + s], slot] if s < t.groups else hot_x[0, s - t.groups]
            forward = contract(block, ppmi_ref[s], 1, 1).astype(bf16)
            result[tab[t.row_i + s]] += forward.astype(f32)
        for r in range(t.groups):
            result[tab[t.main_j + r]] += got_t[r, 0].astype(f32)
        for n, k in enumerate(order):
            ref, place = (hot_a, n) if n < t.groups // 2 else (hot_b, n - t.groups // 2)
            for m in range(t.hot):
                j = tab[t.hot_j + k * t.hot + m]

                @pl.when(j >= 0)
                def _():
                    result[j] += ref[place, m].astype(f32)

    return kernel


def split(x):
    high = x.astype(bf16)
    rest = x - high.astype(f32)
    mid = rest.astype(bf16)
    return high, mid, (rest - mid.astype(f32)).astype(bf16)


def lanes(ref, start, count, rows=None):
    picked = [ref[start + n] if rows is None else ref[start + n, rows, :] for n in range(count)]
    return jnp.concatenate(picked, axis=1)


def own_gram_kernel(own, gram):
    blocks, half, _ = own.shape
    step = 4
    square = jnp.zeros((half, half), f32)
    skew = jnp.zeros((half, half), f32)
    for i in range(0, blocks, step):
        high, mid, low = split(lanes(own, i, step))
        stack = contract(jnp.concatenate([high, mid, low], axis=0), high, 1, 1)
        square += stack[0:half] + contract(mid, mid, 1, 1)
        skew += stack[half : 2 * half] + stack[2 * half :]
    gram[...] = square + (skew + skew.T)


def make_cross_gram_kernel(t):
    def kernel(tab, own, other, square, gram):
        blocks, half, _ = own.shape
        cut = half // 2
        step = 4
        full = square[...]
        row = lax.broadcasted_iota(i32, (half, half), 0)
        lane = lax.broadcasted_iota(i32, (half, half), 1)
        diagonal = jnp.sum(jnp.where(row == lane, full, 0.0), axis=0, keepdims=True)
        gram[pl.ds(0, cut), :] = jnp.where(
            lane[:cut] >= row[:cut], full[:cut], pltpu.roll(full[cut:], cut, 1)
        )
        gram[pl.ds(cut, 8), :] = jnp.broadcast_to(diagonal, (8, half))

        def cross(left, rows, right):
            total = jnp.zeros((cut, half), f32)
            for i in range(0, blocks, step):
                high, mid, low = split(lanes(left, i, step, rows))
                r_high, r_mid, r_low = split(lanes(right, i, step))
                by_high = contract(jnp.concatenate([high, mid, low], axis=0), r_high, 1, 1)
                by_mid = contract(jnp.concatenate([high, mid], axis=0), r_mid, 1, 1)
                small = by_high[2 * cut :] + by_mid[cut:] + contract(high, r_low, 1, 1)
                total += by_high[:cut] + (by_high[cut : 2 * cut] + by_mid[:cut] + small)
            gram[pl.ds(cut + 8, cut), :] = total

        @pl.when(tab[t.col] == 0)
        def _():
            cross(other, pl.ds(0, cut), own)

        @pl.when(tab[t.col] == 1)
        def _():
            cross(own, pl.ds(cut, cut), other)

    return kernel


def pivot_rows(left, right, base):
    full = left.shape
    cols = [jnp.broadcast_to(left[:, base + k : base + k + 1], full) for k in range(8)]
    piv = [[jnp.broadcast_to(cols[k][i : i + 1, :], full) for k in range(i + 1)] for i in range(8)]
    rows = [
        [jnp.broadcast_to(side[i : i + 1, :], full) for side in (left, right)] for i in range(8)
    ]
    zero = jnp.zeros(full, f32)
    inv = [[None] * 8 for _ in range(8)]
    done = []
    solved = [[zero, zero] for _ in range(8)]
    for k in range(0, 8, 2):
        a, b, c = piv[k][k], piv[k + 1][k], piv[k + 1][k + 1]
        det = a * c - b * b
        root, det_root = lax.rsqrt(a), lax.rsqrt(det)
        both = det_root * root
        scale = det_root * (a * root)
        across = b * root
        for i in range(k + 2, 8):
            p, q = piv[i][k], piv[i][k + 1]
            piv[i][k] = p * root
            piv[i][k + 1] = (a * q - b * p) * both
        for i in range(k + 2, 8):
            for m in range(k + 2, i + 1):
                piv[i][m] = piv[i][m] - (
                    piv[i][k] * piv[m][k] + piv[i][k + 1] * piv[m][k + 1]
                )
        pair = []
        for side in range(2):
            first = rows[k][side] * root
            second = (rows[k + 1][side] - across * first) * scale
            pair.append((first, second))
            for i in range(k + 2, 8):
                rows[i][side] = rows[i][side] - (piv[i][k] * first + piv[i][k + 1] * second)
        done += [[pair[0][0], pair[1][0]], [pair[0][1], pair[1][1]]]
        for i in range(k):
            inv[k][i] = inv[k][i] * root
            inv[k + 1][i] = (inv[k + 1][i] - across * inv[k][i]) * scale
        inv[k][k] = root
        inv[k + 1][k] = -across * root * scale
        inv[k + 1][k + 1] = scale
        for i in range(k + 2, 8):
            for m in range(k + 2):
                part = piv[i][k + 1] * inv[k + 1][m]
                if m <= k:
                    part = part + piv[i][k] * inv[k][m]
                inv[i][m] = -part if inv[i][m] is None else inv[i][m] - part
        for n in (k, k + 1):
            for i in range(n + 1):
                for side in range(2):
                    solved[i][side] = solved[i][side] + inv[n][i] * done[n][side]
    return done, solved


def inverse_factor(block):
    size = block.shape[0]
    tiles = size // 8
    panel = 4
    full = (8, size)
    lane = lax.broadcasted_iota(i32, full, 1)
    sub = lax.broadcasted_iota(i32, full, 0)
    sides = [
        [block[8 * t : 8 * t + 8, :], (lane == sub + 8 * t).astype(f32)] for t in range(tiles)
    ]
    for first in range(0, tiles, panel):
        last = first + panel
        for j in range(first, last):
            rows, solved = pivot_rows(*sides[j], 8 * j)
            for t in range(j + 1, last):
                old = sides[t][0]
                new = list(sides[t])
                for k in range(8):
                    col = jnp.broadcast_to(old[:, 8 * j + k : 8 * j + k + 1], full)
                    new = [new[n] - col * solved[k][n] for n in range(2)]
                sides[t] = new
            for n in range(2):
                done = rows[0][n]
                for i in range(1, 8):
                    done = jnp.where(sub == i, rows[i][n], done)
                sides[j][n] = done
        if last < tiles:
            left = jnp.concatenate([sides[t][0] for t in range(first, last)], axis=0)
            right = jnp.concatenate([sides[t][1] for t in range(first, last)], axis=0)
            high, mid, low = split(left)
            r_high, r_mid, r_low = split(jnp.concatenate([left, right], axis=1))
            change = contract(
                jnp.concatenate([high, high, mid, mid, high, low], axis=0),
                jnp.concatenate([r_high, r_mid, r_high, r_mid, r_low, r_high], axis=0),
                0,
                0,
            )
            for t in range(last, tiles):
                part = change[8 * t : 8 * t + 8, :]
                sides[t] = [sides[t][0] - part[:, :size], sides[t][1] - part[:, size:]]
    return jnp.concatenate([side[1] for side in sides], axis=0)


def unpack(packed):
    half = packed.shape[1]
    cut = half // 2
    row = lax.broadcasted_iota(i32, (half, half), 0)
    lane = lax.broadcasted_iota(i32, (half, half), 1)
    folded = packed[:cut]
    keep = lane[:cut] >= row[:cut]
    upper = jnp.where(keep, folded, 0.0)
    lower = pltpu.roll(jnp.where(keep, 0.0, folded), cut, 1)
    triangle = jnp.concatenate([upper, lower], axis=0)
    return jnp.where(row == lane, packed[cut : cut + 1], triangle + triangle.T)


def invert(t, tab, own, other, gram, inverse, scale):
    cut = own.shape[1] // 2
    my_col = tab[t.col]
    gram[my_col] = own[...] * scale
    gram[1 - my_col] = other[...] * scale
    low = inverse_factor(unpack(gram[0]))
    lower = jnp.concatenate([gram[n, pl.ds(cut + 8, cut), :] for n in range(2)], axis=0)
    across = contract(lower, low, 1, 1, HIGHEST)
    high = inverse_factor(unpack(gram[1]) - contract(across, across, 1, 1, HIGHEST))
    inverse[0, 0] = low
    inverse[0, 1] = jnp.zeros_like(low)
    inverse[1, 0] = -contract(high, contract(across, low, 1, 0, HIGHEST), 1, 0, HIGHEST)
    inverse[1, 1] = high


def normal_blocks(t, tab, inverse, mine, other, store):
    my_col = tab[t.col]
    half = mine.shape[1]
    factor = jnp.concatenate([inverse[my_col, my_col], inverse[my_col, 1 - my_col]], axis=1)
    high, mid, _ = split(factor)
    two = jnp.concatenate([high, mid], axis=0)

    @pl.loop(0, mine.shape[0], unroll=4)
    def _(i):
        y_high, y_mid, _ = split(jnp.concatenate([mine[i], other[i]], axis=0))
        by_high = contract(two, y_high, 1, 0)
        store(i, by_high[:half] + (by_high[half:] + contract(high, y_mid, 1, 0)))


def start_copies(pairs, sems):
    copies = [pltpu.make_async_copy(a, b, sems.at[n]) for n, (a, b) in enumerate(pairs)]
    for copy in copies:
        copy.start()
    return copies


def make_second_kernel(t, scale):
    def kernel(
        tab, own_g, other_g, mine_hbm, other_hbm, ppmi_hbm, normal, near, far, hot,
        gram, inverse, mine, other, ppmi, sems,
    ):
        copies = start_copies([(mine_hbm, mine), (other_hbm, other), (ppmi_hbm, ppmi)], sems)
        invert(t, tab, own_g, other_g, gram, inverse, scale)
        for copy in copies:
            copy.wait()

        def store(i, value):
            normal[i] = value.astype(bf16)

        normal_blocks(t, tab, inverse, mine, other, store)
        gather_hot(t, tab, normal, near, far)
        hot_products(t, tab, normal, ppmi, hot)

    return kernel


def make_final_kernel(t, scale):
    def kernel(
        tab, own_g, other_g, mine_hbm, other_hbm, out, gram, inverse, mine, other, held, sems
    ):
        copies = start_copies([(mine_hbm, mine), (other_hbm, other)], sems)
        invert(t, tab, own_g, other_g, gram, inverse, scale)
        for copy in copies:
            copy.wait()

        def leave(i):
            return pltpu.make_async_copy(held.at[i], out.at[i], sems.at[2])

        def store(i, value):
            held[i] = value.T
            leave(i).start()

        normal_blocks(t, tab, inverse, mine, other, store)

        @pl.loop(0, held.shape[0])
        def _(i):
            leave(i).wait()

    return kernel


def body(counts, block_pairs, sketch):
    groups = lax.axis_size("row")
    me = lax.axis_index("row")
    my_col = lax.axis_index("col")
    nnz, rows, _ = counts.shape
    blocks, _, half = sketch.shape
    vocab = blocks * rows * groups
    t = Table(groups, nnz)
    hot = t.hot
    depth = -(-2 * nnz // 8) * 8

    def peer(x, k):
        return lax.ppermute(x, "row", [(r, r ^ k) for r in range(groups)])

    def swap(x):
        return lax.ppermute(x, "col", [(0, 1), (1, 0)])

    def exchange(x):
        return lax.all_to_all(x, "row", split_axis=0, concat_axis=0, tiled=True)

    def add_up(x):
        for bit in t.bits:
            x = x + peer(x, bit)
        return x

    def spread(part, steps, got=None):
        order = [0]
        for n, bit in enumerate(steps):
            if n or got is None:
                got = peer(part, bit)
            order += [k ^ bit for k in order]
            if n < len(steps) - 1:
                part = jnp.concatenate([part, got], axis=0)
        return part, got, order

    def halve(x, kept, bit):
        low = sum(1 for k in kept if k < bit)
        x = x.reshape(-1, 2, low, *x.shape[1:])
        return [x[:, n].reshape(-1, *x.shape[3:]) for n in range(2)]

    def scatter_hot(near, far, got, towards):
        kept = list(range(groups))
        for bit in t.steps:
            if bit != t.steps[0]:
                near, far = halve(part, kept, bit)
                got = peer(far, bit)
            towards = halve(towards, kept, bit)[0]
            kept = [k for k in kept if not k & bit]
            stay = (towards & bit) == 0
            part = jnp.where(stay[:, :, None, None], near, got)
        return part

    def send_shape(slots):
        return shape((groups, slots, half, rows), bf16)

    hot_shape = shape((1, hot, half, rows), bf16)
    side_shape = shape((groups // 2, hot, half, rows), bf16)
    ppmi_shape = shape((nnz, rows, rows), bf16)
    result_shape = shape((blocks, half, rows), f32)

    sums = call(sums_kernel, shape((groups, depth, rows), f32), [VMEM], vmem=8)(counts)
    sums_all = exchange(sums)
    tab, towards = t.build(block_pairs, me, my_col)
    turned, send_x, near, far = call(
        make_source_kernel(t),
        [shape((blocks, half, rows), bf16), send_shape(1), side_shape, side_shape],
        [SMEM, VMEM],
        vmem=8,
    )(tab, sketch)

    row_ids = block_pairs[:, :, 0] * groups + jnp.arange(groups)[:, None]
    col_ids = block_pairs[:, :, 2] * groups + block_pairs[:, :, 1]
    no_id = jnp.full((groups, depth - 2 * nnz), -1, i32)
    ids = jnp.concatenate([row_ids, col_ids, no_id], axis=1)
    my_ids = lax.dynamic_index_in_dim(ids, me, 0, keepdims=False)
    match = (my_ids[:, None] == ids.reshape(-1)[None, :]).astype(bf16)

    send_x, sums_all = lax.optimization_barrier((send_x, sums_all))
    got_x, x_step = exchange(send_x), peer(far, t.steps[0])
    ppmi, hot_t = call(
        make_ppmi_kernel(t),
        [ppmi_shape, hot_shape],
        [SMEM] + [VMEM] * 4,
        scratch=[pltpu.VMEM((depth, rows), f32)],
        vmem=12,
    )(tab, match, counts, turned, sums_all)

    def finish(source, got_x, near, far, x_step, hot_t):
        t_step = peer(hot_t, t.steps[-1])
        if x_step is None:
            x_step = peer(far, t.steps[0])
        merged = got_x is None
        send = call(
            make_main_kernel(t, merged), send_shape(1 + merged), [SMEM, VMEM, VMEM], vmem=8
        )(tab, source, ppmi)
        if merged:
            send, x_step, t_step = lax.optimization_barrier((send, x_step, t_step))
        else:
            send, t_step = lax.optimization_barrier((send, t_step))
        got = [exchange(send)] + ([] if merged else [got_x])
        hot_x = scatter_hot(near, far, x_step, towards)
        hot_a, hot_b, order = spread(hot_t, t.steps[::-1], t_step)
        result = call(
            make_result_kernel(t, order),
            result_shape,
            [SMEM] + [VMEM] * (4 + len(got)),
            vmem=12,
        )(tab, ppmi, *got, hot_x, hot_a, hot_b)
        other = swap(result)
        square = call(own_gram_kernel, shape((half, half), f32), [VMEM], vmem=12)(result)
        gram = call(
            make_cross_gram_kernel(t),
            shape((half + 8, half), f32),
            [SMEM] + [VMEM] * 3,
            vmem=16,
        )(tab, result, other, square)
        gram = add_up(gram)
        return result, other, gram, swap(gram)

    gram_scratch = [
        pltpu.VMEM((2, half + 8, half), f32),
        pltpu.VMEM((2, 2, half, half), f32),
    ]
    result_scratch = [pltpu.VMEM((blocks, half, rows), f32)] * 2
    result, other, gram, other_gram = finish(
        turned, got_x, near, far, x_step, hot_t
    )
    normal, near, far, hot_t = call(
        make_second_kernel(t, 1.0 / vocab),
        [shape((blocks, half, rows), bf16), side_shape, side_shape, hot_shape],
        [SMEM] + [VMEM] * 2 + [ANY] * 3,
        scratch=gram_scratch
        + result_scratch
        + [pltpu.VMEM((nnz, rows, rows), bf16), pltpu.SemaphoreType.DMA((3,))],
    )(tab, gram, other_gram, result, other, ppmi)
    result, other, gram, other_gram = finish(normal, None, near, far, None, hot_t)
    return call(
        make_final_kernel(t, 1.0 / vocab),
        shape((blocks, rows, half), f32),
        [SMEM] + [VMEM] * 2 + [ANY] * 2,
        ANY,
        scratch=gram_scratch
        + result_scratch
        + [pltpu.VMEM((blocks, rows, half), f32), pltpu.SemaphoreType.DMA((3,))],
    )(tab, gram, other_gram, result, other)


def solution(mesh):
    placed = (
        P(("decade", "row"), None, None),
        P("decade", None, None),
        P(None, ("decade", "row"), "col"),
    )
    return jax.shard_map(
        body,
        mesh=mesh,
        in_specs=placed,
        out_specs=P(None, ("decade", "row"), "col"),
        check_vma=False,
    )
```
